128 devices in a mesh: base: 4 (over x), slab: 32 (over z, y, core).
Axes of the slice: x: 4, y: 4, z: 4, core: 2. Of those that a mesh axis runs over, the one named last changes fastest.
Arguments:
- residual: float32 [16384, 2, 128], P(('base', 'slab')), may hold values from -6 to 6
- position: float32 [16384, 2, 128], P(('base', 'slab')), may hold values from 4 to 124
- owner: int32 [16384, 1], P(('base', 'slab')), may hold values from 0 to 127; in each aligned block of 128 rows (0 to 127, 128 to 255, ...) at most 2 rows name the same one
- tile_local: int32 [16384], P(('base', 'slab')), may hold values from 0 to 31
- xi: float32 [4096, 4096], P(('base', 'slab')), may hold values from -6 to 6
- amplitude: float32 [4096, 4096], P(('base', 'slab')), may hold values from 0.05 to 0.5
Outputs:
- gradient: float32 [4096, 4096], P(('base', 'slab'))
The draws below stay inside these ranges and needn't reach their ends.
Inputs may be any that keep to these rules, and one draw needn't show every extreme that they name: Among the blocks of one device no owner region is named by more than 2 blocks, a bound that some owner region reaches on some device.
All inputs are finite; a program needn't handle non-finite values.
Results may differ from the reference program's by a relative error of at most 0.00065.
Values sent between devices are 32-bit elements; how exact they have to be, the bound alone decides.
No kernel may reach another device: no remote copies, remote signals or barrier semaphores. Data moves between devices by JAX's collectives and lax.ppermute only.
A program may use at most 128 MiB of HBM per device.

```python
import math
import jax
import jax.numpy as jnp
import numpy as np
from jax import lax

G = 8192
IMG = 4096
TILE = 128
VB = 128
BLK_DEV = 128
BLOCKS = 16384
CAP = 2
TILES_REG = 32
N_BASE = 4
N_SLAB = 32
DEVICES = 128


def with_ends(values, own_key, low, top_value):
    longest = values.shape.index(max(values.shape))
    spots = []
    for shift in (0, 1):
        where = [jax.random.randint(jax.random.fold_in(own_key, axis), (), 0, length) for axis, length in enumerate(values.shape)]
        where[longest] = (where[longest] + shift) % values.shape[longest]
        spots.append(tuple(where))
    return values.at[spots[0]].set(low).at[spots[1]].set(top_value)


def block_scale(key, dims, split, least, top_value):
    def one(axis_at, blocks):
        heights = jax.random.uniform(jax.random.fold_in(jax.random.fold_in(key, 6), axis_at), (blocks,), jnp.float32, least / len(split), top_value / len(split))
        return jnp.repeat(jnp.exp(heights), dims[axis_at] // blocks).reshape((-1,) + (1,) * (len(dims) - axis_at - 1))

    gain = one(*split[0])
    for cut in split[1:]:
        gain = gain * one(*cut)
    return gain


def deal_out(key, own, number, rows, count, top, reach, skew):
    ranking = jax.random.permutation(key, count)
    packed, usual = portions_of(count, rows * top, reach, skew, True), portions_of(count, rows * top, reach, skew, False)
    places = jnp.arange(count)

    def named(tallies, rotation):
        used = int((tallies > 0).sum())
        fixed = max(1, used // 4)
        moved = fixed + (places - fixed + rotation * (used - fixed)) % max(1, count - fixed)
        return jnp.zeros((count,), jnp.int32).at[ranking[jnp.where(places < fixed, places, moved)]].set(jnp.asarray(tallies, jnp.int32))

    tallies = jnp.where(number % 4 == 0, named(packed, number // 4), named(usual, number - number // 4 - 1))
    mixed = jax.random.permutation(jax.random.fold_in(own, 3), count)
    donor, sink = mixed[0:count // 2 * 2:2], mixed[1:count // 2 * 2:2]
    room = jnp.minimum(tallies[donor] - 1, reach - tallies[sink]) // 2
    room = jnp.where((donor == ranking[0]) | (sink == ranking[0]) | (tallies[sink] == 0), 0, jnp.maximum(room, 0))
    moved = jax.random.randint(jax.random.fold_in(own, 4), (count // 2,), 0, 1 << 20) % (room + 1)
    tallies = tallies.at[donor].add(-moved).at[sink].add(moved)
    members = jnp.searchsorted(jnp.cumsum(tallies), jnp.arange(rows * top), side="right").astype(jnp.int32)
    table = members.reshape(top, rows).T
    table = table[jax.random.permutation(jax.random.fold_in(own, 1), rows)]
    rotation = jax.random.randint(jax.random.fold_in(own, 2), (rows, 1), 0, top)
    return jnp.take_along_axis(table, (jnp.arange(top)[None, :] + rotation) % top, axis=1)


def portions_of(amount, total, limit, slope, full):
    weights = [(1 << 20) // math.isqrt(standing ** slope) + 1 for standing in range(1, amount + 1)]
    largest = limit if full else min(limit, max(-(-total // amount), total * weights[0] // sum(weights)))
    least = 1 if total - largest >= amount - 1 else 0
    holding, rest = [largest] + [least] * (amount - 1), total - largest - least * (amount - 1)
    while rest > 0:
        movable = [i for i in range(1, amount) if holding[i] < largest] or [i for i in range(1, amount) if holding[i] < limit]
        whole, remaining = sum([weights[i] for i in movable]), rest
        for i in movable:
            addition = min(limit - holding[i], max(1, remaining * weights[i] // whole), rest)
            holding[i] = holding[i] + addition
            rest = rest - addition
    return np.array(holding)


def gaussian(rng, shape, width, limit, split=(), kind=jnp.bfloat16):
    result = width * jax.random.normal(rng, shape, jnp.float32)
    if split:
        result = result * block_scale(rng, shape, split, -0.22, 0.18)
    return jnp.clip(result, -limit, limit).astype(kind)


def setup_inputs(seed: int = 0) -> dict:
    keys = jax.random.split(jax.random.key(seed), 7)
    residual = gaussian(keys[0], (BLOCKS, 2, VB), 1.0, 6.0, ((0, 128),), jnp.float32)
    position = jnp.clip(4.0 + 120.0 * jax.random.uniform(keys[1], (BLOCKS, 2, VB), jnp.float32) ** block_scale(keys[1], (BLOCKS, 2, VB), ((0, 128),), -0.2, 0.2), 4.0, 124.0)
    owner_keys = jax.random.split(jax.random.fold_in(keys[2], 1), BLOCKS // BLK_DEV)
    owner_turns = jax.random.permutation(jax.random.fold_in(keys[2], 3), BLOCKS // BLK_DEV)
    owner = jax.vmap(lambda own, number: deal_out(jax.random.fold_in(keys[2], 2), own, number, BLK_DEV, DEVICES, 1, CAP, 2))(owner_keys, owner_turns).reshape((BLOCKS, 1))
    tile_local = with_ends(jax.random.randint(keys[3], (BLOCKS,), 0, TILES_REG), jax.random.fold_in(keys[3], 1), 0, TILES_REG - 1).astype(jnp.int32)
    xi = gaussian(keys[4], (IMG, IMG), 1.0, 6.0, ((0, 128),), jnp.float32)
    amplitude = jnp.clip(jnp.exp(math.log(0.5) - 2.3025851 * jax.random.uniform(keys[5], (IMG, IMG), jnp.float32) ** block_scale(keys[5], (IMG, IMG), ((0, 128),), -0.2, 0.2)), 0.05, 0.5)
    return dict(residual=residual, position=position, owner=owner, tile_local=tile_local, xi=xi, amplitude=amplitude)


def taps(offsets):
    cells = jnp.arange(TILE, dtype=jnp.float32)
    scaled = (cells[None, :, None] - offsets[:, None, :]) * 0.25
    return jnp.maximum(1.0 - scaled * scaled, 0.0) ** 3


def reference(residual, position, owner, tile_local, xi, amplitude):
    rows_tiles = G // N_SLAB // TILE
    cols_tiles = G // N_BASE // TILE
    across = G // TILE
    target = owner[:, 0]
    tile_row = ((target % N_SLAB) * rows_tiles + tile_local // cols_tiles).astype(jnp.int32)
    tile_col = ((target // N_SLAB) * cols_tiles + tile_local % cols_tiles).astype(jnp.int32)

    def step(total, index):
        start = (index * BLK_DEV).astype(jnp.int32)
        values = lax.dynamic_slice_in_dim(residual, start, BLK_DEV, 0)
        places = lax.dynamic_slice_in_dim(position, start, BLK_DEV, 0)
        rows = lax.dynamic_slice_in_dim(tile_row, start, BLK_DEV, 0)
        cols = lax.dynamic_slice_in_dim(tile_col, start, BLK_DEV, 0)
        row_taps = taps(places[:, 0, :])
        col_taps = taps(places[:, 1, :])
        weighted = jnp.concatenate([col_taps * values[:, 0:1, :], col_taps * values[:, 1:2, :]], axis=1)
        subgrid = jnp.einsum("grv,gkv->grk", row_taps, weighted, precision=lax.Precision.HIGHEST)
        total = total.at[rows, cols].add(subgrid.reshape(BLK_DEV, TILE, 2, TILE))
        return total, None

    empty = jnp.zeros((across, across, TILE, 2, TILE), jnp.float32)
    tiles = lax.scan(step, empty, jnp.arange(DEVICES, dtype=jnp.int32))[0]
    grid = tiles.transpose(3, 0, 2, 1, 4).reshape(2, G, G)
    wave = jnp.fft.ifft2(grid[0] + 1j * grid[1])
    lower = G // 4
    back = jnp.real(wave[lower:lower + IMG, lower:lower + IMG]) * G
    spectrum = jnp.fft.fft2(amplitude * xi)
    sky = jnp.exp((jnp.real(spectrum) - jnp.imag(spectrum)) / IMG)
    folded = jnp.fft.fft2(sky * back)
    return amplitude * (jnp.real(folded) - jnp.imag(folded)) / IMG
```

```python
import functools
import math

import jax
import jax.numpy as jnp
import numpy as np
from jax import lax
from jax.experimental import pallas as pl
from jax.experimental.pallas import tpu as pltpu
from jax.sharding import PartitionSpec as P

G = 8192
IMG = 4096
TILE = 128
GROUP = 2

exact = lax.Precision.HIGHEST
NN = (((1,), (0,)), ((), ()))
NT = (((1,), (1,)), ((), ()))
TN = (((0,), (0,)), ((), ()))
f32 = jnp.float32
bf16 = jnp.bfloat16


def mm(a, b, dims=NN):
    return lax.dot_general(a, b, dims, precision=exact, preferred_element_type=f32)


def wave(rows, cols, modulus):
    turn = np.outer(rows, cols).astype(np.int64) % modulus
    angle = turn * (2.0 * np.pi / modulus)
    return np.cos(angle), np.sin(angle)


def turned(c, s):
    return np.block([[c, -s], [s, c]])


@functools.lru_cache(None)
def tables(n_base, n_slab):
    n = np.arange
    devices = n_base * n_slab
    out = {}
    c, s = wave(n(128), n(128), 128)
    out["w128"] = turned(c, s)
    out["w128t"] = turned(c, s).T
    out["tw_row"] = np.stack(wave(n(32), n(128), IMG))
    c, s = wave(n(64) + 32, n(128), 128)
    out["w_cols"] = turned(c, s)
    out["tw_cols"] = np.stack(wave(n(64), n(128), G))
    eye = np.eye(4)
    c, s = wave(n(128), n(32), IMG)
    out["tw_f"] = np.stack([np.tile(c, (1, 4)), np.tile(s, (1, 4))])
    c, s = wave(n(32), n(32), 32)
    out["r_f"] = np.concatenate([np.kron(eye, c + s), np.kron(eye, c - s)]) / IMG
    out["r_y"] = np.concatenate([np.kron(eye, c), np.kron(eye, s)], axis=1)
    src = n(devices)
    place = (src % n_slab) * n_base + src // n_slab
    wb, twb, rb = [], [], []
    for half in range(2):
        c, s = wave(n(128) + 128 * half, place, 256)
        wb.append(turned(c, s))
        c, s = wave(n(128) + 128 * half, n(32), G)
        twb.append(np.stack([np.tile(c, (1, 4)), np.tile(s, (1, 4))]))
        c, s = wave(n(32), n(32) // 2 + 8, 32)
        keep = (n(32) % 2 == half)[None, :]
        rb += [np.kron(eye, c * keep) / G, np.kron(eye, -s * keep) / G]
    out["w_b"] = np.concatenate(wb)
    out["tw_b"] = np.stack(twb)
    out["r_b"] = np.concatenate(rb)
    return {k: v.astype(np.float32) for k, v in out.items()}


def times(z, k, n):
    re, im = z
    k %= n
    if k == 0:
        return z
    if 4 * k == n:
        return -im, re
    c, s = math.cos(2 * math.pi * k / n), math.sin(2 * math.pi * k / n)
    if 8 * k == n:
        return (re - im) * c, (re + im) * c
    if 8 * k == 3 * n:
        return (re + im) * -s, (re - im) * s
    return re * c - im * s, re * s + im * c


def fft_list(xs):
    n = len(xs)
    if n == 1:
        return xs
    even, odd = fft_list(xs[0::2]), fft_list(xs[1::2])
    low, high = [], []
    for k in range(n // 2):
        (a, b), (c, d) = even[k], times(odd[k], k, n)
        low.append((a + c, b + d))
        high.append((a - c, b - d))
    return low + high


def rfft_list(xs):
    n = len(xs)
    if n == 2:
        return [(xs[0] + xs[1], None), (xs[0] - xs[1], None)]
    even, odd = rfft_list(xs[0::2]), rfft_list(xs[1::2])
    out = [None] * (n // 2 + 1)
    out[0] = (even[0][0] + odd[0][0], None)
    out[n // 2] = (even[0][0] - odd[0][0], None)
    out[n // 4] = (even[n // 4][0], odd[n // 4][0])
    for k in range(1, n // 4):
        (a, b), (c, d) = even[k], times(odd[k], k, n)
        out[k] = (a + c, b + d)
        out[n // 2 - k] = (a - c, d - b)
    return out


def call(body, out_shape, in_specs, scratch=(), flops=0):
    nbytes = 4 * math.prod(out_shape)
    return pl.pallas_call(
        body,
        out_shape=jax.ShapeDtypeStruct(out_shape, f32),
        in_specs=[pl.BlockSpec(memory_space=m) for m in in_specs],
        out_specs=pl.BlockSpec(memory_space=pltpu.VMEM),
        scratch_shapes=list(scratch),
        compiler_params=pltpu.CompilerParams(vmem_limit_bytes=48 * 2**20),
        cost_estimate=pl.CostEstimate(flops=flops, bytes_accessed=2 * nbytes, transcendentals=0),
    )


VM = pltpu.VMEM
SM = pltpu.SMEM


def pack_kernel(owner, tile, residual, position, out, count):
    n_base, n_slab = 4, 32
    out[...] = jnp.zeros_like(out)

    def clear(i, _):
        count[i] = 0
        return 0

    lax.fori_loop(0, count.shape[0], clear, 0, unroll=8)
    lane = lax.broadcasted_iota(jnp.int32, (1, 128), 1)

    def step(i, _):
        o, t = owner[i], tile[i]
        row = (o & (n_slab - 1)) * 2 + (t >> 4)
        group, col = o >> 5, t & 15
        flip = (row >= n_slab).astype(jnp.int32)
        row = jnp.where(flip == 1, 2 * n_slab - 1 - row, row)
        group = jnp.where(flip == 1, n_base - 1 - group, group)
        col = jnp.where(flip == 1, 15 - col, col)
        k = count[o]
        count[o] = k + 1
        slot = flip * 2 + (k & 1)
        to = group * n_slab + row
        for part in range(2):
            out[to, slot * 4 + part] = residual[i, part : part + 1, :]
            out[to, slot * 4 + 2 + part] = position[i, part : part + 1, :]
        out[to, 16] = jnp.where(lane == slot, (col + 1).astype(f32), out[to, 16])
        return 0

    lax.fori_loop(0, owner.shape[0], step, 0)


def pieces(x):
    hi = x.astype(bf16)
    rest = x - hi.astype(f32)
    mid = rest.astype(bf16)
    low = (rest - mid.astype(f32)).astype(bf16)
    return hi, mid, low


def taps(cells, offsets):
    d = cells - offsets
    x = jnp.maximum(1.0 - d * d * 0.0625, 0.0)
    return x * x * x


def grid_kernel(tags, data, out, cells, order):
    slots = tags.shape[0]
    up = lax.broadcasted_iota(jnp.int32, (TILE, TILE), 0).astype(f32)
    cells[0] = up
    cells[1] = float(TILE) - up
    out[...] = jnp.zeros_like(out)

    def scan(s, n):
        order[n] = s
        return n + (tags[s] > 0).astype(jnp.int32)

    n = lax.fori_loop(0, slots, scan, jnp.int32(0), unroll=8)
    for extra in range(GROUP):
        order[n + extra] = 0

    def group(g, _):
        for u in range(GROUP):
            at = g * GROUP + u
            s = order[at]
            used = (at < n).astype(f32)
            src, slot = s >> 2, s & 3
            flip = slot >> 1
            t = jnp.maximum(tags[s] - 1, 0)
            value_re = data[src, slot * 4] * used
            value_im = data[src, slot * 4 + 1] * (used * (1.0 - 2.0 * flip.astype(f32)))
            grid = cells[flip]
            rows = taps(grid, data[src, slot * 4 + 2])
            cols = taps(grid, data[src, slot * 4 + 3])
            weighted = jnp.concatenate([cols * value_re, cols * value_im], axis=0)
            a0, a1, a2 = pieces(rows)
            b0, b1, b2 = pieces(weighted)
            left = jnp.concatenate([a0, a0, a1, a1, a0, a2], axis=1)
            right = jnp.concatenate([b0, b1, b0, b1, b2, b0], axis=1)
            sub = lax.dot_general(left, right, NT, preferred_element_type=f32)
            for q in range(4):
                for ri in range(2):
                    out[q, ri, t] += sub[32 * q : 32 * q + 32, 128 * ri : 128 * ri + 128]
        return 0

    lax.fori_loop(0, (n + GROUP - 1) // GROUP, group, 0)


def cols_kernel(x, tw, w, out, mid):
    def rows(i, _):
        at = pl.ds(pl.multiple_of(i * 8, 8), 8)
        first = [(x[b // 16, 0, b % 16, at, :], x[b // 16, 1, b % 16, at, :]) for b in range(64)]
        for c, (re, im) in enumerate(fft_list(first)):
            cos, sin = tw[0, c : c + 1, :], tw[1, c : c + 1, :]
            mid[c, at, 0:128] = re * cos - im * sin
            mid[c, at, 128:256] = re * sin + im * cos
        return 0

    lax.fori_loop(0, 4, rows, 0)
    for pair in range(8):
        part = mid[8 * pair : 8 * pair + 8].reshape(256, 256)
        res = mm(w[...], part, NT)
        for k in range(2):
            chunk = 2 * pair + k
            for ri in range(2):
                out[:, chunk // 8, ri * 8 + chunk % 8, :] = res[64 * ri : 64 * ri + 64, 128 * k : 128 * k + 128]


def row_kernel(xi, amplitude, tw, w, out, mid):
    def rows(i, _):
        at = pl.ds(pl.multiple_of(i * 8, 8), 8)
        first = [
            xi[at, 128 * b : 128 * b + 128] * amplitude[at, 128 * b : 128 * b + 128] for b in range(32)
        ]
        half = rfft_list(first)
        for c in range(32):
            cos, sin = tw[0, c : c + 1, :], tw[1, c : c + 1, :]
            re, im = half[c] if c <= 16 else half[32 - c]
            if im is None:
                mid[c, at, 0:128] = re * cos
                mid[c, at, 128:256] = re * sin
            else:
                im = im if c <= 16 else -im
                mid[c, at, 0:128] = re * cos - im * sin
                mid[c, at, 128:256] = re * sin + im * cos
        return 0

    lax.fori_loop(0, 4, rows, 0)
    for pair in range(4):
        part = mid[8 * pair : 8 * pair + 8].reshape(256, 256)
        res = mm(w[...], part, NT)
        for k in range(2):
            for ri in range(2):
                out[:, ri * 8 + 2 * pair + k, :] = res[128 * ri : 128 * ri + 128, 128 * k : 128 * k + 128]


def image_kernel(field, uv, w, tw_f, r_f, r_y, w_b, tw_b, r_b, out):
    for j in range(8):
        half = jnp.concatenate([field[:, j, :], field[:, 8 + j, :]], axis=0)
        a = mm(w[...], half)
        re, im = a[0:128], a[128:256]
        turn = jnp.concatenate([re * tw_f[0] - im * tw_f[1], re * tw_f[1] + im * tw_f[0]], axis=1)
        sky = jnp.exp(mm(turn, r_f[...]))
        kept = jnp.concatenate([uv[:, j, :], uv[:, 8 + j, :]], axis=0)
        a = mm(w_b[...], kept)
        parts = []
        for h in range(2):
            re, im = a[256 * h : 256 * h + 128], a[256 * h + 128 : 256 * h + 256]
            parts += [re * tw_b[h, 0] - im * tw_b[h, 1], re * tw_b[h, 1] + im * tw_b[h, 0]]
        back = mm(jnp.concatenate(parts, axis=1), r_b[...])
        a = mm(sky * back, r_y[...])
        re, im = a[:, 0:128], a[:, 128:256]
        turn = jnp.concatenate([re * tw_f[0] - im * tw_f[1], re * tw_f[1] + im * tw_f[0]], axis=0)
        res = mm(w[...], turn)
        out[:, j, :] = res[0:128]
        out[:, 8 + j, :] = res[128:256]


def last_kernel(folded, amplitude, tw, w, out, mid):
    for j in range(8):
        z = jnp.concatenate([folded[:, j, :], folded[:, 8 + j, :]], axis=0)
        v = mm(z, w[...], TN)
        for k in range(4):
            c = 4 * j + k
            cos, sin = tw[0, c : c + 1, :], tw[1, c : c + 1, :]
            re, im = v[32 * k : 32 * k + 32, 0:128], v[32 * k : 32 * k + 32, 128:256]
            mid[c, :, 0:128] = re * cos - im * sin
            mid[c, :, 128:256] = re * sin + im * cos

    def rows(i, _):
        at = pl.ds(pl.multiple_of(i * 8, 8), 8)
        first = [(mid[c, at, 0:128], mid[c, at, 128:256]) for c in range(32)]
        for b, (re, im) in enumerate(fft_list(first)):
            to = slice(128 * b, 128 * b + 128)
            out[at, to] = amplitude[at, to] * (re + im) * (1.0 / IMG)
        return 0

    lax.fori_loop(0, 4, rows, 0)


def per_device(residual, position, owner, tile_local, xi, amplitude):
    n_base = lax.axis_size("base")
    n_slab = lax.axis_size("slab")
    devices = n_base * n_slab
    everywhere = ("base", "slab")
    t = {k: jnp.asarray(v) for k, v in tables(n_base, n_slab).items()}

    def exchange(a, axis):
        return lax.all_to_all(a, axis, split_axis=0, concat_axis=0, tiled=True)

    packed = call(
        pack_kernel, (devices, 17, 1, 128), [SM, SM, VM, VM], [SM((devices,), jnp.int32)]
    )(owner[:, 0], tile_local, residual, position)
    data = exchange(packed, everywhere)

    half = call(
        row_kernel, (devices, 16, 128), [VM] * 4, [VM((32, 32, 256), f32)]
    )(xi, amplitude, t["tw_row"], t["w128"])
    half = exchange(half, everywhere)

    tags = data[:, 16, 0, 0:4].reshape(4 * devices).astype(jnp.int32)
    grid = call(
        grid_kernel,
        (4, 2, 16, 32, 128),
        [SM, VM],
        [VM((2, TILE, TILE), f32), SM((4 * devices + GROUP,), jnp.int32)],
    )(tags, data)
    grid = exchange(grid, "base")
    cols = call(
        cols_kernel, (devices // 2, 2, 16, 128), [VM] * 3, [VM((64, 32, 256), f32)]
    )(grid, t["tw_cols"], t["w_cols"])
    cols = exchange(cols.reshape(devices, 16, 128), everywhere)
    fold = call(image_kernel, (devices, 16, 128), [VM] * 9)(
        half, cols, t["w128"], t["tw_f"], t["r_f"], t["r_y"], t["w_b"], t["tw_b"], t["r_b"]
    )
    fold = exchange(fold, everywhere)
    return call(last_kernel, (32, IMG), [VM] * 4, [VM((32, 32, 256), f32)])(
        fold, amplitude, t["tw_row"], t["w128t"]
    )


def solution(mesh):
    placed = (
        P(("base", "slab"), None, None),
        P(("base", "slab"), None, None),
        P(("base", "slab"), None),
        P(("base", "slab")),
        P(("base", "slab"), None),
        P(("base", "slab"), None),
    )
    return jax.shard_map(
        per_device, mesh=mesh, in_specs=placed, out_specs=P(("base", "slab"), None), check_vma=False
    )
```

```python
import functools
import math

import jax
import jax.numpy as jnp
import ml_dtypes
import numpy as np
from jax import lax
from jax.experimental import pallas as pl
from jax.experimental.pallas import tpu as pltpu
from jax.sharding import PartitionSpec as P

G = 8192
IMG = 4096
TILE = 128
GROUP = 8

NN = (((1,), (0,)), ((), ()))
NT = (((1,), (1,)), ((), ()))
TN = (((0,), (0,)), ((), ()))
f32 = jnp.float32
bf16 = jnp.bfloat16


LEFT = {6: (0, 0, 1, 1, 0, 2), 3: (0, 0, 1)}
RIGHT = {6: (0, 1, 0, 1, 2, 0), 3: (0, 1, 0)}


def pieces(x, count=3):
    out, rest = [], x
    for k in range(count):
        out.append(rest.astype(bf16))
        if k + 1 < count:
            rest = rest - out[-1].astype(f32)
    return out


def spread(x, order, axis):
    cut = pieces(x, max(order) + 1)
    return jnp.concatenate([cut[k] for k in order], axis=axis)


def mm(a, b, dims=NN):
    return lax.dot_general(a, b, dims, preferred_element_type=f32)


def spread_table(x, order, axis):
    cut, rest = [], x.astype(np.float64)
    for _ in range(max(order) + 1):
        cut.append(rest.astype(np.float32).astype(ml_dtypes.bfloat16))
        rest = rest - cut[-1].astype(np.float64)
    return np.concatenate([cut[k] for k in order], axis=axis)


def wave(rows, cols, modulus):
    turn = np.outer(rows, cols).astype(np.int64) % modulus
    angle = turn * (2.0 * np.pi / modulus)
    return np.cos(angle), np.sin(angle)


def turned(c, s):
    return np.block([[c, -s], [s, c]])


@functools.lru_cache(None)
def tables(n_base, n_slab):
    n = np.arange
    devices = n_base * n_slab
    out = {}
    c, s = wave(n(128), n(128), 128)
    out["w128"] = spread_table(turned(c, s), LEFT[3], 1)
    out["w128t"] = spread_table(turned(c, s).T, RIGHT[3], 0)
    out["tw_row"] = np.stack(wave(n(32), n(128), IMG))
    c, s = wave(n(64) + 32, n(128), 128)
    out["w_cols"] = spread_table(turned(c, s), LEFT[6], 1)
    out["tw_cols"] = np.stack(wave(n(64), n(128), G))
    eye = np.eye(4)
    c, s = wave(n(128), n(32), IMG)
    out["tw_f"] = np.stack([np.tile(c, (1, 4)), np.tile(s, (1, 4))])
    c, s = wave(n(32), n(32), 32)
    out["r_f"] = spread_table(np.concatenate([np.kron(eye, c + s), np.kron(eye, c - s)]) / IMG, RIGHT[3], 0)
    out["r_y"] = spread_table(np.concatenate([np.kron(eye, c), np.kron(eye, s)], axis=1), RIGHT[3], 0)
    src = n(devices)
    place = (src % n_slab) * n_base + src // n_slab
    wb, twb, rb = [], [], []
    for half in range(2):
        c, s = wave(n(128) + 128 * half, place, 256)
        wb.append(turned(c, s))
        c, s = wave(n(128) + 128 * half, n(32), G)
        twb.append(np.stack([np.tile(c, (1, 4)), np.tile(s, (1, 4))]))
        c, s = wave(n(32), n(32) // 2 + 8, 32)
        keep = (n(32) % 2 == half)[None, :]
        rb += [np.kron(eye, c * keep) / G, np.kron(eye, -s * keep) / G]
    out["w_b"] = spread_table(np.concatenate(wb), LEFT[6], 1)
    out["tw_b"] = np.stack(twb)
    out["r_b"] = spread_table(np.concatenate(rb), RIGHT[6], 0)
    return {k: v if v.dtype == ml_dtypes.bfloat16 else v.astype(np.float32) for k, v in out.items()}


def times(z, k, n):
    re, im = z
    k %= n
    if k == 0:
        return z
    if 4 * k == n:
        return -im, re
    c, s = math.cos(2 * math.pi * k / n), math.sin(2 * math.pi * k / n)
    if 8 * k == n:
        return (re - im) * c, (re + im) * c
    if 8 * k == 3 * n:
        return (re + im) * -s, (re - im) * s
    return re * c - im * s, re * s + im * c


def fft_list(xs):
    n = len(xs)
    if n == 1:
        return xs
    even, odd = fft_list(xs[0::2]), fft_list(xs[1::2])
    low, high = [], []
    for k in range(n // 2):
        (a, b), (c, d) = even[k], times(odd[k], k, n)
        low.append((a + c, b + d))
        high.append((a - c, b - d))
    return low + high


def rfft_list(xs):
    n = len(xs)
    if n == 2:
        return [(xs[0] + xs[1], None), (xs[0] - xs[1], None)]
    even, odd = rfft_list(xs[0::2]), rfft_list(xs[1::2])
    out = [None] * (n // 2 + 1)
    out[0] = (even[0][0] + odd[0][0], None)
    out[n // 2] = (even[0][0] - odd[0][0], None)
    out[n // 4] = (even[n // 4][0], odd[n // 4][0])
    for k in range(1, n // 4):
        (a, b), (c, d) = even[k], times(odd[k], k, n)
        out[k] = (a + c, b + d)
        out[n // 2 - k] = (a - c, d - b)
    return out


def call(body, out_shape, in_specs, scratch=(), flops=0):
    nbytes = 4 * math.prod(out_shape)
    return pl.pallas_call(
        body,
        out_shape=jax.ShapeDtypeStruct(out_shape, f32),
        in_specs=[pl.BlockSpec(memory_space=m) for m in in_specs],
        out_specs=pl.BlockSpec(memory_space=pltpu.VMEM),
        scratch_shapes=list(scratch),
        compiler_params=pltpu.CompilerParams(vmem_limit_bytes=48 * 2**20),
        cost_estimate=pl.CostEstimate(flops=int(flops), bytes_accessed=2 * nbytes, transcendentals=0),
    )


VM = pltpu.VMEM
SM = pltpu.SMEM


def pack_kernel(owner, tile, residual, position, out, count):
    n_base, n_slab = 4, 32
    out[...] = jnp.zeros_like(out)

    def clear(i, _):
        count[i] = 0
        return 0

    lax.fori_loop(0, count.shape[0], clear, 0, unroll=8)
    lane = lax.broadcasted_iota(jnp.int32, (1, 128), 1)

    def step(i, _):
        o, t = owner[i], tile[i]
        row = (o & (n_slab - 1)) * 2 + (t >> 4)
        group, col = o >> 5, t & 15
        flip = (row >= n_slab).astype(jnp.int32)
        row = jnp.where(flip == 1, 2 * n_slab - 1 - row, row)
        group = jnp.where(flip == 1, n_base - 1 - group, group)
        col = jnp.where(flip == 1, 15 - col, col)
        k = count[o]
        count[o] = k + 1
        slot = flip * 2 + (k & 1)
        to = group * n_slab + row
        for part in range(2):
            out[to, slot * 4 + part] = residual[i, part : part + 1, :]
            out[to, slot * 4 + 2 + part] = position[i, part : part + 1, :]
        out[to, 16] = jnp.where(lane == slot, (col + 1).astype(f32), out[to, 16])
        return 0

    lax.fori_loop(0, owner.shape[0], step, 0)


def taps(d):
    x = jnp.maximum(1.0 - d * d, 0.0)
    return x * x * x


def grid_kernel(tags, data, out, cells, order):
    slots = tags.shape[0]
    for axis in range(2):
        at = lax.broadcasted_iota(jnp.int32, (TILE, TILE), axis).astype(f32)
        cells[2 * axis] = at * 0.25
        cells[2 * axis + 1] = (float(TILE) - at) * 0.25
    out[...] = jnp.zeros_like(out)

    def scan(s, n):
        order[n] = s
        return n + (tags[s] > 0).astype(jnp.int32)

    n = lax.fori_loop(0, slots, scan, jnp.int32(0), unroll=8)
    for extra in range(GROUP):
        order[n + extra] = 0

    def down(row):
        return jnp.transpose(jnp.broadcast_to(row, (TILE, TILE)))

    def group(g, _):
        for u in range(GROUP):
            at = g * GROUP + u
            s = order[at]
            used = (at < n).astype(f32)
            src, slot = s >> 2, s & 3
            flip = slot >> 1
            t = jnp.maximum(tags[s] - 1, 0)
            value_re = data[src, slot * 4] * used
            value_im = data[src, slot * 4 + 1] * (used * (1.0 - 2.0 * flip.astype(f32)))
            rows = taps(cells[flip] - data[src, slot * 4 + 2] * 0.25)
            cols = taps(cells[2 + flip] - down(data[src, slot * 4 + 3] * 0.25))
            weighted = jnp.concatenate([cols * down(value_re), cols * down(value_im)], axis=1)
            sub = mm(spread(rows, LEFT[6], 1), spread(weighted, RIGHT[6], 0))
            for q in range(4):
                for ri in range(2):
                    out[q, ri, t] += sub[32 * q : 32 * q + 32, 128 * ri : 128 * ri + 128]
        return 0

    lax.fori_loop(0, (n + GROUP - 1) // GROUP, group, 0)


def cols_kernel(x, tw, w, out, mid):
    def rows(i, _):
        at = pl.ds(pl.multiple_of(i * 8, 8), 8)
        first = [(x[b // 16, 0, b % 16, at, :], x[b // 16, 1, b % 16, at, :]) for b in range(64)]
        for c, (re, im) in enumerate(fft_list(first)):
            cos, sin = tw[0, c : c + 1, :], tw[1, c : c + 1, :]
            mid[c, at, 0:128] = re * cos - im * sin
            mid[c, at, 128:256] = re * sin + im * cos
        return 0

    lax.fori_loop(0, 4, rows, 0)
    for pair in range(8):
        part = spread(mid[8 * pair : 8 * pair + 8].reshape(256, 256), RIGHT[6], 1)
        res = mm(w[...], part, NT)
        for k in range(2):
            chunk = 2 * pair + k
            for ri in range(2):
                out[:, chunk // 8, ri * 8 + chunk % 8, :] = res[64 * ri : 64 * ri + 64, 128 * k : 128 * k + 128]


def row_kernel(xi, amplitude, tw, w, out, mid):
    def rows(i, _):
        at = pl.ds(pl.multiple_of(i * 8, 8), 8)
        first = [
            xi[at, 128 * b : 128 * b + 128] * amplitude[at, 128 * b : 128 * b + 128] for b in range(32)
        ]
        half = rfft_list(first)
        for c in range(32):
            cos, sin = tw[0, c : c + 1, :], tw[1, c : c + 1, :]
            re, im = half[c] if c <= 16 else half[32 - c]
            if im is None:
                mid[c, at, 0:128] = re * cos
                mid[c, at, 128:256] = re * sin
            else:
                im = im if c <= 16 else -im
                mid[c, at, 0:128] = re * cos - im * sin
                mid[c, at, 128:256] = re * sin + im * cos
        return 0

    lax.fori_loop(0, 4, rows, 0)
    for pair in range(4):
        part = spread(mid[8 * pair : 8 * pair + 8].reshape(256, 256), RIGHT[3], 1)
        res = mm(w[...], part, NT)
        for k in range(2):
            for ri in range(2):
                out[:, ri * 8 + 2 * pair + k, :] = res[128 * ri : 128 * ri + 128, 128 * k : 128 * k + 128]


def chunks(ref, pair):
    return jnp.concatenate(
        [jnp.concatenate([ref[:, ri * 8 + 2 * pair + k, :] for k in range(2)], axis=1) for ri in range(2)],
        axis=0,
    )


def twist(re, im, tw):
    return re * tw[0] - im * tw[1], re * tw[1] + im * tw[0]


def halves(a, at):
    return [a[at : at + 128, 128 * k : 128 * k + 128] for k in range(2)]


def stacked(rows):
    return jnp.concatenate([jnp.concatenate(r, axis=1) for r in rows], axis=0)


def sky_kernel(field, w, tw, r, out):
    for pair in range(4):
        a = mm(w[...], spread(chunks(field, pair), RIGHT[3], 0))
        turn = stacked([twist(re, im, tw) for re, im in zip(halves(a, 0), halves(a, 128))])
        out[pair] = jnp.exp(mm(spread(turn, LEFT[3], 1), r[...]))


def image_kernel(sky, uv, w, tw_f, r_y, w_b, tw_b, r_b, out):
    for pair in range(4):
        a = mm(w_b[...], spread(chunks(uv, pair), RIGHT[6], 0))
        parts = [[], []]
        for h in range(2):
            for k, (re, im) in enumerate(zip(halves(a, 256 * h), halves(a, 256 * h + 128))):
                parts[k] += twist(re, im, tw_b[h])
        back = mm(spread(stacked(parts), LEFT[6], 1), r_b[...])
        a = mm(spread(sky[pair] * back, LEFT[3], 1), r_y[...])
        turn = [twist(a[128 * k : 128 * k + 128, 0:128], a[128 * k : 128 * k + 128, 128:256], tw_f) for k in range(2)]
        turn = jnp.concatenate([jnp.concatenate([turn[k][ri] for k in range(2)], axis=1) for ri in range(2)], axis=0)
        res = mm(w[...], spread(turn, RIGHT[3], 0))
        for ri in range(2):
            for k in range(2):
                out[:, ri * 8 + 2 * pair + k, :] = res[128 * ri : 128 * ri + 128, 128 * k : 128 * k + 128]


def last_kernel(folded, amplitude, tw, w, out, mid):
    for j in range(8):
        z = jnp.concatenate([folded[:, j, :], folded[:, 8 + j, :]], axis=0)
        v = mm(spread(z, LEFT[3], 0), w[...], TN)
        for k in range(4):
            c = 4 * j + k
            cos, sin = tw[0, c : c + 1, :], tw[1, c : c + 1, :]
            re, im = v[32 * k : 32 * k + 32, 0:128], v[32 * k : 32 * k + 32, 128:256]
            mid[c, :, 0:128] = re * cos - im * sin
            mid[c, :, 128:256] = re * sin + im * cos

    def rows(i, _):
        at = pl.ds(pl.multiple_of(i * 8, 8), 8)
        first = [(mid[c, at, 0:128], mid[c, at, 128:256]) for c in range(32)]
        for b, (re, im) in enumerate(fft_list(first)):
            to = slice(128 * b, 128 * b + 128)
            out[at, to] = amplitude[at, to] * (re + im) * (1.0 / IMG)
        return 0

    lax.fori_loop(0, 4, rows, 0)


def per_device(residual, position, owner, tile_local, xi, amplitude):
    n_base = lax.axis_size("base")
    n_slab = lax.axis_size("slab")
    devices = n_base * n_slab
    everywhere = ("base", "slab")
    t = {k: jnp.asarray(v) for k, v in tables(n_base, n_slab).items()}

    def exchange(a, axis):
        return lax.all_to_all(a, axis, split_axis=0, concat_axis=0, tiled=True)

    packed = call(
        pack_kernel, (devices, 17, 1, 128), [SM, SM, VM, VM], [SM((devices,), jnp.int32)], 2e9
    )(owner[:, 0], tile_local, residual, position)
    data = exchange(packed, everywhere)

    half = call(row_kernel, (devices, 16, 128), [VM] * 4, [VM((32, 32, 256), f32)], 2e9)(
        xi, amplitude, t["tw_row"], t["w128"]
    )
    half = exchange(half, everywhere)

    tags = data[:, 16, 0, 0:4].reshape(4 * devices).astype(jnp.int32)
    grid = call(
        grid_kernel,
        (4, 2, 16, 32, 128),
        [SM, VM],
        [VM((4, TILE, TILE), f32), SM((4 * devices + GROUP,), jnp.int32)],
        4e10,
    )(tags, data)
    grid, half = lax.optimization_barrier((grid, half))
    grid = exchange(grid, "base")
    sky = call(sky_kernel, (4, 256, 128), [VM] * 4, (), 4e9)(half, t["w128"], t["tw_f"], t["r_f"])
    cols = call(cols_kernel, (devices // 2, 2, 16, 128), [VM] * 3, [VM((64, 32, 256), f32)], 4e9)(
        grid, t["tw_cols"], t["w_cols"]
    )
    cols = exchange(cols.reshape(devices, 16, 128), everywhere)
    fold = call(image_kernel, (devices, 16, 128), [VM] * 8, (), 8e9)(
        sky, cols, t["w128"], t["tw_f"], t["r_y"], t["w_b"], t["tw_b"], t["r_b"]
    )
    fold = exchange(fold, everywhere)
    return call(last_kernel, (32, IMG), [VM] * 4, [VM((32, 32, 256), f32)], 3e9)(
        fold, amplitude, t["tw_row"], t["w128t"]
    )


def solution(mesh):
    placed = (
        P(("base", "slab"), None, None),
        P(("base", "slab"), None, None),
        P(("base", "slab"), None),
        P(("base", "slab")),
        P(("base", "slab"), None),
        P(("base", "slab"), None),
    )
    return jax.shard_map(
        per_device, mesh=mesh, in_specs=placed, out_specs=P(("base", "slab"), None), check_vma=False
    )
```

```python
import functools
import math

import jax
import jax.numpy as jnp
import ml_dtypes
import numpy as np
from jax import lax
from jax.experimental import pallas as pl
from jax.experimental.pallas import tpu as pltpu
from jax.sharding import PartitionSpec as P

G = 8192
IMG = 4096
TILE = 128
GROUP = 8
GRANT = 20 * 2**20

NN = (((1,), (0,)), ((), ()))
NT = (((1,), (1,)), ((), ()))
TN = (((0,), (0,)), ((), ()))
f32 = jnp.float32
bf16 = jnp.bfloat16


LEFT = {6: (0, 0, 1, 1, 0, 2), 3: (0, 0, 1)}
RIGHT = {6: (0, 1, 0, 1, 2, 0), 3: (0, 1, 0)}


def pieces(x, count=3):
    out, rest = [], x
    for k in range(count):
        out.append(rest.astype(bf16))
        if k + 1 < count:
            rest = rest - out[-1].astype(f32)
    return out


def spread(x, order, axis):
    cut = pieces(x, max(order) + 1)
    return jnp.concatenate([cut[k] for k in order], axis=axis)


def mm(a, b, dims=NN):
    return lax.dot_general(a, b, dims, preferred_element_type=f32)


def spread_table(x, order, axis):
    cut, rest = [], x.astype(np.float64)
    for _ in range(max(order) + 1):
        cut.append(rest.astype(np.float32).astype(ml_dtypes.bfloat16))
        rest = rest - cut[-1].astype(np.float64)
    return np.concatenate([cut[k] for k in order], axis=axis)


def wave(rows, cols, modulus):
    turn = np.outer(rows, cols).astype(np.int64) % modulus
    angle = turn * (2.0 * np.pi / modulus)
    return np.cos(angle), np.sin(angle)


def turned(c, s):
    return np.block([[c, -s], [s, c]])


@functools.lru_cache(None)
def tables(n_base, n_slab):
    n = np.arange
    devices = n_base * n_slab
    out = {}
    c, s = wave(n(128), n(128), 128)
    out["w128"] = spread_table(turned(c, s), LEFT[3], 1)
    out["w128t"] = spread_table(turned(c, s).T, RIGHT[3], 0)
    out["tw_row"] = np.stack(wave(n(32), n(128), IMG))
    c, s = wave(n(64) + 32, n(128), 128)
    out["w_cols"] = spread_table(turned(c, s), LEFT[6], 1)
    out["tw_cols"] = np.stack([np.stack(wave(n(64), n(128) + G // n_base * me, G)) for me in range(n_base)])
    eye = np.eye(4)
    c, s = wave(n(128), n(32), IMG)
    out["tw_f"] = np.stack([np.tile(c, (1, 4)), np.tile(s, (1, 4))])
    c, s = wave(n(32), n(32), 32)
    out["r_f"] = spread_table(np.concatenate([np.kron(eye, c + s), np.kron(eye, c - s)]) / IMG, RIGHT[3], 0)
    out["r_y"] = spread_table(np.concatenate([np.kron(eye, c), np.kron(eye, s)], axis=1), RIGHT[3], 0)
    src = n(devices)
    place = (src % n_slab) * n_base + src // n_slab
    wb, twb, rb = [], [], []
    for half in range(2):
        c, s = wave(n(128) + 128 * half, place, 256)
        wb.append(turned(c, s))
        c, s = wave(n(128) + 128 * half, n(32), G)
        twb.append(np.stack([np.tile(c, (1, 4)), np.tile(s, (1, 4))]))
        c, s = wave(n(32), n(32) // 2 + 8, 32)
        keep = (n(32) % 2 == half)[None, :]
        rb += [np.kron(eye, c * keep) / G, np.kron(eye, -s * keep) / G]
    out["w_b"] = spread_table(np.concatenate(wb), LEFT[6], 1)
    out["tw_b"] = np.stack(twb)
    out["r_b"] = spread_table(np.concatenate(rb), RIGHT[6], 0)
    return {k: v if v.dtype == ml_dtypes.bfloat16 else v.astype(np.float32) for k, v in out.items()}


def times(z, k, n):
    re, im = z
    k %= n
    if k == 0:
        return z
    if 4 * k == n:
        return -im, re
    c, s = math.cos(2 * math.pi * k / n), math.sin(2 * math.pi * k / n)
    if 8 * k == n:
        return (re - im) * c, (re + im) * c
    if 8 * k == 3 * n:
        return (re + im) * -s, (re - im) * s
    return re * c - im * s, re * s + im * c


def fft_list(xs):
    n = len(xs)
    if n == 1:
        return xs
    even, odd = fft_list(xs[0::2]), fft_list(xs[1::2])
    low, high = [], []
    for k in range(n // 2):
        (a, b), (c, d) = even[k], times(odd[k], k, n)
        low.append((a + c, b + d))
        high.append((a - c, b - d))
    return low + high


def rfft_list(xs):
    n = len(xs)
    if n == 2:
        return [(xs[0] + xs[1], None), (xs[0] - xs[1], None)]
    even, odd = rfft_list(xs[0::2]), rfft_list(xs[1::2])
    out = [None] * (n // 2 + 1)
    out[0] = (even[0][0] + odd[0][0], None)
    out[n // 2] = (even[0][0] - odd[0][0], None)
    out[n // 4] = (even[n // 4][0], odd[n // 4][0])
    for k in range(1, n // 4):
        (a, b), (c, d) = even[k], times(odd[k], k, n)
        out[k] = (a + c, b + d)
        out[n // 2 - k] = (a - c, d - b)
    return out


def call(body, out_shapes, in_specs, scratch=(), flops=0, far=(), far_out=False):
    outs = [out_shapes] if isinstance(out_shapes[0], int) else list(out_shapes)
    count, own, made = len(in_specs), len(scratch), len(outs)
    specs = [pl.BlockSpec(memory_space=m) for m in in_specs]
    for i, _ in far:
        specs[i] = pl.BlockSpec(memory_space=pltpu.HBM)

    def kernel(*refs):
        ins, results = list(refs[:count]), list(refs[count : count + made])
        rest = refs[count + made : count + made + own]
        spare = refs[count + made + own :]
        copies = []
        for k, (i, _) in enumerate(far):
            copies.append(pltpu.make_async_copy(ins[i], spare[k], spare[-1].at[k]))
            ins[i] = spare[k]
        for c in copies:
            c.start()
        for c in copies:
            c.wait()
        if not far_out:
            body(*ins, *results, *rest)
            return
        body(*ins, spare[len(far)], *rest)
        last = pltpu.make_async_copy(spare[len(far)], results[0], spare[-1].at[len(far)])
        last.start()
        last.wait()

    more = [shape for _, shape in far] + ([VM(outs[0], f32)] if far_out else [])
    if more:
        more.append(pltpu.SemaphoreType.DMA((len(more),)))
    made_in = pltpu.HBM if far_out else pltpu.VMEM
    got = pl.pallas_call(
        kernel,
        out_shape=[(pltpu.HBM if far_out else jax.ShapeDtypeStruct)(shape, f32) for shape in outs],
        in_specs=specs,
        out_specs=[pl.BlockSpec(memory_space=made_in)] * made,
        scratch_shapes=list(scratch) + more,
        compiler_params=pltpu.CompilerParams(vmem_limit_bytes=GRANT),
        cost_estimate=pl.CostEstimate(
            flops=int(flops), bytes_accessed=8 * sum(map(math.prod, outs)), transcendentals=0
        ),
    )

    def placed(*arrays):
        arrays = list(arrays)
        for i, _ in far:
            arrays[i] = pltpu.with_memory_space_constraint(arrays[i], pltpu.HBM)
        results = got(*arrays)
        return results[0] if isinstance(out_shapes[0], int) else results

    return placed


VM = pltpu.VMEM
SM = pltpu.SMEM


def pack_kernel(owner, tile, residual, position, out, count):
    n_base, n_slab = 4, 32
    out[...] = jnp.zeros_like(out)

    def clear(i, _):
        count[i] = 0
        return 0

    lax.fori_loop(0, count.shape[0], clear, 0, unroll=8)
    lane = lax.broadcasted_iota(jnp.int32, (1, 128), 1)

    def step(i, _):
        o, t = owner[i], tile[i]
        row = (o & (n_slab - 1)) * 2 + (t >> 4)
        group, col = o >> 5, t & 15
        flip = (row >= n_slab).astype(jnp.int32)
        row = jnp.where(flip == 1, 2 * n_slab - 1 - row, row)
        group = jnp.where(flip == 1, n_base - 1 - group, group)
        col = jnp.where(flip == 1, 15 - col, col)
        k = count[o]
        count[o] = k + 1
        slot = flip * 2 + (k & 1)
        to = group * n_slab + row
        for part in range(2):
            out[to, slot * 4 + part] = residual[i, part : part + 1, :]
            out[to, slot * 4 + 2 + part] = position[i, part : part + 1, :]
        out[to, 16] = jnp.where(lane == slot, (col + 1).astype(f32), out[to, 16])
        return 0

    lax.fori_loop(0, owner.shape[0], step, 0)


def taps(d):
    x = jnp.maximum(1.0 - d * d, 0.0)
    return x * x * x


def grid_whole_kernel(first, tags, data, total, cells, order):
    grid_into(first, 0, tags, data, total, cells, order)


def grid_parts_kernel(first, me, tags, data, out0, out1, out2, out3, cells, order, total):
    grid_into(first, me[0], tags, data, total, cells, order)
    for k, out in enumerate((out0, out1, out2, out3)):
        out[...] = total[k]


def grid_into(first, me, tags, data, total, cells, order):
    slots, wide = tags.shape[0], total.shape[2]
    for axis in range(2):
        at = lax.broadcasted_iota(jnp.int32, (TILE, TILE), axis).astype(f32)
        cells[2 * axis] = at * 0.25
        cells[2 * axis + 1] = (float(TILE) - at) * 0.25
    total[...] = jnp.zeros_like(total)

    def scan(s, n):
        order[n] = s
        tag = tags[s] - first
        return n + ((tag > 0) & (tag <= wide)).astype(jnp.int32)

    n = lax.fori_loop(0, slots, scan, jnp.int32(0), unroll=8)
    for extra in range(GROUP):
        order[n + extra] = 0

    def down(row):
        return jnp.transpose(jnp.broadcast_to(row, (TILE, TILE)))

    def group(g, _):
        for u in range(GROUP):
            at = g * GROUP + u
            s = order[at]
            used = (at < n).astype(f32)
            src, slot = s >> 2, s & 3
            flip = slot >> 1
            t = jnp.clip(tags[s] - first - 1, 0, wide - 1)
            value_re = data[src, slot * 4] * used
            value_im = data[src, slot * 4 + 1] * (used * (1.0 - 2.0 * flip.astype(f32)))
            rows = taps(cells[flip] - data[src, slot * 4 + 2] * 0.25)
            cols = taps(cells[2 + flip] - down(data[src, slot * 4 + 3] * 0.25))
            weighted = jnp.concatenate([cols * down(value_re), cols * down(value_im)], axis=1)
            sub = mm(spread(rows, LEFT[6], 1), spread(weighted, RIGHT[6], 0))
            for q in range(4):
                for ri in range(2):
                    total[(q - me) & 3, ri, t] += sub[32 * q : 32 * q + 32, 128 * ri : 128 * ri + 128]
        return 0

    lax.fori_loop(0, (n + GROUP - 1) // GROUP, group, 0)


def cols_kernel(*refs):
    me, whole, parts, (tw, w, out, mid) = refs[0], refs[1], refs[2:6], refs[6:]

    def tile(b, ri, at):
        group = b // 16
        if b % 16 < 8:
            return whole[(me[0] + group) & 3, ri, b % 8, at, :]
        return parts[-group % 4][ri, b % 8, at, :]

    def rows(i, _):
        at = pl.ds(pl.multiple_of(i * 8, 8), 8)
        first = [(tile(b, 0, at), tile(b, 1, at)) for b in range(64)]
        for c, (re, im) in enumerate(fft_list(first)):
            cos, sin = tw[me[0], 0, c : c + 1, :], tw[me[0], 1, c : c + 1, :]
            mid[c, at, 0:128] = re * cos - im * sin
            mid[c, at, 128:256] = re * sin + im * cos
        return 0

    lax.fori_loop(0, 4, rows, 0)
    for pair in range(8):
        part = spread(mid[8 * pair : 8 * pair + 8].reshape(256, 256), RIGHT[6], 1)
        res = mm(w[...], part, NT)
        for k in range(2):
            chunk = 2 * pair + k
            for ri in range(2):
                out[:, chunk // 8, ri * 8 + chunk % 8, :] = res[64 * ri : 64 * ri + 64, 128 * k : 128 * k + 128]


def row_kernel(xi, amplitude, tw, w, out, mid):
    def rows(i, _):
        at = pl.ds(pl.multiple_of(i * 8, 8), 8)
        first = [
            xi[at, 128 * b : 128 * b + 128] * amplitude[at, 128 * b : 128 * b + 128] for b in range(32)
        ]
        half = rfft_list(first)
        for c in range(32):
            cos, sin = tw[0, c : c + 1, :], tw[1, c : c + 1, :]
            re, im = half[c] if c <= 16 else half[32 - c]
            if im is None:
                mid[c, at, 0:128] = re * cos
                mid[c, at, 128:256] = re * sin
            else:
                im = im if c <= 16 else -im
                mid[c, at, 0:128] = re * cos - im * sin
                mid[c, at, 128:256] = re * sin + im * cos
        return 0

    lax.fori_loop(0, 4, rows, 0)
    for pair in range(4):
        part = spread(mid[8 * pair : 8 * pair + 8].reshape(256, 256), RIGHT[3], 1)
        res = mm(w[...], part, NT)
        for k in range(2):
            for ri in range(2):
                out[:, ri * 8 + 2 * pair + k, :] = res[128 * ri : 128 * ri + 128, 128 * k : 128 * k + 128]


def chunks(ref, pair):
    return jnp.concatenate(
        [jnp.concatenate([ref[:, ri * 8 + 2 * pair + k, :] for k in range(2)], axis=1) for ri in range(2)],
        axis=0,
    )


def twist(re, im, tw):
    return re * tw[0] - im * tw[1], re * tw[1] + im * tw[0]


def halves(a, at):
    return [a[at : at + 128, 128 * k : 128 * k + 128] for k in range(2)]


def stacked(rows):
    return jnp.concatenate([jnp.concatenate(r, axis=1) for r in rows], axis=0)


def sky_kernel(field, w, tw, r, out):
    for pair in range(4):
        a = mm(w[...], spread(chunks(field, pair), RIGHT[3], 0))
        turn = stacked([twist(re, im, tw) for re, im in zip(halves(a, 0), halves(a, 128))])
        out[pair] = jnp.exp(mm(spread(turn, LEFT[3], 1), r[...]))


def image_kernel(sky, uv, w, tw_f, r_y, w_b, tw_b, r_b, out):
    for pair in range(4):
        a = mm(w_b[...], spread(chunks(uv, pair), RIGHT[6], 0))
        parts = [[], []]
        for h in range(2):
            for k, (re, im) in enumerate(zip(halves(a, 256 * h), halves(a, 256 * h + 128))):
                parts[k] += twist(re, im, tw_b[h])
        back = mm(spread(stacked(parts), LEFT[6], 1), r_b[...])
        a = mm(spread(sky[pair] * back, LEFT[3], 1), r_y[...])
        turn = [twist(a[128 * k : 128 * k + 128, 0:128], a[128 * k : 128 * k + 128, 128:256], tw_f) for k in range(2)]
        turn = jnp.concatenate([jnp.concatenate([turn[k][ri] for k in range(2)], axis=1) for ri in range(2)], axis=0)
        res = mm(w[...], spread(turn, RIGHT[3], 0))
        for ri in range(2):
            for k in range(2):
                out[:, ri * 8 + 2 * pair + k, :] = res[128 * ri : 128 * ri + 128, 128 * k : 128 * k + 128]


def last_kernel(folded, amplitude, tw, w, out, mid):
    for j in range(8):
        z = jnp.concatenate([folded[:, j, :], folded[:, 8 + j, :]], axis=0)
        v = mm(spread(z, LEFT[3], 0), w[...], TN)
        for k in range(4):
            c = 4 * j + k
            cos, sin = tw[0, c : c + 1, :], tw[1, c : c + 1, :]
            re, im = v[32 * k : 32 * k + 32, 0:128], v[32 * k : 32 * k + 32, 128:256]
            mid[c, :, 0:128] = re * cos - im * sin
            mid[c, :, 128:256] = re * sin + im * cos

    def rows(i, _):
        at = pl.ds(pl.multiple_of(i * 8, 8), 8)
        first = [(mid[c, at, 0:128], mid[c, at, 128:256]) for c in range(32)]
        for b, (re, im) in enumerate(fft_list(first)):
            to = slice(128 * b, 128 * b + 128)
            out[at, to] = amplitude[at, to] * (re + im) * (1.0 / IMG)
        return 0

    lax.fori_loop(0, 4, rows, 0)


def per_device(residual, position, owner, tile_local, xi, amplitude):
    n_base = lax.axis_size("base")
    n_slab = lax.axis_size("slab")
    devices = n_base * n_slab
    everywhere = ("base", "slab")
    t = {k: jnp.asarray(v) for k, v in tables(n_base, n_slab).items()}

    def exchange(a, axis):
        return lax.all_to_all(a, axis, split_axis=0, concat_axis=0, tiled=True)

    rows, width = xi.shape
    blocks = residual.shape[0]
    me = lax.axis_index("base").astype(jnp.int32).reshape(1)
    packed = call(
        pack_kernel,
        (devices, 17, 1, 128),
        [SM, SM, VM, VM],
        [SM((devices,), jnp.int32)],
        2e9,
        [
            (0, SM((blocks,), jnp.int32)),
            (1, SM((blocks,), jnp.int32)),
            (2, VM(residual.shape, f32)),
            (3, VM(position.shape, f32)),
        ],
    )(owner[:, 0], tile_local, residual, position)
    data = exchange(packed, everywhere)
    half = call(
        row_kernel,
        (devices, 16, 128),
        [VM] * 4,
        [VM((32, 32, 256), f32)],
        2e9,
        [
            (0, VM((rows, width), f32)),
            (1, VM((rows, width), f32)),
            (2, VM((2, 32, 128), f32)),
            (3, VM((256, 768), bf16)),
        ],
        True,
    )(xi, amplitude, t["tw_row"], t["w128"])

    data, half = lax.optimization_barrier((data, half))
    tags = data[:, 16, 0, 0:4].reshape(4 * devices).astype(jnp.int32)
    spare = [VM((4, TILE, TILE), f32), SM((4 * devices + GROUP,), jnp.int32)]
    shape = (2, 8, 32, 128)
    whole = call(
        functools.partial(grid_whole_kernel, 0), (n_base, *shape), [SM, VM], spare, 2e10
    )(tags, data)
    whole, tags = lax.optimization_barrier((whole, tags))
    whole = exchange(whole, "base")
    parts = call(
        functools.partial(grid_parts_kernel, 8),
        [shape] * n_base,
        [SM, SM, VM],
        [*spare, VM((n_base, *shape), f32)],
        2e10,
    )(me, tags, data)
    parts, half = lax.optimization_barrier((parts, half))
    parts = [parts[0]] + [
        lax.ppermute(parts[k], "base", [(i, (i + k) % n_base) for i in range(n_base)]) for k in range(1, n_base)
    ]
    half = exchange(half, everywhere)
    cols = call(
        cols_kernel,
        (devices // 2, 2, 16, 128),
        [SM] + [VM] * 7,
        [VM((64, 32, 256), f32)],
        4e9,
    )(me, whole, *parts, t["tw_cols"], t["w_cols"])
    cols = exchange(cols.reshape(devices, 16, 128), everywhere)
    sky = call(
        sky_kernel,
        (4, 256, 128),
        [VM] * 4,
        (),
        4e9,
        [
            (0, VM((devices, 16, 128), f32)),
            (1, VM((256, 768), bf16)),
            (2, VM((2, 128, 128), f32)),
            (3, VM((768, 128), bf16)),
        ],
        True,
    )(half, t["w128"], t["tw_f"], t["r_f"])
    fold = call(
        image_kernel,
        (devices, 16, 128),
        [VM] * 8,
        (),
        8e9,
        [
            (0, VM((4, 256, 128), f32)),
            (2, VM((256, 768), bf16)),
            (3, VM((2, 128, 128), f32)),
            (4, VM((384, 256), bf16)),
            (5, VM((512, 1536), bf16)),
            (6, VM((2, 2, 128, 128), f32)),
            (7, VM((3072, 128), bf16)),
        ],
    )(sky, cols, t["w128"], t["tw_f"], t["r_y"], t["w_b"], t["tw_b"], t["r_b"])
    fold = exchange(fold, everywhere)
    return call(last_kernel, (32, IMG), [VM] * 4, [VM((32, 32, 256), f32)], 3e9)(
        fold, amplitude, t["tw_row"], t["w128t"]
    )


def solution(mesh):
    placed = (
        P(("base", "slab"), None, None),
        P(("base", "slab"), None, None),
        P(("base", "slab"), None),
        P(("base", "slab")),
        P(("base", "slab"), None),
        P(("base", "slab"), None),
    )
    return jax.shard_map(
        per_device, mesh=mesh, in_specs=placed, out_specs=P(("base", "slab"), None), check_vma=False
    )
```

```python
import functools
import math

import jax
import jax.numpy as jnp
import ml_dtypes
import numpy as np
from jax import lax
from jax.experimental import pallas as pl
from jax.experimental.pallas import tpu as pltpu
from jax.sharding import PartitionSpec as P

G = 8192
IMG = 4096
TILE = 128
GROUP = 8
GRANT = 20 * 2**20

NN = (((1,), (0,)), ((), ()))
NT = (((1,), (1,)), ((), ()))
TN = (((0,), (0,)), ((), ()))
f32 = jnp.float32
bf16 = jnp.bfloat16


LEFT = {6: (0, 0, 1, 1, 0, 2), 3: (0, 0, 1)}
RIGHT = {6: (0, 1, 0, 1, 2, 0), 3: (0, 1, 0)}


def pieces(x, count=3):
    out, rest = [], x
    for k in range(count):
        out.append(rest.astype(bf16))
        if k + 1 < count:
            rest = rest - out[-1].astype(f32)
    return out


def spread(x, order, axis):
    cut = pieces(x, max(order) + 1)
    return jnp.concatenate([cut[k] for k in order], axis=axis)


def mm(a, b, dims=NN):
    return lax.dot_general(a, b, dims, preferred_element_type=f32)


def spread_table(x, order, axis):
    cut, rest = [], x.astype(np.float64)
    for _ in range(max(order) + 1):
        cut.append(rest.astype(np.float32).astype(ml_dtypes.bfloat16))
        rest = rest - cut[-1].astype(np.float64)
    return np.concatenate([cut[k] for k in order], axis=axis)


def wave(rows, cols, modulus):
    turn = np.outer(rows, cols).astype(np.int64) % modulus
    angle = turn * (2.0 * np.pi / modulus)
    return np.cos(angle), np.sin(angle)


def turned(c, s):
    return np.block([[c, -s], [s, c]])


@functools.lru_cache(None)
def tables(n_base, n_slab):
    n = np.arange
    devices = n_base * n_slab
    out = {}
    c, s = wave(n(128), n(128), 128)
    out["w128"] = spread_table(turned(c, s), LEFT[3], 1)
    out["w128t"] = spread_table(turned(c, s).T, RIGHT[3], 0)
    out["tw_row"] = np.stack(wave(n(32), n(128), IMG))
    c, s = wave(n(64) + 32, n(128), 128)
    out["w_cols"] = spread_table(turned(c, s), LEFT[6], 1)
    out["w_back"] = spread_table(turned(c[::-1], s[::-1]), LEFT[6], 1)
    out["tw_cols"] = np.stack([np.stack(wave(n(64), n(128) + G // n_base * me, G)) for me in range(n_base)])
    eye = np.eye(4)
    c, s = wave(n(128), n(32), IMG)
    out["tw_f"] = np.stack([np.tile(c, (1, 4)), np.tile(s, (1, 4))])
    c, s = wave(n(32), n(32), 32)
    out["r_f"] = spread_table(np.concatenate([np.kron(eye, c + s), np.kron(eye, c - s)]) / IMG, RIGHT[3], 0)
    out["r_y"] = spread_table(np.concatenate([np.kron(eye, c), np.kron(eye, s)], axis=1), RIGHT[3], 0)
    src = n(devices)
    place = (src % n_slab) * n_base + src // n_slab
    wb, twb, rb = [], [], []
    for half in range(2):
        c, s = wave(n(128) + 128 * half, place, 256)
        wb.append(turned(c, s))
        c, s = wave(n(128) + 128 * half, n(32), G)
        twb.append(np.stack([np.tile(c, (1, 4)), np.tile(s, (1, 4))]))
        c, s = wave(n(32), n(32) // 2 + 8, 32)
        keep = (n(32) % 2 == half)[None, :]
        rb += [np.kron(eye, c * keep) / G, np.kron(eye, -s * keep) / G]
    out["w_b"] = spread_table(np.concatenate(wb), LEFT[6], 1)
    out["tw_b"] = np.stack(twb)
    out["r_b"] = spread_table(np.concatenate(rb), RIGHT[6], 0)
    return {k: v if v.dtype == ml_dtypes.bfloat16 else v.astype(np.float32) for k, v in out.items()}


def times(z, k, n):
    re, im = z
    k %= n
    if k == 0:
        return z
    if 4 * k == n:
        return -im, re
    c, s = math.cos(2 * math.pi * k / n), math.sin(2 * math.pi * k / n)
    if 8 * k == n:
        return (re - im) * c, (re + im) * c
    if 8 * k == 3 * n:
        return (re + im) * -s, (re - im) * s
    return re * c - im * s, re * s + im * c


def fft_list(xs):
    n = len(xs)
    if n == 1:
        return xs
    even, odd = fft_list(xs[0::2]), fft_list(xs[1::2])
    low, high = [], []
    for k in range(n // 2):
        if odd[k] is None:
            low.append(even[k])
            high.append(even[k])
            continue
        (a, b), (c, d) = even[k], times(odd[k], k, n)
        low.append((a + c, b + d))
        high.append((a - c, b - d))
    return low + high


def rfft_list(xs):
    n = len(xs)
    if n == 2:
        return [(xs[0] + xs[1], None), (xs[0] - xs[1], None)]
    even, odd = rfft_list(xs[0::2]), rfft_list(xs[1::2])
    out = [None] * (n // 2 + 1)
    out[0] = (even[0][0] + odd[0][0], None)
    out[n // 2] = (even[0][0] - odd[0][0], None)
    out[n // 4] = (even[n // 4][0], odd[n // 4][0])
    for k in range(1, n // 4):
        (a, b), (c, d) = even[k], times(odd[k], k, n)
        out[k] = (a + c, b + d)
        out[n // 2 - k] = (a - c, d - b)
    return out


def call(body, out_shapes, in_specs, scratch=(), flops=0, far=(), far_out=False):
    outs = [out_shapes] if isinstance(out_shapes[0], int) else list(out_shapes)
    count, own, made = len(in_specs), len(scratch), len(outs)
    specs = [pl.BlockSpec(memory_space=m) for m in in_specs]
    for i, _ in far:
        specs[i] = pl.BlockSpec(memory_space=pltpu.HBM)

    def kernel(*refs):
        ins, results = list(refs[:count]), list(refs[count : count + made])
        rest = refs[count + made : count + made + own]
        spare = refs[count + made + own :]
        copies = []
        for k, (i, _) in enumerate(far):
            copies.append(pltpu.make_async_copy(ins[i], spare[k], spare[-1].at[k]))
            ins[i] = spare[k]
        for c in copies:
            c.start()
        for c in copies:
            c.wait()
        if not far_out:
            body(*ins, *results, *rest)
            return
        body(*ins, spare[len(far)], *rest)
        last = pltpu.make_async_copy(spare[len(far)], results[0], spare[-1].at[len(far)])
        last.start()
        last.wait()

    more = [shape for _, shape in far] + ([VM(outs[0], f32)] if far_out else [])
    if more:
        more.append(pltpu.SemaphoreType.DMA((len(more),)))
    made_in = pltpu.HBM if far_out else pltpu.VMEM
    got = pl.pallas_call(
        kernel,
        out_shape=[(pltpu.HBM if far_out else jax.ShapeDtypeStruct)(shape, f32) for shape in outs],
        in_specs=specs,
        out_specs=[pl.BlockSpec(memory_space=made_in)] * made,
        scratch_shapes=list(scratch) + more,
        compiler_params=pltpu.CompilerParams(vmem_limit_bytes=GRANT),
        cost_estimate=pl.CostEstimate(
            flops=int(flops), bytes_accessed=8 * sum(map(math.prod, outs)), transcendentals=0
        ),
    )

    def placed(*arrays):
        arrays = list(arrays)
        for i, _ in far:
            arrays[i] = pltpu.with_memory_space_constraint(arrays[i], pltpu.HBM)
        results = got(*arrays)
        return results[0] if isinstance(out_shapes[0], int) else results

    return placed


VM = pltpu.VMEM
SM = pltpu.SMEM


def first_kernel(owner, tile, residual, position, xi, amplitude, tw, w, out, count, mid):
    n_base, n_slab = 4, 32
    out[:, 0:17] = jnp.zeros((out.shape[0], 17, 1, 128), f32)

    def clear(i, _):
        count[i] = 0
        return 0

    lax.fori_loop(0, count.shape[0], clear, 0, unroll=8)
    lane = lax.broadcasted_iota(jnp.int32, (1, 128), 1)

    def step(i, _):
        o, t = owner[i], tile[i]
        row = (o & (n_slab - 1)) * 2 + (t >> 4)
        group, col = o >> 5, t & 15
        flip = (row >= n_slab).astype(jnp.int32)
        row = jnp.where(flip == 1, 2 * n_slab - 1 - row, row)
        group = jnp.where(flip == 1, n_base - 1 - group, group)
        col = jnp.where(flip == 1, 15 - col, col)
        k = count[o]
        count[o] = k + 1
        slot = flip * 2 + (k & 1)
        to = group * n_slab + row
        for part in range(2):
            out[to, slot * 4 + part] = residual[i, part : part + 1, :]
            out[to, slot * 4 + 2 + part] = position[i, part : part + 1, :]
        out[to, 16] = jnp.where(lane == slot, (col + 1).astype(f32), out[to, 16])
        return 0

    lax.fori_loop(0, owner.shape[0], step, 0, unroll=4)
    row_transform(xi, amplitude, tw, w, out, mid)


def taps(d):
    x = jnp.maximum(1.0 - d * d, 0.0)
    return x * x * x


def grid_whole_kernel(first, tags, data, total, cells, order):
    grid_into(first, 0, tags, data, total, cells, order)


def grid_parts_kernel(first, me, tags, data, out0, out1, out2, out3, cells, order, total):
    grid_into(first, me[0], tags, data, total, cells, order)
    for k, out in enumerate((out0, out1, out2, out3)):
        out[...] = total[k]


def grid_into(first, me, tags, data, total, cells, order):
    slots, wide = tags.shape[0], total.shape[2]
    for axis in range(2):
        at = lax.broadcasted_iota(jnp.int32, (TILE, TILE), axis).astype(f32)
        cells[2 * axis] = at * 0.25
        cells[2 * axis + 1] = (float(TILE) - at) * 0.25
    total[...] = jnp.zeros_like(total)

    def scan(s, n):
        order[n] = s
        tag = tags[s] - first
        return n + ((tag > 0) & (tag <= wide)).astype(jnp.int32)

    n = lax.fori_loop(0, slots, scan, jnp.int32(0), unroll=8)
    for extra in range(GROUP):
        order[n + extra] = 0

    def down(row):
        return jnp.transpose(jnp.broadcast_to(row, (TILE, TILE)))

    def group(g, _):
        for u in range(GROUP):
            at = g * GROUP + u
            s = order[at]
            used = (at < n).astype(f32)
            src, slot = s >> 2, s & 3
            flip = slot >> 1
            t = jnp.clip(tags[s] - first - 1, 0, wide - 1)
            value_re = data[src, slot * 4] * used
            value_im = data[src, slot * 4 + 1] * (used * (1.0 - 2.0 * flip.astype(f32)))
            rows = taps(cells[flip] - data[src, slot * 4 + 2] * 0.25)
            cols = taps(cells[2 + flip] - down(data[src, slot * 4 + 3] * 0.25))
            weighted = jnp.concatenate([cols * down(value_re), cols * down(value_im)], axis=1)
            sub = mm(spread(rows, LEFT[6], 1), spread(weighted, RIGHT[6], 0))
            for q in range(4):
                for ri in range(2):
                    total[(q - me) & 3, ri, t] += sub[32 * q : 32 * q + 32, 128 * ri : 128 * ri + 128]
        return 0

    lax.fori_loop(0, (n + GROUP - 1) // GROUP, group, 0)


def cols_kernel(*refs):
    me, whole, parts, (tw, w, w_back, out, mid) = refs[0], refs[1], refs[2:6], refs[6:]

    def tile(b, ri, at):
        group = b // 16
        if b % 16 < 8:
            return whole[(me[0] + group) & 3, ri, b % 8, at, :]
        return parts[-group % 4][ri, b % 8, at, :]

    def rows(i, _):
        at = pl.ds(pl.multiple_of(i * 8, 8), 8)
        first = [(tile(b, 0, at), tile(b, 1, at)) for b in range(64)]
        for c, (re, im) in enumerate(fft_list(first)):
            cos, sin = tw[me[0], 0, c : c + 1, :], tw[me[0], 1, c : c + 1, :]
            half, c = c // 32, c % 32
            to = 32 * half + c if c <= 16 else 32 * (1 - half) + 48 - c
            mid[to, at, 0:128] = re * cos - im * sin
            mid[to, at, 128:256] = re * sin + im * cos
        return 0

    lax.fori_loop(0, 4, rows, 0)
    for pair in range(8):
        part = spread(mid[8 * pair : 8 * pair + 8].reshape(256, 256), RIGHT[6], 1)
        res = mm((w if pair % 4 < 2 else w_back)[...], part, NT)
        if pair % 4 == 2:
            own = mm(w[...], part[0:128], NT)
            own = jnp.concatenate([jnp.where(low_lanes(), own, res[:, 0:128]), res[:, 128:256]], axis=1)
            res = own
        for k in range(2):
            chunk = 2 * pair + k
            for ri in range(2):
                out[:, chunk // 8, ri * 8 + chunk % 8, :] = res[64 * ri : 64 * ri + 64, 128 * k : 128 * k + 128]


def row_transform(xi, amplitude, tw, w, out, mid):
    def rows(i, _):
        at = pl.ds(pl.multiple_of(i * 8, 8), 8)
        first = [
            xi[at, 128 * b : 128 * b + 128] * amplitude[at, 128 * b : 128 * b + 128] for b in range(32)
        ]
        for c, (re, im) in enumerate(rfft_list(first)):
            cos, sin = tw[0, c : c + 1, :], tw[1, c : c + 1, :]
            if im is None:
                mid[c, at, 0:128] = re * cos
                mid[c, at, 128:256] = re * sin
            else:
                mid[c, at, 0:128] = re * cos - im * sin
                mid[c, at, 128:256] = re * sin + im * cos
        return 0

    lax.fori_loop(0, 4, rows, 0)
    for pair in range(2):
        part = spread(mid[8 * pair : 8 * pair + 8].reshape(256, 256), RIGHT[3], 1)
        res = mm(w[...], part, NT)
        for k in range(2):
            for ri in range(2):
                out[:, 17 + ri * 4 + 2 * pair + k, 0, :] = res[128 * ri : 128 * ri + 128, 128 * k : 128 * k + 128]
    part = spread(mid[16:20].reshape(128, 256), RIGHT[3], 1)
    res = mm(w[...], part, NT)
    out[:, 25, 0, :] = beside(res[0:128], res[128:256])


def low_lanes():
    return lax.broadcasted_iota(jnp.int32, (128, 128), 1) < 32


def beside(a, b):
    lane = lax.broadcasted_iota(jnp.int32, (128, 128), 1)
    return jnp.where(lane < 32, a, jnp.where(lane < 64, pltpu.roll(b, 32, 1), 0.0))


def column_pairs(field, pair):
    chunk = []
    for k in range(2):
        j = 2 * pair + k
        re, im = field[:, 17 + j % 4, 0, :], field[:, 21 + j % 4, 0, :]
        if j >= 4:
            im = -im
        if j == 4:
            own = field[:, 25, 0, :]
            re, im = jnp.where(low_lanes(), own, re), jnp.where(low_lanes(), pltpu.roll(own, 96, 1), im)
        chunk.append((re, im))
    return jnp.concatenate(
        [jnp.concatenate([chunk[k][ri] for k in range(2)], axis=1) for ri in range(2)], axis=0
    )


def chunks(ref, pair):
    return jnp.concatenate(
        [jnp.concatenate([ref[:, ri * 8 + 2 * pair + k, :] for k in range(2)], axis=1) for ri in range(2)],
        axis=0,
    )


def twist(re, im, tw):
    return re * tw[0] - im * tw[1], re * tw[1] + im * tw[0]


def halves(a, at):
    return [a[at : at + 128, 128 * k : 128 * k + 128] for k in range(2)]


def stacked(rows):
    return jnp.concatenate([jnp.concatenate(r, axis=1) for r in rows], axis=0)


def sky_kernel(field, w, tw, r, out):
    for pair in range(4):
        a = mm(w[...], spread(column_pairs(field, pair), RIGHT[3], 0))
        turn = stacked([twist(re, im, tw) for re, im in zip(halves(a, 0), halves(a, 128))])
        out[pair] = jnp.exp(mm(spread(turn, LEFT[3], 1), r[...]))


def image_kernel(sky, uv, w, tw_f, r_y, w_b, tw_b, r_b, out):
    done = []
    for pair in range(4):
        a = mm(w_b[...], spread(chunks(uv, pair), RIGHT[6], 0))
        parts = [[], []]
        for h in range(2):
            for k, (re, im) in enumerate(zip(halves(a, 256 * h), halves(a, 256 * h + 128))):
                parts[k] += twist(re, im, tw_b[h])
        back = mm(spread(stacked(parts), LEFT[6], 1), r_b[...])
        a = mm(spread(sky[pair] * back, LEFT[3], 1), r_y[...])
        turn = [twist(a[128 * k : 128 * k + 128, 0:128], a[128 * k : 128 * k + 128, 128:256], tw_f) for k in range(2)]
        turn = jnp.concatenate([jnp.concatenate([turn[k][ri] for k in range(2)], axis=1) for ri in range(2)], axis=0)
        done.append(mm(w[...], spread(turn, RIGHT[3], 0)))
    for j in range(4):
        at = slice(128 * (j % 2), 128 * (j % 2) + 128)
        straight, mirrored = done[j // 2][:, at], done[2 + j // 2][:, at]
        re, im = mirrored[0:128], mirrored[128:256]
        if j == 0:
            out[:, 8, 0, :] = beside(re, im)
            re, im = jnp.where(low_lanes(), 0.0, re), jnp.where(low_lanes(), 0.0, im)
        out[:, j, 0, :] = straight[0:128] + im
        out[:, 4 + j, 0, :] = straight[128:256] + re


def last_kernel(folded, amplitude, tw, w, out, mid):
    def residue(c, v):
        cos, sin = tw[0, c : c + 1, :], tw[1, c : c + 1, :]
        re, im = v[:, 0:128], v[:, 128:256]
        mid[c, :, 0:128] = re * cos - im * sin
        mid[c, :, 128:256] = re * sin + im * cos

    for j in range(4):
        z = jnp.concatenate([folded[:, j, 0, :], folded[:, 4 + j, 0, :]], axis=0)
        v = mm(spread(z, LEFT[3], 0), w[...], TN)
        for k in range(4):
            residue(4 * j + k, v[32 * k : 32 * k + 32])
    own = folded[:, 8, 0, :]
    z = jnp.concatenate([own, pltpu.roll(own, 96, 1)], axis=0)
    residue(16, mm(spread(z, LEFT[3], 0), w[...], TN)[0:32])

    def rows(i, _):
        at = pl.ds(pl.multiple_of(i * 8, 8), 8)
        first = [(mid[c, at, 0:128], mid[c, at, 128:256]) for c in range(17)] + [None] * 15
        for b, (re, im) in enumerate(fft_list(first)):
            to = slice(128 * b, 128 * b + 128)
            out[at, to] = amplitude[at, to] * (re + im) * (1.0 / IMG)
        return 0

    lax.fori_loop(0, 4, rows, 0)


def per_device(residual, position, owner, tile_local, xi, amplitude):
    n_base = lax.axis_size("base")
    n_slab = lax.axis_size("slab")
    devices = n_base * n_slab
    everywhere = ("base", "slab")
    t = {k: jnp.asarray(v) for k, v in tables(n_base, n_slab).items()}

    def exchange(a, axis):
        return lax.all_to_all(a, axis, split_axis=0, concat_axis=0, tiled=True)

    rows, width = xi.shape
    blocks = residual.shape[0]
    me = lax.axis_index("base").astype(jnp.int32).reshape(1)
    packed = call(
        first_kernel,
        (devices, 26, 1, 128),
        [SM, SM] + [VM] * 6,
        [SM((devices,), jnp.int32), VM((20, 32, 256), f32)],
        2e9,
        [
            (0, SM((blocks,), jnp.int32)),
            (1, SM((blocks,), jnp.int32)),
            (2, VM(residual.shape, f32)),
            (3, VM(position.shape, f32)),
            (4, VM((rows, width), f32)),
            (5, VM((rows, width), f32)),
            (6, VM((2, 32, 128), f32)),
            (7, VM((256, 768), bf16)),
        ],
    )(owner[:, 0], tile_local, residual, position, xi, amplitude, t["tw_row"], t["w128"])
    data = exchange(packed, everywhere)
    tags = data[:, 16, 0, 0:4].reshape(4 * devices).astype(jnp.int32)
    spare = [VM((4, TILE, TILE), f32), SM((4 * devices + GROUP,), jnp.int32)]
    shape = (2, 8, 32, 128)
    whole = call(
        functools.partial(grid_whole_kernel, 0), (n_base, *shape), [SM, VM], spare, 2e10
    )(tags, data)
    whole, tags = lax.optimization_barrier((whole, tags))
    whole = exchange(whole, "base")
    parts = call(
        functools.partial(grid_parts_kernel, 8),
        [shape] * n_base,
        [SM, SM, VM],
        [*spare, VM((n_base, *shape), f32)],
        2e10,
    )(me, tags, data)
    parts, field = lax.optimization_barrier((parts, data))
    parts = [parts[0]] + [
        lax.ppermute(parts[k], "base", [(i, (i + k) % n_base) for i in range(n_base)]) for k in range(1, n_base)
    ]
    sky = call(
        sky_kernel,
        (4, 256, 128),
        [VM] * 4,
        (),
        4e9,
        [(1, VM((256, 768), bf16)), (2, VM((2, 128, 128), f32)), (3, VM((768, 128), bf16))],
        True,
    )(field, t["w128"], t["tw_f"], t["r_f"])
    parts[0], sky = lax.optimization_barrier((parts[0], sky))
    cols = call(
        cols_kernel,
        (devices // 2, 2, 16, 128),
        [SM] + [VM] * 8,
        [VM((64, 32, 256), f32)],
        4e9,
        [
            (1, VM((n_base, *shape), f32)),
            (6, VM((n_base, 2, 64, 128), f32)),
            (7, VM((128, 1536), bf16)),
            (8, VM((128, 1536), bf16)),
        ],
    )(me, whole, *parts, t["tw_cols"], t["w_cols"], t["w_back"])
    cols = exchange(cols.reshape(devices, 16, 128), everywhere)
    fold = call(
        image_kernel,
        (devices, 9, 1, 128),
        [VM] * 8,
        (),
        8e9,
        [
            (0, VM((4, 256, 128), f32)),
            (2, VM((256, 768), bf16)),
            (3, VM((2, 128, 128), f32)),
            (4, VM((384, 256), bf16)),
            (5, VM((512, 1536), bf16)),
            (6, VM((2, 2, 128, 128), f32)),
            (7, VM((3072, 128), bf16)),
        ],
    )(sky, cols, t["w128"], t["tw_f"], t["r_y"], t["w_b"], t["tw_b"], t["r_b"])
    fold = exchange(fold, everywhere)
    return call(last_kernel, (32, IMG), [VM] * 4, [VM((32, 32, 256), f32)], 3e9)(
        fold, amplitude, t["tw_row"], t["w128t"]
    )


def solution(mesh):
    placed = (
        P(("base", "slab"), None, None),
        P(("base", "slab"), None, None),
        P(("base", "slab"), None),
        P(("base", "slab")),
        P(("base", "slab"), None),
        P(("base", "slab"), None),
    )
    return jax.shard_map(
        per_device, mesh=mesh, in_specs=placed, out_specs=P(("base", "slab"), None), check_vma=False
    )
```

```python
import functools
import math

import jax
import jax.numpy as jnp
import ml_dtypes
import numpy as np
from jax import lax
from jax.experimental import pallas as pl
from jax.experimental.pallas import tpu as pltpu
from jax.sharding import PartitionSpec as P

G = 8192
IMG = 4096
TILE = 128
GROUP = 8
GRANT = 20 * 2**20

NN = (((1,), (0,)), ((), ()))
NT = (((1,), (1,)), ((), ()))
TN = (((0,), (0,)), ((), ()))
f32 = jnp.float32
bf16 = jnp.bfloat16


LEFT = {6: (0, 0, 1, 1, 0, 2), 3: (0, 0, 1)}
RIGHT = {6: (0, 1, 0, 1, 2, 0), 3: (0, 1, 0)}


def pieces(x, count=3):
    out, rest = [], x
    for k in range(count):
        out.append(rest.astype(bf16))
        if k + 1 < count:
            rest = rest - out[-1].astype(f32)
    return out


def spread(x, order, axis):
    cut = pieces(x, max(order) + 1)
    return jnp.concatenate([cut[k] for k in order], axis=axis)


def mm(a, b, dims=NN):
    return lax.dot_general(a, b, dims, preferred_element_type=f32)


def spread_table(x, order, axis):
    cut, rest = [], x.astype(np.float64)
    for _ in range(max(order) + 1):
        cut.append(rest.astype(np.float32).astype(ml_dtypes.bfloat16))
        rest = rest - cut[-1].astype(np.float64)
    return np.concatenate([cut[k] for k in order], axis=axis)


def wave(rows, cols, modulus):
    turn = np.outer(rows, cols).astype(np.int64) % modulus
    angle = turn * (2.0 * np.pi / modulus)
    return np.cos(angle), np.sin(angle)


def turned(c, s):
    return np.block([[c, -s], [s, c]])


@functools.lru_cache(None)
def tables(n_base, n_slab):
    n = np.arange
    devices = n_base * n_slab
    out = {}
    c, s = wave(n(128), n(128), 128)
    out["w128"] = spread_table(turned(c, s), LEFT[3], 1)
    out["w128t"] = spread_table(turned(c, s).T, RIGHT[3], 0)
    out["tw_row"] = np.stack(wave(n(32), n(128), IMG))
    c, s = wave(n(64) + 32, n(128), 128)
    out["w_cols"] = spread_table(turned(c, s), LEFT[6], 1)
    out["w_back"] = spread_table(turned(c[::-1], s[::-1]), LEFT[6], 1)
    out["tw_cols"] = np.stack([np.stack(wave(n(64), n(128) + G // n_base * me, G)) for me in range(n_base)])
    eye = np.eye(4)
    c, s = wave(n(128), n(32), IMG)
    out["tw_f"] = np.stack([np.tile(c, (1, 4)), np.tile(s, (1, 4))])
    c, s = wave(n(32), n(32), 32)
    out["r_f"] = spread_table(np.concatenate([np.kron(eye, c + s), np.kron(eye, c - s)]) / IMG, RIGHT[3], 0)
    out["r_y"] = spread_table(np.concatenate([np.kron(eye, c), np.kron(eye, s)], axis=1), RIGHT[3], 0)
    src = n(devices)
    place = (src % n_slab) * n_base + src // n_slab
    wb, twb, rb = [], [], []
    for half in range(2):
        c, s = wave(n(128) + 128 * half, place, 256)
        wb.append(turned(c, s))
        c, s = wave(n(128) + 128 * half, n(32), G)
        twb.append(np.stack([np.tile(c, (1, 4)), np.tile(s, (1, 4))]))
        c, s = wave(n(32), n(32) // 2 + 8, 32)
        keep = (n(32) % 2 == half)[None, :]
        rb += [np.kron(eye, c * keep) / G, np.kron(eye, -s * keep) / G]
    out["w_b"] = spread_table(np.concatenate(wb), LEFT[6], 1)
    out["tw_b"] = np.stack(twb)
    out["r_b"] = spread_table(np.concatenate(rb), RIGHT[6], 0)
    return {k: v if v.dtype == ml_dtypes.bfloat16 else v.astype(np.float32) for k, v in out.items()}


def times(z, k, n):
    re, im = z
    k %= n
    if k == 0:
        return z
    if 4 * k == n:
        return -im, re
    c, s = math.cos(2 * math.pi * k / n), math.sin(2 * math.pi * k / n)
    if 8 * k == n:
        return (re - im) * c, (re + im) * c
    if 8 * k == 3 * n:
        return (re + im) * -s, (re - im) * s
    return re * c - im * s, re * s + im * c


def fft_list(xs):
    n = len(xs)
    if n == 1:
        return xs
    even, odd = fft_list(xs[0::2]), fft_list(xs[1::2])
    low, high = [], []
    for k in range(n // 2):
        if odd[k] is None:
            low.append(even[k])
            high.append(even[k])
            continue
        (a, b), (c, d) = even[k], times(odd[k], k, n)
        low.append((a + c, b + d))
        high.append((a - c, b - d))
    return low + high


def rfft_list(xs):
    n = len(xs)
    if n == 2:
        return [(xs[0] + xs[1], None), (xs[0] - xs[1], None)]
    even, odd = rfft_list(xs[0::2]), rfft_list(xs[1::2])
    out = [None] * (n // 2 + 1)
    out[0] = (even[0][0] + odd[0][0], None)
    out[n // 2] = (even[0][0] - odd[0][0], None)
    out[n // 4] = (even[n // 4][0], odd[n // 4][0])
    for k in range(1, n // 4):
        (a, b), (c, d) = even[k], times(odd[k], k, n)
        out[k] = (a + c, b + d)
        out[n // 2 - k] = (a - c, d - b)
    return out


class Late:
    def __init__(self, ref, copy):
        self.ref, self.copy, self.shape = ref, copy, ref.shape

    def ready(self):
        if self.copy is not None:
            self.copy.wait()
            self.copy = None
        return self.ref

    def __getitem__(self, at):
        return self.ready()[at]


def call(body, out_shapes, in_specs, scratch=(), flops=0, far=(), far_out=False):
    outs = [out_shapes] if isinstance(out_shapes[0], int) else list(out_shapes)
    count, own, made = len(in_specs), len(scratch), len(outs)
    specs = [pl.BlockSpec(memory_space=m) for m in in_specs]
    for i, _ in far:
        specs[i] = pl.BlockSpec(memory_space=pltpu.HBM)

    def kernel(*refs):
        ins, results = list(refs[:count]), list(refs[count : count + made])
        rest = refs[count + made : count + made + own]
        spare = refs[count + made + own :]
        copies = []
        for k, (i, _) in enumerate(far):
            copies.append(pltpu.make_async_copy(ins[i], spare[k], spare[-1].at[k]))
            copies[-1].start()
            ins[i] = Late(spare[k], copies[-1])
        if not far_out:
            body(*ins, *results, *rest)
            return
        body(*ins, spare[len(far)], *rest)
        last = pltpu.make_async_copy(spare[len(far)], results[0], spare[-1].at[len(far)])
        last.start()
        last.wait()

    more = [shape for _, shape in far] + ([VM(outs[0], f32)] if far_out else [])
    if more:
        more.append(pltpu.SemaphoreType.DMA((len(more),)))
    made_in = pltpu.HBM if far_out else pltpu.VMEM
    got = pl.pallas_call(
        kernel,
        out_shape=[(pltpu.HBM if far_out else jax.ShapeDtypeStruct)(shape, f32) for shape in outs],
        in_specs=specs,
        out_specs=[pl.BlockSpec(memory_space=made_in)] * made,
        scratch_shapes=list(scratch) + more,
        compiler_params=pltpu.CompilerParams(vmem_limit_bytes=GRANT),
        cost_estimate=pl.CostEstimate(
            flops=int(flops), bytes_accessed=8 * sum(map(math.prod, outs)), transcendentals=0
        ),
    )

    def placed(*arrays):
        arrays = list(arrays)
        for i, _ in far:
            arrays[i] = pltpu.with_memory_space_constraint(arrays[i], pltpu.HBM)
        results = got(*arrays)
        return results[0] if isinstance(out_shapes[0], int) else results

    return placed


VM = pltpu.VMEM
SM = pltpu.SMEM


def first_kernel(owner, tile, residual, position, xi, amplitude, tw, w, out, count, mid):
    n_base, n_slab = 4, 32
    out[:, 16] = jnp.zeros((out.shape[0], 1, 128), f32)

    def clear(i, _):
        count[i] = 0
        return 0

    lax.fori_loop(0, count.shape[0], clear, 0, unroll=8)
    owner, tile, residual, position = (a.ready() for a in (owner, tile, residual, position))
    lane = lax.broadcasted_iota(jnp.int32, (1, 128), 1)

    def step(i, _):
        o, t = owner[i], tile[i]
        row = (o & (n_slab - 1)) * 2 + (t >> 4)
        group, col = o >> 5, t & 15
        flip = (row >= n_slab).astype(jnp.int32)
        row = jnp.where(flip == 1, 2 * n_slab - 1 - row, row)
        group = jnp.where(flip == 1, n_base - 1 - group, group)
        col = jnp.where(flip == 1, 15 - col, col)
        k = count[o]
        count[o] = k + 1
        slot = flip * 2 + (k & 1)
        to = group * n_slab + row
        for part in range(2):
            out[to, slot * 4 + part] = residual[i, part : part + 1, :]
            out[to, slot * 4 + 2 + part] = position[i, part : part + 1, :]
        out[to, 16] = jnp.where(lane == slot, (col + 1).astype(f32), out[to, 16])
        return 0

    lax.fori_loop(0, owner.shape[0], step, 0, unroll=4)
    row_transform(*(a.ready() for a in (xi, amplitude, tw, w)), out, mid)


def taps(d):
    x = jnp.maximum(1.0 - d * d, 0.0)
    return x * x * x


def grid_whole_kernel(first, tags, data, total, cells, order):
    grid_into(first, 0, tags, data, total, cells, order)


def grid_parts_kernel(first, me, tags, data, out0, out1, out2, out3, cells, order, total):
    grid_into(first, me[0], tags, data, total, cells, order)
    for k, out in enumerate((out0, out1, out2, out3)):
        out[...] = total[k]


def grid_into(first, me, tags, data, total, cells, order):
    slots, wide = tags.shape[0], total.shape[2]
    for axis in range(2):
        at = lax.broadcasted_iota(jnp.int32, (TILE, TILE), axis).astype(f32)
        cells[2 * axis] = at * 0.25
        cells[2 * axis + 1] = (float(TILE) - at) * 0.25
    total[...] = jnp.zeros_like(total)

    def scan(s, n):
        order[n] = s
        tag = tags[s] - first
        return n + ((tag > 0) & (tag <= wide)).astype(jnp.int32)

    n = lax.fori_loop(0, slots, scan, jnp.int32(0), unroll=8)
    for extra in range(GROUP):
        order[n + extra] = order[jnp.maximum(n - 1, 0)]

    def down(row):
        return jnp.transpose(jnp.broadcast_to(row, (TILE, TILE)))

    def group(g, _):
        for u in range(GROUP):
            at = g * GROUP + u
            s = order[at]
            used = (at < n).astype(f32)
            src, slot = s >> 2, s & 3
            flip = slot >> 1
            t = jnp.clip(tags[s] - first - 1, 0, wide - 1)
            value_re = data[src, slot * 4] * used
            value_im = data[src, slot * 4 + 1] * (used * (1.0 - 2.0 * flip.astype(f32)))
            rows = taps(cells[flip] - data[src, slot * 4 + 2] * 0.25)
            cols = taps(cells[2 + flip] - down(data[src, slot * 4 + 3] * 0.25))
            weighted = jnp.concatenate([cols * down(value_re), cols * down(value_im)], axis=1)
            sub = mm(spread(rows, LEFT[6], 1), spread(weighted, RIGHT[6], 0))
            for q in range(4):
                for ri in range(2):
                    total[(q - me) & 3, ri, t] += sub[32 * q : 32 * q + 32, 128 * ri : 128 * ri + 128]
        return 0

    lax.fori_loop(0, (n + GROUP - 1) // GROUP, group, 0)


def cols_kernel(*refs):
    me, whole, parts, (tw, w, w_back, out, mid) = refs[0], refs[1].ready(), refs[2:6], refs[6:]
    tw = tw.ready()

    def tile(b, ri, at):
        group = b // 16
        if b % 16 < 8:
            return whole[(me[0] + group) & 3, ri, b % 8, at, :]
        return parts[-group % 4][ri, b % 8, at, :]

    def rows(i, _):
        at = pl.ds(pl.multiple_of(i * 8, 8), 8)
        first = [(tile(b, 0, at), tile(b, 1, at)) for b in range(64)]
        for c, (re, im) in enumerate(fft_list(first)):
            cos, sin = tw[me[0], 0, c : c + 1, :], tw[me[0], 1, c : c + 1, :]
            half, c = c // 32, c % 32
            to = 32 * half + c if c <= 16 else 32 * (1 - half) + 48 - c
            mid[to, at, 0:128] = re * cos - im * sin
            mid[to, at, 128:256] = re * sin + im * cos
        return 0

    lax.fori_loop(0, 4, rows, 0)
    for pair in range(8):
        part = spread(mid[8 * pair : 8 * pair + 8].reshape(256, 256), RIGHT[6], 1)
        res = mm((w if pair % 4 < 2 else w_back)[...], part, NT)
        if pair % 4 == 2:
            own = mm(w[...], part[0:128], NT)
            own = jnp.concatenate([jnp.where(low_lanes(), own, res[:, 0:128]), res[:, 128:256]], axis=1)
            res = own
        for k in range(2):
            chunk = 2 * pair + k
            for ri in range(2):
                out[:, chunk // 8, ri * 8 + chunk % 8, :] = res[64 * ri : 64 * ri + 64, 128 * k : 128 * k + 128]


def row_transform(xi, amplitude, tw, w, out, mid):
    def rows(i, _):
        at = pl.ds(pl.multiple_of(i * 8, 8), 8)
        first = [
            xi[at, 128 * b : 128 * b + 128] * amplitude[at, 128 * b : 128 * b + 128] for b in range(32)
        ]
        for c, (re, im) in enumerate(rfft_list(first)):
            cos, sin = tw[0, c : c + 1, :], tw[1, c : c + 1, :]
            if im is None:
                mid[c, at, 0:128] = re * cos
                mid[c, at, 128:256] = re * sin
            else:
                mid[c, at, 0:128] = re * cos - im * sin
                mid[c, at, 128:256] = re * sin + im * cos
        return 0

    lax.fori_loop(0, 4, rows, 0)
    for pair in range(2):
        part = spread(mid[8 * pair : 8 * pair + 8].reshape(256, 256), RIGHT[3], 1)
        res = mm(w[...], part, NT)
        for k in range(2):
            for ri in range(2):
                out[:, 17 + ri * 4 + 2 * pair + k, 0, :] = res[128 * ri : 128 * ri + 128, 128 * k : 128 * k + 128]
    part = spread(mid[16:20].reshape(128, 256), RIGHT[3], 1)
    res = mm(w[...], part, NT)
    out[:, 25, 0, :] = beside(res[0:128], res[128:256])


def low_lanes():
    return lax.broadcasted_iota(jnp.int32, (128, 128), 1) < 32


def beside(a, b):
    lane = lax.broadcasted_iota(jnp.int32, (128, 128), 1)
    return jnp.where(lane < 32, a, jnp.where(lane < 64, pltpu.roll(b, 32, 1), 0.0))


def column_pairs(field, pair):
    chunk = []
    for k in range(2):
        j = 2 * pair + k
        re, im = field[:, 17 + j % 4, 0, :], field[:, 21 + j % 4, 0, :]
        if j >= 4:
            im = -im
        if j == 4:
            own = field[:, 25, 0, :]
            re, im = jnp.where(low_lanes(), own, re), jnp.where(low_lanes(), pltpu.roll(own, 96, 1), im)
        chunk.append((re, im))
    return jnp.concatenate(
        [jnp.concatenate([chunk[k][ri] for k in range(2)], axis=1) for ri in range(2)], axis=0
    )


def chunks(ref, pair):
    return jnp.concatenate(
        [jnp.concatenate([ref[:, ri * 8 + 2 * pair + k, :] for k in range(2)], axis=1) for ri in range(2)],
        axis=0,
    )


def twist(re, im, tw):
    return re * tw[0] - im * tw[1], re * tw[1] + im * tw[0]


def halves(a, at):
    return [a[at : at + 128, 128 * k : 128 * k + 128] for k in range(2)]


def stacked(rows):
    return jnp.concatenate([jnp.concatenate(r, axis=1) for r in rows], axis=0)


def sky_kernel(field, w, tw, r, out):
    for pair in range(4):
        a = mm(w[...], spread(column_pairs(field, pair), RIGHT[3], 0))
        turn = stacked([twist(re, im, tw) for re, im in zip(halves(a, 0), halves(a, 128))])
        out[pair] = jnp.exp(mm(spread(turn, LEFT[3], 1), r[...]))


def image_kernel(sky, uv, w, tw_f, r_y, w_b, tw_b, r_b, out):
    done = []
    for pair in range(4):
        a = mm(w_b[...], spread(chunks(uv, pair), RIGHT[6], 0))
        parts = [[], []]
        for h in range(2):
            for k, (re, im) in enumerate(zip(halves(a, 256 * h), halves(a, 256 * h + 128))):
                parts[k] += twist(re, im, tw_b[h])
        back = mm(spread(stacked(parts), LEFT[6], 1), r_b[...])
        a = mm(spread(sky[pair] * back, LEFT[3], 1), r_y[...])
        turn = [twist(a[128 * k : 128 * k + 128, 0:128], a[128 * k : 128 * k + 128, 128:256], tw_f) for k in range(2)]
        turn = jnp.concatenate([jnp.concatenate([turn[k][ri] for k in range(2)], axis=1) for ri in range(2)], axis=0)
        done.append(mm(w[...], spread(turn, RIGHT[3], 0)))
    for j in range(4):
        at = slice(128 * (j % 2), 128 * (j % 2) + 128)
        straight, mirrored = done[j // 2][:, at], done[2 + j // 2][:, at]
        re, im = mirrored[0:128], mirrored[128:256]
        if j == 0:
            out[:, 8, 0, :] = beside(re, im)
            re, im = jnp.where(low_lanes(), 0.0, re), jnp.where(low_lanes(), 0.0, im)
        out[:, j, 0, :] = straight[0:128] + im
        out[:, 4 + j, 0, :] = straight[128:256] + re


def last_kernel(folded, amplitude, tw, w, out, mid):
    def residue(c, v):
        cos, sin = tw[0, c : c + 1, :], tw[1, c : c + 1, :]
        re, im = v[:, 0:128], v[:, 128:256]
        mid[c, :, 0:128] = re * cos - im * sin
        mid[c, :, 128:256] = re * sin + im * cos

    for j in range(4):
        z = jnp.concatenate([folded[:, j, 0, :], folded[:, 4 + j, 0, :]], axis=0)
        v = mm(spread(z, LEFT[3], 0), w[...], TN)
        for k in range(4):
            residue(4 * j + k, v[32 * k : 32 * k + 32])
    own = folded[:, 8, 0, :]
    z = jnp.concatenate([own, pltpu.roll(own, 96, 1)], axis=0)
    residue(16, mm(spread(z, LEFT[3], 0), w[...], TN)[0:32])

    def rows(i, _):
        at = pl.ds(pl.multiple_of(i * 8, 8), 8)
        first = [(mid[c, at, 0:128], mid[c, at, 128:256]) for c in range(17)] + [None] * 15
        for b, (re, im) in enumerate(fft_list(first)):
            to = slice(128 * b, 128 * b + 128)
            out[at, to] = amplitude[at, to] * (re + im) * (1.0 / IMG)
        return 0

    lax.fori_loop(0, 4, rows, 0)


def per_device(residual, position, owner, tile_local, xi, amplitude):
    n_base = lax.axis_size("base")
    n_slab = lax.axis_size("slab")
    devices = n_base * n_slab
    everywhere = ("base", "slab")
    t = {k: jnp.asarray(v) for k, v in tables(n_base, n_slab).items()}

    def exchange(a, axis):
        return lax.all_to_all(a, axis, split_axis=0, concat_axis=0, tiled=True)

    rows, width = xi.shape
    blocks = residual.shape[0]
    me = lax.axis_index("base").astype(jnp.int32).reshape(1)
    packed = call(
        first_kernel,
        (devices, 26, 1, 128),
        [SM, SM] + [VM] * 6,
        [SM((devices,), jnp.int32), VM((20, 32, 256), f32)],
        2e9,
        [
            (0, SM((blocks,), jnp.int32)),
            (1, SM((blocks,), jnp.int32)),
            (2, VM(residual.shape, f32)),
            (3, VM(position.shape, f32)),
            (4, VM((rows, width), f32)),
            (5, VM((rows, width), f32)),
            (6, VM((2, 32, 128), f32)),
            (7, VM((256, 768), bf16)),
        ],
    )(owner[:, 0], tile_local, residual, position, xi, amplitude, t["tw_row"], t["w128"])
    data = exchange(packed, everywhere)
    tags = data[:, 16, 0, 0:4].reshape(4 * devices).astype(jnp.int32)
    spare = [VM((4, TILE, TILE), f32), SM((4 * devices + GROUP,), jnp.int32)]
    shape = (2, 8, 32, 128)
    whole = call(
        functools.partial(grid_whole_kernel, 0), (n_base, *shape), [SM, VM], spare, 2e10
    )(tags, data)
    whole, tags = lax.optimization_barrier((whole, tags))
    whole = exchange(whole, "base")
    parts = call(
        functools.partial(grid_parts_kernel, 8),
        [shape] * n_base,
        [SM, SM, VM],
        [*spare, VM((n_base, *shape), f32)],
        2e10,
    )(me, tags, data)
    parts, field = lax.optimization_barrier((parts, data))
    parts = [parts[0]] + [
        lax.ppermute(parts[k], "base", [(i, (i + k) % n_base) for i in range(n_base)]) for k in range(1, n_base)
    ]
    sky = call(
        sky_kernel,
        (4, 256, 128),
        [VM] * 4,
        (),
        4e9,
        [(1, VM((256, 768), bf16)), (2, VM((2, 128, 128), f32)), (3, VM((768, 128), bf16))],
        True,
    )(field, t["w128"], t["tw_f"], t["r_f"])
    parts[0], sky = lax.optimization_barrier((parts[0], sky))
    cols = call(
        cols_kernel,
        (devices // 2, 2, 16, 128),
        [SM] + [VM] * 8,
        [VM((64, 32, 256), f32)],
        4e9,
        [
            (1, VM((n_base, *shape), f32)),
            (6, VM((n_base, 2, 64, 128), f32)),
            (7, VM((128, 1536), bf16)),
            (8, VM((128, 1536), bf16)),
        ],
    )(me, whole, *parts, t["tw_cols"], t["w_cols"], t["w_back"])
    cols = exchange(cols.reshape(devices, 16, 128), everywhere)
    fold = call(
        image_kernel,
        (devices, 9, 1, 128),
        [VM] * 8,
        (),
        8e9,
        [
            (0, VM((4, 256, 128), f32)),
            (5, VM((512, 1536), bf16)),
            (7, VM((3072, 128), bf16)),
        ],
    )(sky, cols, t["w128"], t["tw_f"], t["r_y"], t["w_b"], t["tw_b"], t["r_b"])
    fold = exchange(fold, everywhere)
    return call(last_kernel, (32, IMG), [VM] * 4, [VM((32, 32, 256), f32)], 3e9)(
        fold, amplitude, t["tw_row"], t["w128t"]
    )


def solution(mesh):
    placed = (
        P(("base", "slab"), None, None),
        P(("base", "slab"), None, None),
        P(("base", "slab"), None),
        P(("base", "slab")),
        P(("base", "slab"), None),
        P(("base", "slab"), None),
    )
    return jax.shard_map(
        per_device, mesh=mesh, in_specs=placed, out_specs=P(("base", "slab"), None), check_vma=False
    )
```

```python
import functools
import math

import jax
import jax.numpy as jnp
import ml_dtypes
import numpy as np
from jax import lax
from jax.experimental import pallas as pl
from jax.experimental.pallas import tpu as pltpu
from jax.sharding import PartitionSpec as P

G = 8192
IMG = 4096
TILE = 128
GROUP = 12
GRANT = 20 * 2**20

NN = (((1,), (0,)), ((), ()))
NT = (((1,), (1,)), ((), ()))
TN = (((0,), (0,)), ((), ()))
f32 = jnp.float32
bf16 = jnp.bfloat16


LEFT = {6: (0, 0, 1, 1, 0, 2), 3: (0, 0, 1)}
RIGHT = {6: (0, 1, 0, 1, 2, 0), 3: (0, 1, 0)}


def pieces(x, count=3):
    out, rest = [], x
    for k in range(count):
        out.append(rest.astype(bf16))
        if k + 1 < count:
            rest = rest - out[-1].astype(f32)
    return out


def spread(x, order, axis):
    cut = pieces(x, max(order) + 1)
    return jnp.concatenate([cut[k] for k in order], axis=axis)


def mm(a, b, dims=NN):
    return lax.dot_general(a, b, dims, preferred_element_type=f32)


def spread_table(x, order, axis):
    cut, rest = [], x.astype(np.float64)
    for _ in range(max(order) + 1):
        cut.append(rest.astype(np.float32).astype(ml_dtypes.bfloat16))
        rest = rest - cut[-1].astype(np.float64)
    return np.concatenate([cut[k] for k in order], axis=axis)


def wave(rows, cols, modulus):
    turn = np.outer(rows, cols).astype(np.int64) % modulus
    angle = turn * (2.0 * np.pi / modulus)
    return np.cos(angle), np.sin(angle)


def turned(c, s):
    return np.block([[c, -s], [s, c]])


@functools.lru_cache(None)
def tables(n_base, n_slab):
    n = np.arange
    devices = n_base * n_slab
    out = {}
    c, s = wave(n(128), n(128), 128)
    out["w128"] = spread_table(turned(c, s), LEFT[3], 1)
    out["w128t"] = spread_table(turned(c, s).T, RIGHT[3], 0)
    out["tw_row"] = np.stack(wave(n(32), n(128), IMG))
    c, s = wave(n(64) + 32, n(128), 128)
    out["w_cols"] = spread_table(turned(c, s), LEFT[6], 1)
    out["w_back"] = spread_table(turned(c[::-1], s[::-1]), LEFT[6], 1)
    out["tw_cols"] = np.stack([np.stack(wave(n(64), n(128) + G // n_base * me, G)) for me in range(n_base)])
    eye = np.eye(4)
    c, s = wave(n(128), n(32), IMG)
    out["tw_f"] = np.stack([np.tile(c, (1, 4)), np.tile(s, (1, 4))])
    c, s = wave(n(32), n(32), 32)
    out["r_f"] = spread_table(np.concatenate([np.kron(eye, c + s), np.kron(eye, c - s)]) / IMG, RIGHT[3], 0)
    out["r_y"] = spread_table(np.concatenate([np.kron(eye, c), np.kron(eye, s)], axis=1), RIGHT[3], 0)
    src = n(devices)
    place = (src % n_slab) * n_base + src // n_slab
    wb, twb, rb = [], [], []
    for half in range(2):
        c, s = wave(n(128) + 128 * half, place, 256)
        wb.append(turned(c, s))
        c, s = wave(n(128) + 128 * half, n(32), G)
        twb.append(np.stack([np.tile(c, (1, 4)), np.tile(s, (1, 4))]))
        c, s = wave(n(32), n(32) // 2 + 8, 32)
        keep = (n(32) % 2 == half)[None, :]
        rb += [np.kron(eye, c * keep) / G, np.kron(eye, -s * keep) / G]
    out["w_b"] = spread_table(np.concatenate(wb), LEFT[3], 1)
    out["tw_b"] = np.stack(twb)
    out["r_b"] = spread_table(np.concatenate(rb), RIGHT[3], 0)
    return {k: v if v.dtype == ml_dtypes.bfloat16 else v.astype(np.float32) for k, v in out.items()}


def times(z, k, n):
    re, im = z
    k %= n
    if k == 0:
        return z
    if 4 * k == n:
        return -im, re
    c, s = math.cos(2 * math.pi * k / n), math.sin(2 * math.pi * k / n)
    if 8 * k == n:
        return (re - im) * c, (re + im) * c
    if 8 * k == 3 * n:
        return (re + im) * -s, (re - im) * s
    return re * c - im * s, re * s + im * c


def fft_list(xs):
    n = len(xs)
    if n == 1:
        return xs
    even, odd = fft_list(xs[0::2]), fft_list(xs[1::2])
    low, high = [], []
    for k in range(n // 2):
        if odd[k] is None:
            low.append(even[k])
            high.append(even[k])
            continue
        (a, b), (c, d) = even[k], times(odd[k], k, n)
        low.append((a + c, b + d))
        high.append((a - c, b - d))
    return low + high


def rfft_list(xs):
    n = len(xs)
    if n == 2:
        return [(xs[0] + xs[1], None), (xs[0] - xs[1], None)]
    even, odd = rfft_list(xs[0::2]), rfft_list(xs[1::2])
    out = [None] * (n // 2 + 1)
    out[0] = (even[0][0] + odd[0][0], None)
    out[n // 2] = (even[0][0] - odd[0][0], None)
    out[n // 4] = (even[n // 4][0], odd[n // 4][0])
    for k in range(1, n // 4):
        (a, b), (c, d) = even[k], times(odd[k], k, n)
        out[k] = (a + c, b + d)
        out[n // 2 - k] = (a - c, d - b)
    return out


class Late:
    def __init__(self, ref, copy):
        self.ref, self.copy, self.shape = ref, copy, ref.shape

    def ready(self):
        if self.copy is not None:
            self.copy.wait()
            self.copy = None
        return self.ref

    def __getitem__(self, at):
        return self.ready()[at]


def call(body, out_shapes, in_specs, scratch=(), flops=0, far=(), far_out=False):
    outs = [out_shapes] if isinstance(out_shapes[0], int) else list(out_shapes)
    count, own, made = len(in_specs), len(scratch), len(outs)
    specs = [pl.BlockSpec(memory_space=m) for m in in_specs]
    for i, _ in far:
        specs[i] = pl.BlockSpec(memory_space=pltpu.HBM)

    def kernel(*refs):
        ins, results = list(refs[:count]), list(refs[count : count + made])
        rest = refs[count + made : count + made + own]
        spare = refs[count + made + own :]
        copies = []
        for k, (i, _) in enumerate(far):
            copies.append(pltpu.make_async_copy(ins[i], spare[k], spare[-1].at[k]))
            copies[-1].start()
            ins[i] = Late(spare[k], copies[-1])
        if not far_out:
            body(*ins, *results, *rest)
            return
        body(*ins, spare[len(far)], *rest)
        last = pltpu.make_async_copy(spare[len(far)], results[0], spare[-1].at[len(far)])
        last.start()
        last.wait()

    more = [shape for _, shape in far] + ([VM(outs[0], f32)] if far_out else [])
    if more:
        more.append(pltpu.SemaphoreType.DMA((len(more),)))
    made_in = pltpu.HBM if far_out else pltpu.VMEM
    got = pl.pallas_call(
        kernel,
        out_shape=[(pltpu.HBM if far_out else jax.ShapeDtypeStruct)(shape, f32) for shape in outs],
        in_specs=specs,
        out_specs=[pl.BlockSpec(memory_space=made_in)] * made,
        scratch_shapes=list(scratch) + more,
        compiler_params=pltpu.CompilerParams(vmem_limit_bytes=GRANT),
        cost_estimate=pl.CostEstimate(
            flops=int(flops), bytes_accessed=8 * sum(map(math.prod, outs)), transcendentals=0
        ),
    )

    def placed(*arrays):
        arrays = list(arrays)
        for i, _ in far:
            arrays[i] = pltpu.with_memory_space_constraint(arrays[i], pltpu.HBM)
        results = got(*arrays)
        return results[0] if isinstance(out_shapes[0], int) else results

    return placed


VM = pltpu.VMEM
SM = pltpu.SMEM


def first_kernel(owner, tile, residual, position, xi, amplitude, tw, w, out, count, mid):
    n_base, n_slab = 4, 32

    def clear(i, _):
        count[i] = 0
        return 0

    lax.fori_loop(0, count.shape[0], clear, 0, unroll=8)
    owner, tile, residual, position = (a.ready() for a in (owner, tile, residual, position))
    lane = lax.broadcasted_iota(jnp.int32, (1, 128), 1)

    def step(i, _):
        o, t = owner[i], tile[i]
        row = (o & (n_slab - 1)) * 2 + (t >> 4)
        group, col = o >> 5, t & 15
        flip = (row >= n_slab).astype(jnp.int32)
        row = jnp.where(flip == 1, 2 * n_slab - 1 - row, row)
        group = jnp.where(flip == 1, n_base - 1 - group, group)
        col = jnp.where(flip == 1, 15 - col, col)
        k = count[o]
        count[o] = k + 1
        slot = flip * 2 + (k & 1)
        to = group * n_slab + row
        for part in range(2):
            out[to, slot * 4 + part] = residual[i, part : part + 1, :]
            out[to, slot * 4 + 2 + part] = position[i, part : part + 1, :]
        out[to, 24] = jnp.where(lane == 64 + slot, (col + 1).astype(f32), out[to, 24])
        return 0

    row_transform(*(a.ready() for a in (xi, amplitude, tw, w)), out, mid)
    lax.fori_loop(0, owner.shape[0], step, 0, unroll=4)


def taps(d):
    x = jnp.maximum(1.0 - d * d, 0.0)
    return x * x * x


def grid_whole_kernel(first, tags, data, total, cells, order):
    grid_into(first, 0, tags, data, total, cells, order)


def grid_parts_kernel(first, me, tags, data, out0, out1, out2, out3, cells, order, total):
    grid_into(first, me[0], tags, data, total, cells, order)
    for k, out in enumerate((out0, out1, out2, out3)):
        out[...] = total[k]


def grid_into(first, me, tags, data, total, cells, order):
    slots, wide = tags.shape[0], total.shape[2]
    for axis in range(2):
        at = lax.broadcasted_iota(jnp.int32, (TILE, TILE), axis).astype(f32)
        cells[2 * axis] = at * 0.25
        cells[2 * axis + 1] = (float(TILE) - at) * 0.25
    total[...] = jnp.zeros_like(total)

    def scan(s, n):
        order[n] = s
        tag = tags[s] - first
        return n + ((tag > 0) & (tag <= wide)).astype(jnp.int32)

    n = lax.fori_loop(0, slots, scan, jnp.int32(0), unroll=8)
    for extra in range(GROUP):
        order[n + extra] = order[jnp.maximum(n - 1, 0)]

    def down(row):
        return jnp.transpose(jnp.broadcast_to(row, (TILE, TILE)))

    def group(g, _):
        for u in range(GROUP):
            at = g * GROUP + u
            s = order[at]
            used = (at < n).astype(f32)
            src, slot = s >> 2, s & 3
            flip = slot >> 1
            t = jnp.clip(tags[s] - first - 1, 0, wide - 1)
            value_re = data[src, slot * 4] * used
            value_im = data[src, slot * 4 + 1] * (used * (1.0 - 2.0 * flip.astype(f32)))
            rows = taps(cells[flip] - data[src, slot * 4 + 2] * 0.25)
            cols = taps(cells[2 + flip] - down(data[src, slot * 4 + 3] * 0.25))
            weighted = jnp.concatenate([cols * down(value_re), cols * down(value_im)], axis=1)
            sub = mm(spread(rows, LEFT[6], 1), spread(weighted, RIGHT[6], 0))
            for q in range(4):
                for ri in range(2):
                    total[(q - me) & 3, ri, t] += sub[32 * q : 32 * q + 32, 128 * ri : 128 * ri + 128]
        return 0

    lax.fori_loop(0, (n + GROUP - 1) // GROUP, group, 0)


def cols_kernel(*refs):
    me, whole, parts, (tw, w, w_back, out, mid) = refs[0], refs[1].ready(), refs[2:6], refs[6:]
    tw = tw.ready()

    def tile(b, ri, at):
        group = b // 16
        if b % 16 < 8:
            return whole[(me[0] + group) & 3, ri, b % 8, at, :]
        return parts[-group % 4][ri, b % 8, at, :]

    def rows(i, _):
        at = pl.ds(pl.multiple_of(i * 8, 8), 8)
        first = [(tile(b, 0, at), tile(b, 1, at)) for b in range(64)]
        for c, (re, im) in enumerate(fft_list(first)):
            cos, sin = tw[me[0], 0, c : c + 1, :], tw[me[0], 1, c : c + 1, :]
            half, c = c // 32, c % 32
            to = 32 * half + c if c <= 16 else 32 * (1 - half) + 48 - c
            mid[to, at, 0:128] = re * cos - im * sin
            mid[to, at, 128:256] = re * sin + im * cos
        return 0

    lax.fori_loop(0, 4, rows, 0)
    for pair in range(8):
        part = spread(mid[8 * pair : 8 * pair + 8].reshape(256, 256), RIGHT[6], 1)
        res = mm((w if pair % 4 < 2 else w_back)[...], part, NT)
        if pair % 4 == 2:
            own = mm(w[...], part[0:128], NT)
            own = jnp.concatenate([jnp.where(low_lanes(), own, res[:, 0:128]), res[:, 128:256]], axis=1)
            res = own
        for k in range(2):
            chunk = 2 * pair + k
            for ri in range(2):
                out[:, chunk // 8, ri * 8 + chunk % 8, :] = res[64 * ri : 64 * ri + 64, 128 * k : 128 * k + 128]


def row_transform(xi, amplitude, tw, w, out, mid):
    def rows(i, _):
        at = pl.ds(pl.multiple_of(i * 8, 8), 8)
        first = [
            xi[at, 128 * b : 128 * b + 128] * amplitude[at, 128 * b : 128 * b + 128] for b in range(32)
        ]
        for c, (re, im) in enumerate(rfft_list(first)):
            cos, sin = tw[0, c : c + 1, :], tw[1, c : c + 1, :]
            if im is None:
                mid[c, at, 0:128] = re * cos
                mid[c, at, 128:256] = re * sin
            else:
                mid[c, at, 0:128] = re * cos - im * sin
                mid[c, at, 128:256] = re * sin + im * cos
        return 0

    lax.fori_loop(0, 4, rows, 0)
    for pair in range(2):
        part = spread(mid[8 * pair : 8 * pair + 8].reshape(256, 256), RIGHT[3], 1)
        res = mm(w[...], part, NT)
        for k in range(2):
            for ri in range(2):
                out[:, 16 + ri * 4 + 2 * pair + k, 0, :] = res[128 * ri : 128 * ri + 128, 128 * k : 128 * k + 128]
    part = spread(mid[16:20].reshape(128, 256), RIGHT[3], 1)
    res = mm(w[...], part, NT)
    out[:, 24, 0, :] = beside(res[0:128], res[128:256])


def low_lanes():
    return lax.broadcasted_iota(jnp.int32, (128, 128), 1) < 32


def beside(a, b):
    lane = lax.broadcasted_iota(jnp.int32, (128, 128), 1)
    return jnp.where(lane < 32, a, jnp.where(lane < 64, pltpu.roll(b, 32, 1), 0.0))


def column_pairs(field, pair):
    chunk = []
    for k in range(2):
        j = 2 * pair + k
        re, im = field[:, 16 + j % 4, 0, :], field[:, 20 + j % 4, 0, :]
        if j >= 4:
            im = -im
        if j == 4:
            own = field[:, 24, 0, :]
            re, im = jnp.where(low_lanes(), own, re), jnp.where(low_lanes(), pltpu.roll(own, 96, 1), im)
        chunk.append((re, im))
    return jnp.concatenate(
        [jnp.concatenate([chunk[k][ri] for k in range(2)], axis=1) for ri in range(2)], axis=0
    )


def chunks(ref, pair):
    return jnp.concatenate(
        [jnp.concatenate([ref[:, ri * 8 + 2 * pair + k, :] for k in range(2)], axis=1) for ri in range(2)],
        axis=0,
    )


def twist(re, im, tw):
    return re * tw[0] - im * tw[1], re * tw[1] + im * tw[0]


def halves(a, at):
    return [a[at : at + 128, 128 * k : 128 * k + 128] for k in range(2)]


def stacked(rows):
    return jnp.concatenate([jnp.concatenate(r, axis=1) for r in rows], axis=0)


def sky_kernel(field, w, tw, r, out):
    for pair in range(4):
        a = mm(w[...], spread(column_pairs(field, pair), RIGHT[3], 0))
        turn = stacked([twist(re, im, tw) for re, im in zip(halves(a, 0), halves(a, 128))])
        out[pair] = jnp.exp(mm(spread(turn, LEFT[3], 1), r[...]))


def image_kernel(sky, uv, w, tw_f, r_y, w_b, tw_b, r_b, out):
    done = []
    for pair in range(4):
        a = mm(w_b[...], spread(chunks(uv, pair), RIGHT[3], 0))
        parts = [[], []]
        for h in range(2):
            for k, (re, im) in enumerate(zip(halves(a, 256 * h), halves(a, 256 * h + 128))):
                parts[k] += twist(re, im, tw_b[h])
        back = mm(spread(stacked(parts), LEFT[3], 1), r_b[...])
        a = mm(spread(sky[pair] * back, LEFT[3], 1), r_y[...])
        turn = [twist(a[128 * k : 128 * k + 128, 0:128], a[128 * k : 128 * k + 128, 128:256], tw_f) for k in range(2)]
        turn = jnp.concatenate([jnp.concatenate([turn[k][ri] for k in range(2)], axis=1) for ri in range(2)], axis=0)
        done.append(mm(w[...], spread(turn, RIGHT[3], 0)))
    for j in range(4):
        at = slice(128 * (j % 2), 128 * (j % 2) + 128)
        straight, mirrored = done[j // 2][:, at], done[2 + j // 2][:, at]
        re, im = mirrored[0:128], mirrored[128:256]
        if j == 0:
            out[:, 8, 0, :] = beside(re, im)
            re, im = jnp.where(low_lanes(), 0.0, re), jnp.where(low_lanes(), 0.0, im)
        out[:, j, 0, :] = straight[0:128] + im
        out[:, 4 + j, 0, :] = straight[128:256] + re


def last_kernel(folded, amplitude, tw, w, out, mid):
    def residue(c, v):
        cos, sin = tw[0, c : c + 1, :], tw[1, c : c + 1, :]
        re, im = v[:, 0:128], v[:, 128:256]
        mid[c, :, 0:128] = re * cos - im * sin
        mid[c, :, 128:256] = re * sin + im * cos

    for j in range(4):
        z = jnp.concatenate([folded[:, j, 0, :], folded[:, 4 + j, 0, :]], axis=0)
        v = mm(spread(z, LEFT[3], 0), w[...], TN)
        for k in range(4):
            residue(4 * j + k, v[32 * k : 32 * k + 32])
    own = folded[:, 8, 0, :]
    z = jnp.concatenate([own, pltpu.roll(own, 96, 1)], axis=0)
    residue(16, mm(spread(z, LEFT[3], 0), w[...], TN)[0:32])

    def rows(i, _):
        at = pl.ds(pl.multiple_of(i * 8, 8), 8)
        first = [(mid[c, at, 0:128], mid[c, at, 128:256]) for c in range(17)] + [None] * 15
        for b, (re, im) in enumerate(fft_list(first)):
            to = slice(128 * b, 128 * b + 128)
            out[at, to] = amplitude[at, to] * (re + im) * (1.0 / IMG)
        return 0

    lax.fori_loop(0, 4, rows, 0)


def per_device(residual, position, owner, tile_local, xi, amplitude):
    n_base = lax.axis_size("base")
    n_slab = lax.axis_size("slab")
    devices = n_base * n_slab
    everywhere = ("base", "slab")
    t = {k: jnp.asarray(v) for k, v in tables(n_base, n_slab).items()}

    def exchange(a, axis):
        return lax.all_to_all(a, axis, split_axis=0, concat_axis=0, tiled=True)

    rows, width = xi.shape
    blocks = residual.shape[0]
    me = lax.axis_index("base").astype(jnp.int32).reshape(1)
    packed = call(
        first_kernel,
        (devices, 25, 1, 128),
        [SM, SM] + [VM] * 6,
        [SM((devices,), jnp.int32), VM((20, 32, 256), f32)],
        2e9,
        [
            (0, SM((blocks,), jnp.int32)),
            (1, SM((blocks,), jnp.int32)),
            (2, VM(residual.shape, f32)),
            (3, VM(position.shape, f32)),
            (4, VM((rows, width), f32)),
            (5, VM((rows, width), f32)),
            (6, VM((2, 32, 128), f32)),
            (7, VM((256, 768), bf16)),
        ],
    )(owner[:, 0], tile_local, residual, position, xi, amplitude, t["tw_row"], t["w128"])
    data = exchange(packed, everywhere)
    tags = data[:, 24, 0, 64:68].reshape(4 * devices).astype(jnp.int32)
    spare = [VM((4, TILE, TILE), f32), SM((4 * devices + GROUP,), jnp.int32)]
    shape = (2, 8, 32, 128)
    whole = call(
        functools.partial(grid_whole_kernel, 0), (n_base, *shape), [SM, VM], spare, 2e10
    )(tags, data)
    whole, tags = lax.optimization_barrier((whole, tags))
    whole = exchange(whole, "base")
    parts = call(
        functools.partial(grid_parts_kernel, 8),
        [shape] * n_base,
        [SM, SM, VM],
        [*spare, VM((n_base, *shape), f32)],
        2e10,
    )(me, tags, data)
    parts, field = lax.optimization_barrier((parts, data))
    parts = [parts[0]] + [
        lax.ppermute(parts[k], "base", [(i, (i + k) % n_base) for i in range(n_base)]) for k in range(1, n_base)
    ]
    sky = call(
        sky_kernel,
        (4, 256, 128),
        [VM] * 4,
        (),
        4e9,
        [(1, VM((256, 768), bf16)), (2, VM((2, 128, 128), f32)), (3, VM((768, 128), bf16))],
        True,
    )(field, t["w128"], t["tw_f"], t["r_f"])
    parts[0], sky = lax.optimization_barrier((parts[0], sky))
    cols = call(
        cols_kernel,
        (devices // 2, 2, 16, 128),
        [SM] + [VM] * 8,
        [VM((64, 32, 256), f32)],
        4e9,
        [
            (1, VM((n_base, *shape), f32)),
            (6, VM((n_base, 2, 64, 128), f32)),
            (7, VM((128, 1536), bf16)),
            (8, VM((128, 1536), bf16)),
        ],
    )(me, whole, *parts, t["tw_cols"], t["w_cols"], t["w_back"])
    cols = exchange(cols.reshape(devices, 16, 128), everywhere)
    fold = call(
        image_kernel,
        (devices, 9, 1, 128),
        [VM] * 8,
        (),
        8e9,
        [
            (0, VM((4, 256, 128), f32)),
            (5, VM((512, 768), bf16)),
            (7, VM((1536, 128), bf16)),
        ],
    )(sky, cols, t["w128"], t["tw_f"], t["r_y"], t["w_b"], t["tw_b"], t["r_b"])
    fold = exchange(fold, everywhere)
    return call(last_kernel, (32, IMG), [VM] * 4, [VM((32, 32, 256), f32)], 3e9)(
        fold, amplitude, t["tw_row"], t["w128t"]
    )


def solution(mesh):
    placed = (
        P(("base", "slab"), None, None),
        P(("base", "slab"), None, None),
        P(("base", "slab"), None),
        P(("base", "slab")),
        P(("base", "slab"), None),
        P(("base", "slab"), None),
    )
    return jax.shard_map(
        per_device, mesh=mesh, in_specs=placed, out_specs=P(("base", "slab"), None), check_vma=False
    )
```

```python
import functools
import math

import jax
import jax.numpy as jnp
import ml_dtypes
import numpy as np
from jax import lax
from jax.experimental import pallas as pl
from jax.experimental.pallas import tpu as pltpu
from jax.sharding import PartitionSpec as P

G = 8192
IMG = 4096
TILE = 128
GROUP = 24
REST = 8
GRANT = 20 * 2**20

NN = (((1,), (0,)), ((), ()))
NT = (((1,), (1,)), ((), ()))
TN = (((0,), (0,)), ((), ()))
f32 = jnp.float32
bf16 = jnp.bfloat16


LEFT = {6: (0, 0, 1, 1, 0, 2), 3: (0, 0, 1)}
RIGHT = {6: (0, 1, 0, 1, 2, 0), 3: (0, 1, 0)}


def pieces(x, count=3):
    out, rest = [], x
    for k in range(count):
        out.append(rest.astype(bf16))
        if k + 1 < count:
            rest = rest - out[-1].astype(f32)
    return out


def spread(x, order, axis):
    cut = pieces(x, max(order) + 1)
    return jnp.concatenate([cut[k] for k in order], axis=axis)


def mm(a, b, dims=NN):
    return lax.dot_general(a, b, dims, preferred_element_type=f32)


def spread_table(x, order, axis):
    cut, rest = [], x.astype(np.float64)
    for _ in range(max(order) + 1):
        cut.append(rest.astype(np.float32).astype(ml_dtypes.bfloat16))
        rest = rest - cut[-1].astype(np.float64)
    return np.concatenate([cut[k] for k in order], axis=axis)


def wave(rows, cols, modulus):
    turn = np.outer(rows, cols).astype(np.int64) % modulus
    angle = turn * (2.0 * np.pi / modulus)
    return np.cos(angle), np.sin(angle)


def turned(c, s):
    return np.block([[c, -s], [s, c]])


@functools.lru_cache(None)
def tables(n_base, n_slab):
    n = np.arange
    devices = n_base * n_slab
    out = {}
    c, s = wave(n(128), n(128), 128)
    out["w128"] = spread_table(turned(c, s), LEFT[3], 1)
    out["w128t"] = spread_table(turned(c, s).T, RIGHT[3], 0)
    out["tw_row"] = np.stack(wave(n(32), n(128), IMG))
    c, s = wave(n(64) + 32, n(128), 128)
    out["w_cols"] = spread_table(turned(c, s), LEFT[6], 1)
    out["w_back"] = spread_table(turned(c[::-1], s[::-1]), LEFT[6], 1)
    out["tw_cols"] = np.stack([np.stack(wave(n(64), n(128) + G // n_base * me, G)) for me in range(n_base)])
    eye = np.eye(4)
    c, s = wave(n(128), n(32), IMG)
    out["tw_f"] = np.stack([np.tile(c, (1, 4)), np.tile(s, (1, 4))])
    c, s = wave(n(32), n(32), 32)
    out["r_f"] = spread_table(np.concatenate([np.kron(eye, c + s), np.kron(eye, c - s)]) / IMG, RIGHT[3], 0)
    out["r_y"] = spread_table(np.concatenate([np.kron(eye, c), np.kron(eye, s)], axis=1), RIGHT[3], 0)
    src = n(devices)
    place = (src % n_slab) * n_base + src // n_slab
    wb, twb, rb = [], [], []
    for half in range(2):
        c, s = wave(n(128) + 128 * half, place, 256)
        wb.append(turned(c, s))
        c, s = wave(n(128) + 128 * half, n(32), G)
        twb.append(np.stack([np.tile(c, (1, 4)), np.tile(s, (1, 4))]))
        c, s = wave(n(32), n(32) // 2 + 8, 32)
        keep = (n(32) % 2 == half)[None, :]
        rb += [np.kron(eye, c * keep) / G, np.kron(eye, -s * keep) / G]
    out["w_b"] = spread_table(np.concatenate(wb), LEFT[3], 1)
    out["tw_b"] = np.stack(twb)
    out["r_b"] = spread_table(np.concatenate(rb), RIGHT[3], 0)
    return {k: v if v.dtype == ml_dtypes.bfloat16 else v.astype(np.float32) for k, v in out.items()}


def times(z, k, n):
    re, im = z
    k %= n
    if k == 0:
        return z
    if 4 * k == n:
        return -im, re
    c, s = math.cos(2 * math.pi * k / n), math.sin(2 * math.pi * k / n)
    if 8 * k == n:
        return (re - im) * c, (re + im) * c
    if 8 * k == 3 * n:
        return (re + im) * -s, (re - im) * s
    return re * c - im * s, re * s + im * c


def fft_list(xs):
    n = len(xs)
    if n == 1:
        return xs
    even, odd = fft_list(xs[0::2]), fft_list(xs[1::2])
    low, high = [], []
    for k in range(n // 2):
        if odd[k] is None:
            low.append(even[k])
            high.append(even[k])
            continue
        (a, b), (c, d) = even[k], times(odd[k], k, n)
        low.append((a + c, b + d))
        high.append((a - c, b - d))
    return low + high


def rfft_list(xs):
    n = len(xs)
    if n == 2:
        return [(xs[0] + xs[1], None), (xs[0] - xs[1], None)]
    even, odd = rfft_list(xs[0::2]), rfft_list(xs[1::2])
    out = [None] * (n // 2 + 1)
    out[0] = (even[0][0] + odd[0][0], None)
    out[n // 2] = (even[0][0] - odd[0][0], None)
    out[n // 4] = (even[n // 4][0], odd[n // 4][0])
    for k in range(1, n // 4):
        (a, b), (c, d) = even[k], times(odd[k], k, n)
        out[k] = (a + c, b + d)
        out[n // 2 - k] = (a - c, d - b)
    return out


class Late:
    def __init__(self, ref, copy):
        self.ref, self.copy, self.shape = ref, copy, ref.shape

    def ready(self):
        if self.copy is not None:
            self.copy.wait()
            self.copy = None
        return self.ref

    def __getitem__(self, at):
        return self.ready()[at]


def call(body, out_shapes, in_specs, scratch=(), flops=0, far=(), far_out=False):
    outs = [out_shapes] if isinstance(out_shapes[0], int) else list(out_shapes)
    count, own, made = len(in_specs), len(scratch), len(outs)
    specs = [pl.BlockSpec(memory_space=m) for m in in_specs]
    for i, _ in far:
        specs[i] = pl.BlockSpec(memory_space=pltpu.HBM)

    def kernel(*refs):
        ins, results = list(refs[:count]), list(refs[count : count + made])
        rest = refs[count + made : count + made + own]
        spare = refs[count + made + own :]
        copies = []
        for k, (i, _) in enumerate(far):
            copies.append(pltpu.make_async_copy(ins[i], spare[k], spare[-1].at[k]))
            copies[-1].start()
            ins[i] = Late(spare[k], copies[-1])
        if not far_out:
            body(*ins, *results, *rest)
            return
        body(*ins, spare[len(far)], *rest)
        last = pltpu.make_async_copy(spare[len(far)], results[0], spare[-1].at[len(far)])
        last.start()
        last.wait()

    more = [shape for _, shape in far] + ([VM(outs[0], f32)] if far_out else [])
    if more:
        more.append(pltpu.SemaphoreType.DMA((len(more),)))
    made_in = pltpu.HBM if far_out else pltpu.VMEM
    got = pl.pallas_call(
        kernel,
        out_shape=[(pltpu.HBM if far_out else jax.ShapeDtypeStruct)(shape, f32) for shape in outs],
        in_specs=specs,
        out_specs=[pl.BlockSpec(memory_space=made_in)] * made,
        scratch_shapes=list(scratch) + more,
        compiler_params=pltpu.CompilerParams(vmem_limit_bytes=GRANT),
        cost_estimate=pl.CostEstimate(
            flops=int(flops), bytes_accessed=8 * sum(map(math.prod, outs)), transcendentals=0
        ),
    )

    def placed(*arrays):
        arrays = list(arrays)
        for i, _ in far:
            arrays[i] = pltpu.with_memory_space_constraint(arrays[i], pltpu.HBM)
        results = got(*arrays)
        return results[0] if isinstance(out_shapes[0], int) else results

    return placed


VM = pltpu.VMEM
SM = pltpu.SMEM


def first_kernel(owner, tile, residual, position, xi, amplitude, tw, w, out, count, mid, tags):
    n_base, n_slab = 4, 32

    def clear(i, _):
        count[i] = 0
        return 0

    lax.fori_loop(0, count.shape[0], clear, 0, unroll=8)
    owner, tile, residual, position = (a.ready() for a in (owner, tile, residual, position))
    lane = lax.broadcasted_iota(jnp.int32, (1, 128), 1)
    tags[...] = jnp.zeros_like(tags)

    def step(i, _):
        placed = []
        for u in range(8):
            at = i * 8 + u
            o, t = owner[at], tile[at]
            row = (o & (n_slab - 1)) * 2 + (t >> 4)
            group, col = o >> 5, t & 15
            flip = (row >= n_slab).astype(jnp.int32)
            row = jnp.where(flip == 1, 2 * n_slab - 1 - row, row)
            group = jnp.where(flip == 1, n_base - 1 - group, group)
            col = jnp.where(flip == 1, 15 - col, col)
            k = count[o]
            count[o] = k + 1
            placed.append((at, group * n_slab + row, flip * 2 + (k & 1), (col + 1).astype(f32)))
        parts = [(residual[at], position[at]) for at, _, _, _ in placed]
        for (at, to, slot, tag), (value, place) in zip(placed, parts):
            for part in range(2):
                out[to, slot * 4 + part] = value[part : part + 1]
                out[to, slot * 4 + 2 + part] = place[part : part + 1]
            tags[to] = jnp.where(lane == 64 + slot, tag, tags[to])
        return 0

    lax.fori_loop(0, owner.shape[0] // 8, step, 0)
    row_transform(*(a.ready() for a in (xi, amplitude, tw, w)), out, mid, tags)


def taps(d):
    x = jnp.maximum(1.0 - d * d, 0.0)
    return x * x * x


def grid_whole_kernel(first, tags, data, total, cells, order):
    grid_into(first, 0, tags, data, total, cells, order)


def grid_parts_kernel(first, me, tags, data, out0, out1, out2, out3, cells, order, total):
    grid_into(first, me[0], tags, data, total, cells, order)
    for k, out in enumerate((out0, out1, out2, out3)):
        out[...] = total[k]


def grid_into(first, me, tags, data, total, cells, order):
    slots, wide = tags.shape[0], total.shape[2]
    for axis in range(2):
        at = lax.broadcasted_iota(jnp.int32, (TILE, TILE), axis).astype(f32)
        cells[2 * axis] = at * 0.25
        cells[2 * axis + 1] = (float(TILE) - at) * 0.25
    total[...] = jnp.zeros_like(total)

    def scan(s, n):
        order[n] = s
        tag = tags[s] - first
        return n + ((tag > 0) & (tag <= wide)).astype(jnp.int32)

    n = lax.fori_loop(0, slots, scan, jnp.int32(0), unroll=8)
    for extra in range(REST):
        order[n + extra] = order[jnp.maximum(n - 1, 0)]

    def down(row):
        return jnp.transpose(jnp.broadcast_to(row, (TILE, TILE)))

    def add(at):
        s = order[at]
        used = (at < n).astype(f32)
        src, slot = s >> 2, s & 3
        flip = slot >> 1
        t = jnp.clip(tags[s] - first - 1, 0, wide - 1)
        value_re = data[src, slot * 4] * used
        value_im = data[src, slot * 4 + 1] * (used * (1.0 - 2.0 * flip.astype(f32)))
        rows = taps(cells[flip] - data[src, slot * 4 + 2] * 0.25)
        cols = taps(cells[2 + flip] - down(data[src, slot * 4 + 3] * 0.25))
        weighted = jnp.concatenate([cols * down(value_re), cols * down(value_im)], axis=1)
        sub = mm(spread(rows, LEFT[6], 1), spread(weighted, RIGHT[6], 0))
        for q in range(4):
            for ri in range(2):
                total[(q - me) & 3, ri, t] += sub[32 * q : 32 * q + 32, 128 * ri : 128 * ri + 128]

    def turn(start, count):
        def body(g, _):
            for u in range(count):
                add(start + g * count + u)
            return 0

        return body

    whole = n // GROUP
    lax.fori_loop(0, whole, turn(0, GROUP), 0)
    begun = whole * GROUP
    lax.fori_loop(0, (n - begun + REST - 1) // REST, turn(begun, REST), 0)


def cols_kernel(*refs):
    me, whole, parts, (tw, w, w_back, out, mid) = refs[0], refs[1].ready(), refs[2:6], refs[6:]
    tw = tw.ready()

    def tile(b, ri, at):
        group = b // 16
        if b % 16 < 8:
            return whole[(me[0] + group) & 3, ri, b % 8, at, :]
        return parts[-group % 4][ri, b % 8, at, :]

    def rows(i, _):
        at = pl.ds(pl.multiple_of(i * 8, 8), 8)
        first = [(tile(b, 0, at), tile(b, 1, at)) for b in range(64)]
        for c, (re, im) in enumerate(fft_list(first)):
            cos, sin = tw[me[0], 0, c : c + 1, :], tw[me[0], 1, c : c + 1, :]
            half, c = c // 32, c % 32
            to = 32 * half + c if c <= 16 else 32 * (1 - half) + 48 - c
            mid[to, at, 0:128] = re * cos - im * sin
            mid[to, at, 128:256] = re * sin + im * cos
        return 0

    lax.fori_loop(0, 4, rows, 0)
    for pair in range(8):
        part = spread(mid[8 * pair : 8 * pair + 8].reshape(256, 256), RIGHT[6], 1)
        res = mm((w if pair % 4 < 2 else w_back)[...], part, NT)
        if pair % 4 == 2:
            own = mm(w[...], part[0:128], NT)
            own = jnp.concatenate([jnp.where(low_lanes(), own, res[:, 0:128]), res[:, 128:256]], axis=1)
            res = own
        for k in range(2):
            chunk = 2 * pair + k
            for ri in range(2):
                out[:, chunk // 8, ri * 8 + chunk % 8, :] = res[64 * ri : 64 * ri + 64, 128 * k : 128 * k + 128]


def row_transform(xi, amplitude, tw, w, out, mid, tags):
    def rows(i, _):
        at = pl.ds(pl.multiple_of(i * 8, 8), 8)
        first = [
            xi[at, 128 * b : 128 * b + 128] * amplitude[at, 128 * b : 128 * b + 128] for b in range(32)
        ]
        for c, (re, im) in enumerate(rfft_list(first)):
            cos, sin = tw[0, c : c + 1, :], tw[1, c : c + 1, :]
            if im is None:
                mid[c, at, 0:128] = re * cos
                mid[c, at, 128:256] = re * sin
            else:
                mid[c, at, 0:128] = re * cos - im * sin
                mid[c, at, 128:256] = re * sin + im * cos
        return 0

    lax.fori_loop(0, 4, rows, 0)
    for pair in range(2):
        part = spread(mid[8 * pair : 8 * pair + 8].reshape(256, 256), RIGHT[3], 1)
        res = mm(w[...], part, NT)
        for k in range(2):
            for ri in range(2):
                out[:, 16 + ri * 4 + 2 * pair + k, 0, :] = res[128 * ri : 128 * ri + 128, 128 * k : 128 * k + 128]
    part = spread(mid[16:20].reshape(128, 256), RIGHT[3], 1)
    res = mm(w[...], part, NT)
    out[:, 24, 0, :] = beside(res[0:128], res[128:256]) + tags[:, 0, :]


def low_lanes():
    return lax.broadcasted_iota(jnp.int32, (128, 128), 1) < 32


def beside(a, b):
    lane = lax.broadcasted_iota(jnp.int32, (128, 128), 1)
    return jnp.where(lane < 32, a, jnp.where(lane < 64, pltpu.roll(b, 32, 1), 0.0))


def column_pairs(field, pair):
    chunk = []
    for k in range(2):
        j = 2 * pair + k
        re, im = field[:, 16 + j % 4, 0, :], field[:, 20 + j % 4, 0, :]
        if j >= 4:
            im = -im
        if j == 4:
            own = field[:, 24, 0, :]
            re, im = jnp.where(low_lanes(), own, re), jnp.where(low_lanes(), pltpu.roll(own, 96, 1), im)
        chunk.append((re, im))
    return jnp.concatenate(
        [jnp.concatenate([chunk[k][ri] for k in range(2)], axis=1) for ri in range(2)], axis=0
    )


def chunks(ref, pair):
    return jnp.concatenate(
        [jnp.concatenate([ref[:, ri * 8 + 2 * pair + k, :] for k in range(2)], axis=1) for ri in range(2)],
        axis=0,
    )


def twist(re, im, tw):
    return re * tw[0] - im * tw[1], re * tw[1] + im * tw[0]


def halves(a, at):
    return [a[at : at + 128, 128 * k : 128 * k + 128] for k in range(2)]


def stacked(rows):
    return jnp.concatenate([jnp.concatenate(r, axis=1) for r in rows], axis=0)


def sky_kernel(field, w, tw, r, out):
    for pair in range(4):
        a = mm(w[...], spread(column_pairs(field, pair), RIGHT[3], 0))
        turn = stacked([twist(re, im, tw) for re, im in zip(halves(a, 0), halves(a, 128))])
        out[pair] = jnp.exp(mm(spread(turn, LEFT[3], 1), r[...]))


def image_kernel(sky, uv, w, tw_f, r_y, w_b, tw_b, r_b, out):
    done = []
    for pair in range(4):
        a = mm(w_b[...], spread(chunks(uv, pair), RIGHT[3], 0))
        parts = [[], []]
        for h in range(2):
            for k, (re, im) in enumerate(zip(halves(a, 256 * h), halves(a, 256 * h + 128))):
                parts[k] += twist(re, im, tw_b[h])
        back = mm(spread(stacked(parts), LEFT[3], 1), r_b[...])
        a = mm(spread(sky[pair] * back, LEFT[3], 1), r_y[...])
        turn = [twist(a[128 * k : 128 * k + 128, 0:128], a[128 * k : 128 * k + 128, 128:256], tw_f) for k in range(2)]
        turn = jnp.concatenate([jnp.concatenate([turn[k][ri] for k in range(2)], axis=1) for ri in range(2)], axis=0)
        done.append(mm(w[...], spread(turn, RIGHT[3], 0)))
    for j in range(4):
        at = slice(128 * (j % 2), 128 * (j % 2) + 128)
        straight, mirrored = done[j // 2][:, at], done[2 + j // 2][:, at]
        re, im = mirrored[0:128], mirrored[128:256]
        if j == 0:
            out[:, 8, 0, :] = beside(re, im)
            re, im = jnp.where(low_lanes(), 0.0, re), jnp.where(low_lanes(), 0.0, im)
        out[:, j, 0, :] = straight[0:128] + im
        out[:, 4 + j, 0, :] = straight[128:256] + re


def last_kernel(folded, amplitude, tw, w, out, mid):
    def residue(c, v):
        cos, sin = tw[0, c : c + 1, :], tw[1, c : c + 1, :]
        re, im = v[:, 0:128], v[:, 128:256]
        mid[c, :, 0:128] = re * cos - im * sin
        mid[c, :, 128:256] = re * sin + im * cos

    for j in range(4):
        z = jnp.concatenate([folded[:, j, 0, :], folded[:, 4 + j, 0, :]], axis=0)
        v = mm(spread(z, LEFT[3], 0), w[...], TN)
        for k in range(4):
            residue(4 * j + k, v[32 * k : 32 * k + 32])
    own = folded[:, 8, 0, :]
    z = jnp.concatenate([own, pltpu.roll(own, 96, 1)], axis=0)
    residue(16, mm(spread(z, LEFT[3], 0), w[...], TN)[0:32])

    def rows(i, _):
        at = pl.ds(pl.multiple_of(i * 8, 8), 8)
        first = [(mid[c, at, 0:128], mid[c, at, 128:256]) for c in range(17)] + [None] * 15
        for b, (re, im) in enumerate(fft_list(first)):
            to = slice(128 * b, 128 * b + 128)
            out[at, to] = amplitude[at, to] * (re + im) * (1.0 / IMG)
        return 0

    lax.fori_loop(0, 4, rows, 0)


def per_device(residual, position, owner, tile_local, xi, amplitude):
    n_base = lax.axis_size("base")
    n_slab = lax.axis_size("slab")
    devices = n_base * n_slab
    everywhere = ("base", "slab")
    t = {k: jnp.asarray(v) for k, v in tables(n_base, n_slab).items()}

    def exchange(a, axis):
        return lax.all_to_all(a, axis, split_axis=0, concat_axis=0, tiled=True)

    rows, width = xi.shape
    blocks = residual.shape[0]
    me = lax.axis_index("base").astype(jnp.int32).reshape(1)
    packed = call(
        first_kernel,
        (devices, 25, 1, 128),
        [SM, SM] + [VM] * 6,
        [SM((devices,), jnp.int32), VM((20, 32, 256), f32), VM((devices, 1, 128), f32)],
        2e9,
        [
            (0, SM((blocks,), jnp.int32)),
            (1, SM((blocks,), jnp.int32)),
            (2, VM(residual.shape, f32)),
            (3, VM(position.shape, f32)),
            (4, VM((rows, width), f32)),
            (5, VM((rows, width), f32)),
            (6, VM((2, 32, 128), f32)),
            (7, VM((256, 768), bf16)),
        ],
    )(owner[:, 0], tile_local, residual, position, xi, amplitude, t["tw_row"], t["w128"])
    data = exchange(packed, everywhere)
    tags = data[:, 24, 0, 64:68].reshape(4 * devices).astype(jnp.int32)
    spare = [VM((4, TILE, TILE), f32), SM((4 * devices + REST,), jnp.int32)]
    shape = (2, 8, 32, 128)
    whole = call(
        functools.partial(grid_whole_kernel, 0), (n_base, *shape), [SM, VM], spare, 2e10
    )(tags, data)
    whole, tags = lax.optimization_barrier((whole, tags))
    whole = exchange(whole, "base")
    parts = call(
        functools.partial(grid_parts_kernel, 8),
        [shape] * n_base,
        [SM, SM, VM],
        [*spare, VM((n_base, *shape), f32)],
        2e10,
    )(me, tags, data)
    parts, field = lax.optimization_barrier((parts, data))
    parts = [parts[0]] + [
        lax.ppermute(parts[k], "base", [(i, (i + k) % n_base) for i in range(n_base)]) for k in range(1, n_base)
    ]
    sky = call(
        sky_kernel,
        (4, 256, 128),
        [VM] * 4,
        (),
        4e9,
        [(1, VM((256, 768), bf16)), (2, VM((2, 128, 128), f32)), (3, VM((768, 128), bf16))],
        True,
    )(field, t["w128"], t["tw_f"], t["r_f"])
    parts[0], sky = lax.optimization_barrier((parts[0], sky))
    cols = call(
        cols_kernel,
        (devices // 2, 2, 16, 128),
        [SM] + [VM] * 8,
        [VM((64, 32, 256), f32)],
        4e9,
        [
            (1, VM((n_base, *shape), f32)),
            (6, VM((n_base, 2, 64, 128), f32)),
            (7, VM((128, 1536), bf16)),
            (8, VM((128, 1536), bf16)),
        ],
    )(me, whole, *parts, t["tw_cols"], t["w_cols"], t["w_back"])
    cols = exchange(cols.reshape(devices, 16, 128), everywhere)
    fold = call(
        image_kernel,
        (devices, 9, 1, 128),
        [VM] * 8,
        (),
        8e9,
        [
            (0, VM((4, 256, 128), f32)),
            (5, VM((512, 768), bf16)),
            (7, VM((1536, 128), bf16)),
        ],
    )(sky, cols, t["w128"], t["tw_f"], t["r_y"], t["w_b"], t["tw_b"], t["r_b"])
    fold = exchange(fold, everywhere)
    return call(last_kernel, (32, IMG), [VM] * 4, [VM((32, 32, 256), f32)], 3e9)(
        fold, amplitude, t["tw_row"], t["w128t"]
    )


def solution(mesh):
    placed = (
        P(("base", "slab"), None, None),
        P(("base", "slab"), None, None),
        P(("base", "slab"), None),
        P(("base", "slab")),
        P(("base", "slab"), None),
        P(("base", "slab"), None),
    )
    return jax.shard_map(
        per_device, mesh=mesh, in_specs=placed, out_specs=P(("base", "slab"), None), check_vma=False
    )
```

```python
import functools
import math

import jax
import jax.numpy as jnp
import ml_dtypes
import numpy as np
from jax import lax
from jax.experimental import pallas as pl
from jax.experimental.pallas import tpu as pltpu
from jax.sharding import PartitionSpec as P

G = 8192
IMG = 4096
TILE = 128
GROUP = 24
REST = 8
GRANT = 20 * 2**20

NN = (((1,), (0,)), ((), ()))
NT = (((1,), (1,)), ((), ()))
TN = (((0,), (0,)), ((), ()))
f32 = jnp.float32
bf16 = jnp.bfloat16


LEFT = {6: (0, 0, 1, 1, 0, 2), 3: (0, 0, 1)}
RIGHT = {6: (0, 1, 0, 1, 2, 0), 3: (0, 1, 0)}


def pieces(x, count=3):
    out, rest = [], x
    for k in range(count):
        out.append(rest.astype(bf16))
        if k + 1 < count:
            rest = rest - out[-1].astype(f32)
    return out


def spread(x, order, axis):
    cut = pieces(x, max(order) + 1)
    return jnp.concatenate([cut[k] for k in order], axis=axis)


def mm(a, b, dims=NN):
    return lax.dot_general(a, b, dims, preferred_element_type=f32)


def spread_table(x, order, axis):
    cut, rest = [], x.astype(np.float64)
    for _ in range(max(order) + 1):
        cut.append(rest.astype(np.float32).astype(ml_dtypes.bfloat16))
        rest = rest - cut[-1].astype(np.float64)
    return np.concatenate([cut[k] for k in order], axis=axis)


def wave(rows, cols, modulus):
    turn = np.outer(rows, cols).astype(np.int64) % modulus
    angle = turn * (2.0 * np.pi / modulus)
    return np.cos(angle), np.sin(angle)


def turned(c, s):
    return np.block([[c, -s], [s, c]])


@functools.lru_cache(None)
def tables(n_base, n_slab):
    n = np.arange
    devices = n_base * n_slab
    out = {}
    c, s = wave(n(128), n(128), 128)
    out["w128"] = spread_table(turned(c, s), LEFT[3], 1)
    out["w128t"] = spread_table(turned(c, s).T, RIGHT[3], 0)
    out["tw_row"] = np.stack(wave(n(32), n(128), IMG))
    c, s = wave(n(64) + 32, n(128), 128)
    out["w_cols"] = spread_table(turned(c, s), LEFT[6], 1)
    out["w_back"] = spread_table(turned(c[::-1], s[::-1]), LEFT[6], 1)
    out["tw_cols"] = np.stack([np.stack(wave(n(64), n(128) + G // n_base * me, G)) for me in range(n_base)])
    eye = np.eye(4)
    c, s = wave(n(128), n(32), IMG)
    out["tw_f"] = np.stack([np.tile(c, (1, 4)), np.tile(s, (1, 4))])
    c, s = wave(n(32), n(32), 32)
    out["r_f"] = spread_table(np.concatenate([np.kron(eye, c + s), np.kron(eye, c - s)]) / IMG, RIGHT[3], 0)
    out["r_y"] = spread_table(np.concatenate([np.kron(eye, c), np.kron(eye, s)], axis=1), RIGHT[3], 0)
    src = n(devices)
    place = (src % n_slab) * n_base + src // n_slab
    wb, twb, rb = [], [], []
    for half in range(2):
        c, s = wave(n(128) + 128 * half, place, 256)
        wb.append(turned(c, s))
        c, s = wave(n(128) + 128 * half, n(32), G)
        twb.append(np.stack([np.tile(c, (1, 4)), np.tile(s, (1, 4))]))
        c, s = wave(n(32), n(32) // 2 + 8, 32)
        keep = (n(32) % 2 == half)[None, :]
        rb += [np.kron(eye, c * keep) / G, np.kron(eye, -s * keep) / G]
    out["w_b"] = spread_table(np.concatenate(wb), LEFT[3], 1)
    out["tw_b"] = np.stack(twb)
    out["r_b"] = spread_table(np.concatenate(rb), RIGHT[3], 0)
    return {k: v if v.dtype == ml_dtypes.bfloat16 else v.astype(np.float32) for k, v in out.items()}


def times(z, k, n):
    re, im = z
    k %= n
    if k == 0:
        return z
    if 4 * k == n:
        return -im, re
    c, s = math.cos(2 * math.pi * k / n), math.sin(2 * math.pi * k / n)
    if 8 * k == n:
        return (re - im) * c, (re + im) * c
    if 8 * k == 3 * n:
        return (re + im) * -s, (re - im) * s
    return re * c - im * s, re * s + im * c


def fft_list(xs):
    n = len(xs)
    if n == 1:
        return xs
    even, odd = fft_list(xs[0::2]), fft_list(xs[1::2])
    low, high = [], []
    for k in range(n // 2):
        if odd[k] is None:
            low.append(even[k])
            high.append(even[k])
            continue
        (a, b), (c, d) = even[k], times(odd[k], k, n)
        low.append((a + c, b + d))
        high.append((a - c, b - d))
    return low + high


def rfft_list(xs):
    n = len(xs)
    if n == 2:
        return [(xs[0] + xs[1], None), (xs[0] - xs[1], None)]
    even, odd = rfft_list(xs[0::2]), rfft_list(xs[1::2])
    out = [None] * (n // 2 + 1)
    out[0] = (even[0][0] + odd[0][0], None)
    out[n // 2] = (even[0][0] - odd[0][0], None)
    out[n // 4] = (even[n // 4][0], odd[n // 4][0])
    for k in range(1, n // 4):
        (a, b), (c, d) = even[k], times(odd[k], k, n)
        out[k] = (a + c, b + d)
        out[n // 2 - k] = (a - c, d - b)
    return out


class Late:
    def __init__(self, ref, copy):
        self.ref, self.copy, self.shape = ref, copy, ref.shape

    def ready(self):
        if self.copy is not None:
            self.copy.wait()
            self.copy = None
        return self.ref

    def __getitem__(self, at):
        return self.ready()[at]


def call(body, out_shapes, in_specs, scratch=(), flops=0, far=(), far_out=False):
    outs = [out_shapes] if isinstance(out_shapes[0], int) else list(out_shapes)
    count, own, made = len(in_specs), len(scratch), len(outs)
    specs = [pl.BlockSpec(memory_space=m) for m in in_specs]
    for i, _ in far:
        specs[i] = pl.BlockSpec(memory_space=pltpu.HBM)

    def kernel(*refs):
        ins, results = list(refs[:count]), list(refs[count : count + made])
        rest = refs[count + made : count + made + own]
        spare = refs[count + made + own :]
        copies = []
        for k, (i, _) in enumerate(far):
            copies.append(pltpu.make_async_copy(ins[i], spare[k], spare[-1].at[k]))
            copies[-1].start()
            ins[i] = Late(spare[k], copies[-1])
        if not far_out:
            body(*ins, *results, *rest)
            return
        body(*ins, spare[len(far)], *rest)
        last = pltpu.make_async_copy(spare[len(far)], results[0], spare[-1].at[len(far)])
        last.start()
        last.wait()

    more = [shape for _, shape in far] + ([VM(outs[0], f32)] if far_out else [])
    if more:
        more.append(pltpu.SemaphoreType.DMA((len(more),)))
    made_in = pltpu.HBM if far_out else pltpu.VMEM
    got = pl.pallas_call(
        kernel,
        out_shape=[(pltpu.HBM if far_out else jax.ShapeDtypeStruct)(shape, f32) for shape in outs],
        in_specs=specs,
        out_specs=[pl.BlockSpec(memory_space=made_in)] * made,
        scratch_shapes=list(scratch) + more,
        compiler_params=pltpu.CompilerParams(vmem_limit_bytes=GRANT),
        cost_estimate=pl.CostEstimate(
            flops=int(flops), bytes_accessed=8 * sum(map(math.prod, outs)), transcendentals=0
        ),
    )

    def placed(*arrays):
        arrays = list(arrays)
        for i, _ in far:
            arrays[i] = pltpu.with_memory_space_constraint(arrays[i], pltpu.HBM)
        results = got(*arrays)
        return results[0] if isinstance(out_shapes[0], int) else results

    return placed


VM = pltpu.VMEM
SM = pltpu.SMEM


def first_kernel(owner, tile, residual, position, xi, amplitude, tw, w, out, count, mid, tags):
    n_base, n_slab = 4, 32

    def clear(i, _):
        count[i] = 0
        return 0

    lax.fori_loop(0, count.shape[0], clear, 0, unroll=8)
    owner, tile, residual, position = (a.ready() for a in (owner, tile, residual, position))
    lane = lax.broadcasted_iota(jnp.int32, (1, 128), 1)
    tags[...] = jnp.zeros_like(tags)

    def step(i, _):
        placed = []
        for u in range(8):
            at = i * 8 + u
            o, t = owner[at], tile[at]
            row = (o & (n_slab - 1)) * 2 + (t >> 4)
            group, col = o >> 5, t & 15
            flip = (row >= n_slab).astype(jnp.int32)
            row = jnp.where(flip == 1, 2 * n_slab - 1 - row, row)
            group = jnp.where(flip == 1, n_base - 1 - group, group)
            col = jnp.where(flip == 1, 15 - col, col)
            k = count[o]
            count[o] = k + 1
            to = group * n_slab + (row & ~1) + flip
            placed.append((at, to, k & 1, ((row & 1) * 16 + col + 1).astype(f32)))
        parts = [(residual[at], position[at]) for at, _, _, _ in placed]
        for (at, to, slot, tag), (value, place) in zip(placed, parts):
            for part in range(2):
                out[to, slot * 4 + part] = value[part : part + 1]
                out[to, slot * 4 + 2 + part] = place[part : part + 1]
            tags[to] = jnp.where(lane == 64 + slot, tag, tags[to])
        return 0

    lax.fori_loop(0, owner.shape[0] // 8, step, 0)
    row_transform(*(a.ready() for a in (xi, amplitude, tw, w)), out, mid, tags)


def taps(d):
    x = jnp.maximum(1.0 - d * d, 0.0)
    return x * x * x


def grid_whole_kernel(first, me, own, others, data, mate, total, cells, order):
    grid_into(first, 0, me[1], own, others, data, mate, total, cells, order)


def grid_parts_kernel(first, me, own, others, data, mate, out0, out1, out2, out3, cells, order, total):
    grid_into(first, me[0], me[1], own, others, data, mate, total, cells, order)
    for k, out in enumerate((out0, out1, out2, out3)):
        out[...] = total[k]


def grid_into(first, me, core, own, others, data, mate, total, cells, order):
    first = first + 16 * core
    slots, wide = own.shape[0], total.shape[2]
    for axis in range(2):
        at = lax.broadcasted_iota(jnp.int32, (TILE, TILE), axis).astype(f32)
        cells[2 * axis] = at * 0.25
        cells[2 * axis + 1] = (float(TILE) - at) * 0.25
    total[...] = jnp.zeros_like(total)

    def scan(tags, begin):
        def step(s, n):
            order[n] = begin + s
            tag = tags[s] - first
            return n + ((tag > 0) & (tag <= wide)).astype(jnp.int32)

        return step

    n = lax.fori_loop(0, slots, scan(own, 0), jnp.int32(0), unroll=8)
    n = lax.fori_loop(0, slots, scan(others, slots), n, unroll=8)
    for extra in range(REST):
        order[n + extra] = order[jnp.maximum(n - 1, 0)]

    def down(row):
        return jnp.transpose(jnp.broadcast_to(row, (TILE, TILE)))

    def add(at):
        s = order[at]
        used = (at < n).astype(f32)
        far = (s >= slots).astype(jnp.int32)
        s = s - far * slots
        src, slot = s >> 1, s & 1
        flip = (core + far) & 1
        t = jnp.clip(jnp.where(far == 1, others[s], own[s]) - first - 1, 0, wide - 1)
        value_re, value_im, row, col = (
            jnp.where(far == 1, mate[src, slot * 4 + i], data[src, slot * 4 + i]) for i in range(4)
        )
        value_re = value_re * used
        value_im = value_im * (used * (1.0 - 2.0 * flip.astype(f32)))
        rows = taps(cells[flip] - row * 0.25)
        cols = taps(cells[2 + flip] - down(col * 0.25))
        weighted = jnp.concatenate([cols * down(value_re), cols * down(value_im)], axis=1)
        sub = mm(spread(rows, LEFT[6], 1), spread(weighted, RIGHT[6], 0))
        for q in range(4):
            for ri in range(2):
                total[(q - me) & 3, ri, t] += sub[32 * q : 32 * q + 32, 128 * ri : 128 * ri + 128]

    def turn(start, count):
        def body(g, _):
            for u in range(count):
                add(start + g * count + u)
            return 0

        return body

    whole = n // GROUP
    lax.fori_loop(0, whole, turn(0, GROUP), 0)
    begun = whole * GROUP
    lax.fori_loop(0, (n - begun + REST - 1) // REST, turn(begun, REST), 0)


def cols_kernel(*refs):
    me, whole, parts, (tw, w, w_back, out, mid) = refs[0], refs[1], refs[2:6], refs[6:]
    tw = tw.ready()

    def tile(b, ri, at):
        group = b // 16
        if b % 16 < 8:
            return whole[(me[0] + group) & 3, ri, b % 8, at, :]
        return parts[-group % 4][ri, b % 8, at, :]

    def rows(i, _):
        at = pl.ds(pl.multiple_of(i * 8, 8), 8)
        first = [(tile(b, 0, at), tile(b, 1, at)) for b in range(64)]
        for c, (re, im) in enumerate(fft_list(first)):
            cos, sin = tw[me[0], 0, c : c + 1, :], tw[me[0], 1, c : c + 1, :]
            half, c = c // 32, c % 32
            to = 32 * half + c if c <= 16 else 32 * (1 - half) + 48 - c
            mid[to, at, 0:128] = re * cos - im * sin
            mid[to, at, 128:256] = re * sin + im * cos
        return 0

    lax.fori_loop(0, 4, rows, 0)
    for pair in range(8):
        part = spread(mid[8 * pair : 8 * pair + 8].reshape(256, 256), RIGHT[6], 1)
        res = mm((w if pair % 4 < 2 else w_back)[...], part, NT)
        if pair % 4 == 2:
            own = mm(w[...], part[0:128], NT)
            own = jnp.concatenate([jnp.where(low_lanes(), own, res[:, 0:128]), res[:, 128:256]], axis=1)
            res = own
        for k in range(2):
            chunk = 2 * pair + k
            for ri in range(2):
                out[:, chunk // 8, ri * 8 + chunk % 8, :] = res[64 * ri : 64 * ri + 64, 128 * k : 128 * k + 128]


def row_transform(xi, amplitude, tw, w, out, mid, tags):
    def rows(i, _):
        at = pl.ds(pl.multiple_of(i * 8, 8), 8)
        first = [
            xi[at, 128 * b : 128 * b + 128] * amplitude[at, 128 * b : 128 * b + 128] for b in range(32)
        ]
        for c, (re, im) in enumerate(rfft_list(first)):
            cos, sin = tw[0, c : c + 1, :], tw[1, c : c + 1, :]
            if im is None:
                mid[c, at, 0:128] = re * cos
                mid[c, at, 128:256] = re * sin
            else:
                mid[c, at, 0:128] = re * cos - im * sin
                mid[c, at, 128:256] = re * sin + im * cos
        return 0

    lax.fori_loop(0, 4, rows, 0)
    for pair in range(2):
        part = spread(mid[8 * pair : 8 * pair + 8].reshape(256, 256), RIGHT[3], 1)
        res = mm(w[...], part, NT)
        for k in range(2):
            for ri in range(2):
                out[:, 8 + ri * 4 + 2 * pair + k, 0, :] = res[128 * ri : 128 * ri + 128, 128 * k : 128 * k + 128]
    part = spread(mid[16:20].reshape(128, 256), RIGHT[3], 1)
    res = mm(w[...], part, NT)
    out[:, 16, 0, :] = beside(res[0:128], res[128:256]) + tags[:, 0, :]


def low_lanes():
    return lax.broadcasted_iota(jnp.int32, (128, 128), 1) < 32


def beside(a, b):
    lane = lax.broadcasted_iota(jnp.int32, (128, 128), 1)
    return jnp.where(lane < 32, a, jnp.where(lane < 64, pltpu.roll(b, 32, 1), 0.0))


def column_pairs(field, pair):
    chunk = []
    for k in range(2):
        j = 2 * pair + k
        re, im = field[:, 8 + j % 4, 0, :], field[:, 12 + j % 4, 0, :]
        if j >= 4:
            im = -im
        if j == 4:
            own = field[:, 16, 0, :]
            re, im = jnp.where(low_lanes(), own, re), jnp.where(low_lanes(), pltpu.roll(own, 96, 1), im)
        chunk.append((re, im))
    return jnp.concatenate(
        [jnp.concatenate([chunk[k][ri] for k in range(2)], axis=1) for ri in range(2)], axis=0
    )


def chunks(ref, pair):
    return jnp.concatenate(
        [jnp.concatenate([ref[:, ri * 8 + 2 * pair + k, :] for k in range(2)], axis=1) for ri in range(2)],
        axis=0,
    )


def twist(re, im, tw):
    return re * tw[0] - im * tw[1], re * tw[1] + im * tw[0]


def halves(a, at):
    return [a[at : at + 128, 128 * k : 128 * k + 128] for k in range(2)]


def stacked(rows):
    return jnp.concatenate([jnp.concatenate(r, axis=1) for r in rows], axis=0)


def sky_kernel(field, w, tw, r, out):
    for pair in range(4):
        a = mm(w[...], spread(column_pairs(field, pair), RIGHT[3], 0))
        turn = stacked([twist(re, im, tw) for re, im in zip(halves(a, 0), halves(a, 128))])
        out[pair] = jnp.exp(mm(spread(turn, LEFT[3], 1), r[...]))


def image_kernel(sky, uv, w, tw_f, r_y, w_b, tw_b, r_b, out):
    done = []
    for pair in range(4):
        a = mm(w_b[...], spread(chunks(uv, pair), RIGHT[3], 0))
        parts = [[], []]
        for h in range(2):
            for k, (re, im) in enumerate(zip(halves(a, 256 * h), halves(a, 256 * h + 128))):
                parts[k] += twist(re, im, tw_b[h])
        back = mm(spread(stacked(parts), LEFT[3], 1), r_b[...])
        a = mm(spread(sky[pair] * back, LEFT[3], 1), r_y[...])
        turn = [twist(a[128 * k : 128 * k + 128, 0:128], a[128 * k : 128 * k + 128, 128:256], tw_f) for k in range(2)]
        turn = jnp.concatenate([jnp.concatenate([turn[k][ri] for k in range(2)], axis=1) for ri in range(2)], axis=0)
        done.append(mm(w[...], spread(turn, RIGHT[3], 0)))
    for j in range(4):
        at = slice(128 * (j % 2), 128 * (j % 2) + 128)
        straight, mirrored = done[j // 2][:, at], done[2 + j // 2][:, at]
        re, im = mirrored[0:128], mirrored[128:256]
        if j == 0:
            out[:, 8, 0, :] = beside(re, im)
            re, im = jnp.where(low_lanes(), 0.0, re), jnp.where(low_lanes(), 0.0, im)
        out[:, j, 0, :] = straight[0:128] + im
        out[:, 4 + j, 0, :] = straight[128:256] + re


def last_kernel(folded, amplitude, tw, w, out, mid):
    def residue(c, v):
        cos, sin = tw[0, c : c + 1, :], tw[1, c : c + 1, :]
        re, im = v[:, 0:128], v[:, 128:256]
        mid[c, :, 0:128] = re * cos - im * sin
        mid[c, :, 128:256] = re * sin + im * cos

    for j in range(4):
        z = jnp.concatenate([folded[:, j, 0, :], folded[:, 4 + j, 0, :]], axis=0)
        v = mm(spread(z, LEFT[3], 0), w[...], TN)
        for k in range(4):
            residue(4 * j + k, v[32 * k : 32 * k + 32])
    own = folded[:, 8, 0, :]
    z = jnp.concatenate([own, pltpu.roll(own, 96, 1)], axis=0)
    residue(16, mm(spread(z, LEFT[3], 0), w[...], TN)[0:32])

    def rows(i, _):
        at = pl.ds(pl.multiple_of(i * 8, 8), 8)
        first = [(mid[c, at, 0:128], mid[c, at, 128:256]) for c in range(17)] + [None] * 15
        for b, (re, im) in enumerate(fft_list(first)):
            to = slice(128 * b, 128 * b + 128)
            out[at, to] = amplitude[at, to] * (re + im) * (1.0 / IMG)
        return 0

    lax.fori_loop(0, 4, rows, 0)


def per_device(residual, position, owner, tile_local, xi, amplitude):
    n_base = lax.axis_size("base")
    n_slab = lax.axis_size("slab")
    devices = n_base * n_slab
    everywhere = ("base", "slab")
    t = {k: jnp.asarray(v) for k, v in tables(n_base, n_slab).items()}

    def exchange(a, axis):
        return lax.all_to_all(a, axis, split_axis=0, concat_axis=0, tiled=True)

    rows, width = xi.shape
    blocks = residual.shape[0]
    me = jnp.stack([lax.axis_index("base"), lax.axis_index("slab") & 1]).astype(jnp.int32)
    packed = call(
        first_kernel,
        (devices, 17, 1, 128),
        [SM, SM] + [VM] * 6,
        [SM((devices,), jnp.int32), VM((20, 32, 256), f32), VM((devices, 1, 128), f32)],
        2e9,
        [
            (0, SM((blocks,), jnp.int32)),
            (1, SM((blocks,), jnp.int32)),
            (2, VM(residual.shape, f32)),
            (3, VM(position.shape, f32)),
            (4, VM((rows, width), f32)),
            (5, VM((rows, width), f32)),
            (6, VM((2, 32, 128), f32)),
            (7, VM((256, 768), bf16)),
        ],
    )(owner[:, 0], tile_local, residual, position, xi, amplitude, t["tw_row"], t["w128"])
    data = exchange(packed, everywhere)
    mate = lax.ppermute(data, "slab", [(i, i ^ 1) for i in range(n_slab)])
    tags = tuple(a[:, 16, 0, 64:66].reshape(2 * devices).astype(jnp.int32) for a in (data, mate))
    spare = [VM((4, TILE, TILE), f32), SM((4 * devices + REST,), jnp.int32)]
    shape = (2, 8, 32, 128)
    whole = call(
        functools.partial(grid_whole_kernel, 0), (n_base, *shape), [SM, SM, SM, VM, VM], spare, 2e10
    )(me, *tags, data, mate)
    whole, tags = lax.optimization_barrier((whole, tags))
    whole = exchange(whole, "base")
    parts = call(
        functools.partial(grid_parts_kernel, 8),
        [shape] * n_base,
        [SM, SM, SM, VM, VM],
        [*spare, VM((n_base, *shape), f32)],
        2e10,
    )(me, *tags, data, mate)
    parts, field = lax.optimization_barrier((parts, data))
    parts = [parts[0]] + [
        lax.ppermute(parts[k], "base", [(i, (i + k) % n_base) for i in range(n_base)]) for k in range(1, n_base)
    ]
    sky = call(
        sky_kernel,
        (4, 256, 128),
        [VM] * 4,
        (),
        4e9,
        [(1, VM((256, 768), bf16)), (2, VM((2, 128, 128), f32)), (3, VM((768, 128), bf16))],
        True,
    )(field, t["w128"], t["tw_f"], t["r_f"])
    parts[0], sky = lax.optimization_barrier((parts[0], sky))
    cols = call(
        cols_kernel,
        (devices // 2, 2, 16, 128),
        [SM] + [VM] * 8,
        [VM((64, 32, 256), f32)],
        4e9,
        [
            (6, VM((n_base, 2, 64, 128), f32)),
            (7, VM((128, 1536), bf16)),
            (8, VM((128, 1536), bf16)),
        ],
    )(me, whole, *parts, t["tw_cols"], t["w_cols"], t["w_back"])
    cols = exchange(cols.reshape(devices, 16, 128), everywhere)
    fold = call(
        image_kernel,
        (devices, 9, 1, 128),
        [VM] * 8,
        (),
        8e9,
        [
            (0, VM((4, 256, 128), f32)),
            (5, VM((512, 768), bf16)),
            (7, VM((1536, 128), bf16)),
        ],
    )(sky, cols, t["w128"], t["tw_f"], t["r_y"], t["w_b"], t["tw_b"], t["r_b"])
    fold = exchange(fold, everywhere)
    return call(last_kernel, (32, IMG), [VM] * 4, [VM((32, 32, 256), f32)], 3e9)(
        fold, amplitude, t["tw_row"], t["w128t"]
    )


def solution(mesh):
    placed = (
        P(("base", "slab"), None, None),
        P(("base", "slab"), None, None),
        P(("base", "slab"), None),
        P(("base", "slab")),
        P(("base", "slab"), None),
        P(("base", "slab"), None),
    )
    return jax.shard_map(
        per_device, mesh=mesh, in_specs=placed, out_specs=P(("base", "slab"), None), check_vma=False
    )
```

```python
import functools
import math

import jax
import jax.numpy as jnp
import ml_dtypes
import numpy as np
from jax import lax
from jax.experimental import pallas as pl
from jax.experimental.pallas import tpu as pltpu
from jax.sharding import PartitionSpec as P

G = 8192
IMG = 4096
TILE = 128
GROUP = 24
REST = 8
CUT = 10
GRANT = 20 * 2**20

NN = (((1,), (0,)), ((), ()))
NT = (((1,), (1,)), ((), ()))
TN = (((0,), (0,)), ((), ()))
f32 = jnp.float32
bf16 = jnp.bfloat16


LEFT = {6: (0, 0, 1, 1, 0, 2), 3: (0, 0, 1)}
RIGHT = {6: (0, 1, 0, 1, 2, 0), 3: (0, 1, 0)}


def pieces(x, count=3):
    out, rest = [], x
    for k in range(count):
        out.append(rest.astype(bf16))
        if k + 1 < count:
            rest = rest - out[-1].astype(f32)
    return out


def spread(x, order, axis):
    cut = pieces(x, max(order) + 1)
    return jnp.concatenate([cut[k] for k in order], axis=axis)


def mm(a, b, dims=NN):
    return lax.dot_general(a, b, dims, preferred_element_type=f32)


def spread_table(x, order, axis):
    cut, rest = [], x.astype(np.float64)
    for _ in range(max(order) + 1):
        cut.append(rest.astype(np.float32).astype(ml_dtypes.bfloat16))
        rest = rest - cut[-1].astype(np.float64)
    return np.concatenate([cut[k] for k in order], axis=axis)


def wave(rows, cols, modulus):
    turn = np.outer(rows, cols).astype(np.int64) % modulus
    angle = turn * (2.0 * np.pi / modulus)
    return np.cos(angle), np.sin(angle)


def turned(c, s):
    return np.block([[c, -s], [s, c]])


@functools.lru_cache(None)
def tables(n_base, n_slab):
    n = np.arange
    devices = n_base * n_slab
    out = {}
    c, s = wave(n(128), n(128), 128)
    out["w128"] = spread_table(turned(c, s), LEFT[3], 1)
    out["w128t"] = spread_table(turned(c, s).T, RIGHT[3], 0)
    out["tw_row"] = np.stack(wave(n(32), n(128), IMG))
    c, s = wave(n(64) + 32, n(128), 128)
    out["w_cols"] = spread_table(turned(c, s), LEFT[6], 1)
    out["w_back"] = spread_table(turned(c[::-1], s[::-1]), LEFT[6], 1)
    out["tw_cols"] = np.stack([np.stack(wave(n(64), n(128) + G // n_base * me, G)) for me in range(n_base)])
    eye = np.eye(4)
    c, s = wave(n(128), n(32), IMG)
    out["tw_f"] = np.stack([np.tile(c, (1, 4)), np.tile(s, (1, 4))])
    c, s = wave(n(32), n(32), 32)
    out["r_f"] = spread_table(np.concatenate([np.kron(eye, c + s), np.kron(eye, c - s)]) / IMG, RIGHT[3], 0)
    out["r_y"] = spread_table(np.concatenate([np.kron(eye, c), np.kron(eye, s)], axis=1), RIGHT[3], 0)
    src = n(devices)
    place = (src % n_slab) * n_base + src // n_slab
    wb, twb, rb = [], [], []
    for half in range(2):
        c, s = wave(n(128) + 128 * half, place, 256)
        wb.append(turned(c, s))
        c, s = wave(n(128) + 128 * half, n(32), G)
        twb.append(np.stack([np.tile(c, (1, 4)), np.tile(s, (1, 4))]))
        c, s = wave(n(32), n(32) // 2 + 8, 32)
        keep = (n(32) % 2 == half)[None, :]
        rb += [np.kron(eye, c * keep) / G, np.kron(eye, -s * keep) / G]
    out["w_b"] = spread_table(np.concatenate(wb), LEFT[3], 1)
    out["tw_b"] = np.stack(twb)
    out["r_b"] = spread_table(np.concatenate(rb), RIGHT[3], 0)
    return {k: v if v.dtype == ml_dtypes.bfloat16 else v.astype(np.float32) for k, v in out.items()}


def times(z, k, n):
    re, im = z
    k %= n
    if k == 0:
        return z
    if 4 * k == n:
        return -im, re
    c, s = math.cos(2 * math.pi * k / n), math.sin(2 * math.pi * k / n)
    if 8 * k == n:
        return (re - im) * c, (re + im) * c
    if 8 * k == 3 * n:
        return (re + im) * -s, (re - im) * s
    return re * c - im * s, re * s + im * c


def fft_list(xs):
    n = len(xs)
    if n == 1:
        return xs
    even, odd = fft_list(xs[0::2]), fft_list(xs[1::2])
    low, high = [], []
    for k in range(n // 2):
        if odd[k] is None:
            low.append(even[k])
            high.append(even[k])
            continue
        (a, b), (c, d) = even[k], times(odd[k], k, n)
        low.append((a + c, b + d))
        high.append((a - c, b - d))
    return low + high


def rfft_list(xs):
    n = len(xs)
    if n == 2:
        return [(xs[0] + xs[1], None), (xs[0] - xs[1], None)]
    even, odd = rfft_list(xs[0::2]), rfft_list(xs[1::2])
    out = [None] * (n // 2 + 1)
    out[0] = (even[0][0] + odd[0][0], None)
    out[n // 2] = (even[0][0] - odd[0][0], None)
    out[n // 4] = (even[n // 4][0], odd[n // 4][0])
    for k in range(1, n // 4):
        (a, b), (c, d) = even[k], times(odd[k], k, n)
        out[k] = (a + c, b + d)
        out[n // 2 - k] = (a - c, d - b)
    return out


class Late:
    def __init__(self, ref, copy):
        self.ref, self.copy, self.shape = ref, copy, ref.shape

    def ready(self):
        if self.copy is not None:
            self.copy.wait()
            self.copy = None
        return self.ref

    def __getitem__(self, at):
        return self.ready()[at]


def call(body, out_shapes, in_specs, scratch=(), flops=0, far=(), far_out=False):
    outs = [out_shapes] if isinstance(out_shapes[0], int) else list(out_shapes)
    count, own, made = len(in_specs), len(scratch), len(outs)
    specs = [pl.BlockSpec(memory_space=m) for m in in_specs]
    for i, _ in far:
        specs[i] = pl.BlockSpec(memory_space=pltpu.HBM)

    def kernel(*refs):
        ins, results = list(refs[:count]), list(refs[count : count + made])
        rest = refs[count + made : count + made + own]
        spare = refs[count + made + own :]
        copies = []
        for k, (i, _) in enumerate(far):
            copies.append(pltpu.make_async_copy(ins[i], spare[k], spare[-1].at[k]))
            copies[-1].start()
            ins[i] = Late(spare[k], copies[-1])
        if not far_out:
            body(*ins, *results, *rest)
            return
        body(*ins, spare[len(far)], *rest)
        last = pltpu.make_async_copy(spare[len(far)], results[0], spare[-1].at[len(far)])
        last.start()
        last.wait()

    more = [shape for _, shape in far] + ([VM(outs[0], f32)] if far_out else [])
    if more:
        more.append(pltpu.SemaphoreType.DMA((len(more),)))
    made_in = pltpu.HBM if far_out else pltpu.VMEM
    got = pl.pallas_call(
        kernel,
        out_shape=[(pltpu.HBM if far_out else jax.ShapeDtypeStruct)(shape, f32) for shape in outs],
        in_specs=specs,
        out_specs=[pl.BlockSpec(memory_space=made_in)] * made,
        scratch_shapes=list(scratch) + more,
        compiler_params=pltpu.CompilerParams(vmem_limit_bytes=GRANT),
        cost_estimate=pl.CostEstimate(
            flops=int(flops), bytes_accessed=8 * sum(map(math.prod, outs)), transcendentals=0
        ),
    )

    def placed(*arrays):
        arrays = list(arrays)
        for i, _ in far:
            arrays[i] = pltpu.with_memory_space_constraint(arrays[i], pltpu.HBM)
        results = got(*arrays)
        return results[0] if isinstance(out_shapes[0], int) else results

    return placed


VM = pltpu.VMEM
SM = pltpu.SMEM


def first_kernel(owner, tile, residual, position, xi, amplitude, tw, w, out, count, mid, tags):
    n_base, n_slab = 4, 32

    def clear(i, _):
        count[i] = 0
        return 0

    lax.fori_loop(0, count.shape[0], clear, 0, unroll=8)
    owner, tile, residual, position = (a.ready() for a in (owner, tile, residual, position))
    lane = lax.broadcasted_iota(jnp.int32, (1, 128), 1)
    tags[...] = jnp.zeros_like(tags)

    def step(i, _):
        placed = []
        for u in range(8):
            at = i * 8 + u
            o, t = owner[at], tile[at]
            row = (o & (n_slab - 1)) * 2 + (t >> 4)
            group, col = o >> 5, t & 15
            flip = (row >= n_slab).astype(jnp.int32)
            row = jnp.where(flip == 1, 2 * n_slab - 1 - row, row)
            group = jnp.where(flip == 1, n_base - 1 - group, group)
            col = jnp.where(flip == 1, 15 - col, col)
            k = count[o]
            count[o] = k + 1
            to = group * n_slab + (row & ~1) + flip
            placed.append((at, to, k & 1, ((row & 1) * 16 + col + 1).astype(f32)))
        parts = [(residual[at], position[at]) for at, _, _, _ in placed]
        for (at, to, slot, tag), (value, place) in zip(placed, parts):
            for part in range(2):
                out[to, slot * 4 + part] = value[part : part + 1]
                out[to, slot * 4 + 2 + part] = place[part : part + 1]
            tags[to] = jnp.where(lane == 64 + slot, tag, tags[to])
        return 0

    lax.fori_loop(0, owner.shape[0] // 8, step, 0)
    row_transform(*(a.ready() for a in (xi, amplitude, tw, w)), out, mid, tags)


def taps(d):
    x = jnp.maximum(1.0 - d * d, 0.0)
    return x * x * x


def grid_whole_kernel(first, me, own, others, data, mate, total, cells, order):
    grid_into(first, 0, me[1], own, others, data, mate, total, cells, order)


def grid_parts_kernel(first, me, own, others, data, mate, out0, out1, out2, out3, cells, order, total):
    grid_into(first, me[0], me[1], own, others, data, mate, total, cells, order)
    for k, out in enumerate((out0, out1, out2, out3)):
        out[...] = total[k]


def grid_into(first, me, core, own, others, data, mate, total, cells, order):
    first = first + 16 * core
    slots, wide = own.shape[0], total.shape[2]
    for axis in range(2):
        at = lax.broadcasted_iota(jnp.int32, (TILE, TILE), axis).astype(f32)
        cells[2 * axis] = at * 0.25
        cells[2 * axis + 1] = (float(TILE) - at) * 0.25
    total[...] = jnp.zeros_like(total)

    def scan(tags, begin):
        def step(s, n):
            order[n] = begin + s
            tag = tags[s] - first
            return n + ((tag > 0) & (tag <= wide)).astype(jnp.int32)

        return step

    n = lax.fori_loop(0, slots, scan(own, 0), jnp.int32(0), unroll=8)
    n = lax.fori_loop(0, slots, scan(others, slots), n, unroll=8)
    for extra in range(REST):
        order[n + extra] = order[jnp.maximum(n - 1, 0)]

    def down(row):
        return jnp.transpose(jnp.broadcast_to(row, (TILE, TILE)))

    def add(at):
        s = order[at]
        used = (at < n).astype(f32)
        far = (s >= slots).astype(jnp.int32)
        s = s - far * slots
        src, slot = s >> 1, s & 1
        flip = (core + far) & 1
        t = jnp.clip(jnp.where(far == 1, others[s], own[s]) - first - 1, 0, wide - 1)
        value_re, value_im, row, col = (
            jnp.where(far == 1, mate[src, slot * 4 + i], data[src, slot * 4 + i]) for i in range(4)
        )
        value_re = value_re * used
        value_im = value_im * (used * (1.0 - 2.0 * flip.astype(f32)))
        rows = taps(cells[flip] - row * 0.25)
        cols = taps(cells[2 + flip] - down(col * 0.25))
        weighted = jnp.concatenate([cols * down(value_re), cols * down(value_im)], axis=1)
        sub = mm(spread(rows, LEFT[6], 1), spread(weighted, RIGHT[6], 0))
        for q in range(4):
            for ri in range(2):
                total[(q - me) & 3, ri, t] += sub[32 * q : 32 * q + 32, 128 * ri : 128 * ri + 128]

    def turn(start, count):
        def body(g, _):
            for u in range(count):
                add(start + g * count + u)
            return 0

        return body

    whole = n // GROUP
    lax.fori_loop(0, whole, turn(0, GROUP), 0)
    begun = whole * GROUP
    lax.fori_loop(0, (n - begun + REST - 1) // REST, turn(begun, REST), 0)


def cols_kernel(*refs):
    me, whole, parts, (tw, w, w_back, out, mid) = refs[0], refs[1], refs[2:6], refs[6:]
    parts = (parts[0].ready(), *parts[1:])
    tw = tw.ready()

    def tile(b, ri, at):
        group = b // 16
        if b % 16 < CUT:
            return whole[(me[0] + group) & 3, ri, b % 16, at, :]
        return parts[-group % 4][ri, b % 16 - CUT, at, :]

    def rows(i, _):
        at = pl.ds(pl.multiple_of(i * 8, 8), 8)
        first = [(tile(b, 0, at), tile(b, 1, at)) for b in range(64)]
        for c, (re, im) in enumerate(fft_list(first)):
            cos, sin = tw[me[0], 0, c : c + 1, :], tw[me[0], 1, c : c + 1, :]
            half, c = c // 32, c % 32
            to = 32 * half + c if c <= 16 else 32 * (1 - half) + 48 - c
            mid[to, at, 0:128] = re * cos - im * sin
            mid[to, at, 128:256] = re * sin + im * cos
        return 0

    lax.fori_loop(0, 4, rows, 0)
    for pair in range(8):
        part = spread(mid[8 * pair : 8 * pair + 8].reshape(256, 256), RIGHT[6], 1)
        res = mm((w if pair % 4 < 2 else w_back)[...], part, NT)
        if pair % 4 == 2:
            own = mm(w[...], part[0:128], NT)
            own = jnp.concatenate([jnp.where(low_lanes(), own, res[:, 0:128]), res[:, 128:256]], axis=1)
            res = own
        for k in range(2):
            chunk = 2 * pair + k
            for ri in range(2):
                out[:, chunk // 8, ri * 8 + chunk % 8, :] = res[64 * ri : 64 * ri + 64, 128 * k : 128 * k + 128]


def row_transform(xi, amplitude, tw, w, out, mid, tags):
    def rows(i, _):
        at = pl.ds(pl.multiple_of(i * 8, 8), 8)
        first = [
            xi[at, 128 * b : 128 * b + 128] * amplitude[at, 128 * b : 128 * b + 128] for b in range(32)
        ]
        for c, (re, im) in enumerate(rfft_list(first)):
            cos, sin = tw[0, c : c + 1, :], tw[1, c : c + 1, :]
            if im is None:
                mid[c, at, 0:128] = re * cos
                mid[c, at, 128:256] = re * sin
            else:
                mid[c, at, 0:128] = re * cos - im * sin
                mid[c, at, 128:256] = re * sin + im * cos
        return 0

    lax.fori_loop(0, 4, rows, 0)
    for pair in range(2):
        part = spread(mid[8 * pair : 8 * pair + 8].reshape(256, 256), RIGHT[3], 1)
        res = mm(w[...], part, NT)
        for k in range(2):
            for ri in range(2):
                out[:, 8 + ri * 4 + 2 * pair + k, 0, :] = res[128 * ri : 128 * ri + 128, 128 * k : 128 * k + 128]
    part = spread(mid[16:20].reshape(128, 256), RIGHT[3], 1)
    res = mm(w[...], part, NT)
    out[:, 16, 0, :] = beside(res[0:128], res[128:256]) + tags[:, 0, :]


def low_lanes():
    return lax.broadcasted_iota(jnp.int32, (128, 128), 1) < 32


def beside(a, b):
    lane = lax.broadcasted_iota(jnp.int32, (128, 128), 1)
    return jnp.where(lane < 32, a, jnp.where(lane < 64, pltpu.roll(b, 32, 1), 0.0))


def column_pairs(field, pair):
    chunk = []
    for k in range(2):
        j = 2 * pair + k
        re, im = field[:, 8 + j % 4, 0, :], field[:, 12 + j % 4, 0, :]
        if j >= 4:
            im = -im
        if j == 4:
            own = field[:, 16, 0, :]
            re, im = jnp.where(low_lanes(), own, re), jnp.where(low_lanes(), pltpu.roll(own, 96, 1), im)
        chunk.append((re, im))
    return jnp.concatenate(
        [jnp.concatenate([chunk[k][ri] for k in range(2)], axis=1) for ri in range(2)], axis=0
    )


def chunks(ref, pair):
    return jnp.concatenate(
        [jnp.concatenate([ref[:, ri * 8 + 2 * pair + k, :] for k in range(2)], axis=1) for ri in range(2)],
        axis=0,
    )


def twist(re, im, tw):
    return re * tw[0] - im * tw[1], re * tw[1] + im * tw[0]


def halves(a, at):
    return [a[at : at + 128, 128 * k : 128 * k + 128] for k in range(2)]


def stacked(rows):
    return jnp.concatenate([jnp.concatenate(r, axis=1) for r in rows], axis=0)


def sky_kernel(field, w, tw, r, out):
    for pair in range(4):
        a = mm(w[...], spread(column_pairs(field, pair), RIGHT[3], 0))
        turn = stacked([twist(re, im, tw) for re, im in zip(halves(a, 0), halves(a, 128))])
        out[pair] = jnp.exp(mm(spread(turn, LEFT[3], 1), r[...]))


def image_kernel(sky, uv, w, tw_f, r_y, w_b, tw_b, r_b, out):
    done = []
    for pair in range(4):
        a = mm(w_b[...], spread(chunks(uv, pair), RIGHT[3], 0))
        parts = [[], []]
        for h in range(2):
            for k, (re, im) in enumerate(zip(halves(a, 256 * h), halves(a, 256 * h + 128))):
                parts[k] += twist(re, im, tw_b[h])
        back = mm(spread(stacked(parts), LEFT[3], 1), r_b[...])
        a = mm(spread(sky[pair] * back, LEFT[3], 1), r_y[...])
        turn = [twist(a[128 * k : 128 * k + 128, 0:128], a[128 * k : 128 * k + 128, 128:256], tw_f) for k in range(2)]
        turn = jnp.concatenate([jnp.concatenate([turn[k][ri] for k in range(2)], axis=1) for ri in range(2)], axis=0)
        done.append(mm(w[...], spread(turn, RIGHT[3], 0)))
    for j in range(4):
        at = slice(128 * (j % 2), 128 * (j % 2) + 128)
        straight, mirrored = done[j // 2][:, at], done[2 + j // 2][:, at]
        re, im = mirrored[0:128], mirrored[128:256]
        if j == 0:
            out[:, 8, 0, :] = beside(re, im)
            re, im = jnp.where(low_lanes(), 0.0, re), jnp.where(low_lanes(), 0.0, im)
        out[:, j, 0, :] = straight[0:128] + im
        out[:, 4 + j, 0, :] = straight[128:256] + re


def last_kernel(folded, amplitude, tw, w, out, mid):
    def residue(c, v):
        cos, sin = tw[0, c : c + 1, :], tw[1, c : c + 1, :]
        re, im = v[:, 0:128], v[:, 128:256]
        mid[c, :, 0:128] = re * cos - im * sin
        mid[c, :, 128:256] = re * sin + im * cos

    for j in range(4):
        z = jnp.concatenate([folded[:, j, 0, :], folded[:, 4 + j, 0, :]], axis=0)
        v = mm(spread(z, LEFT[3], 0), w[...], TN)
        for k in range(4):
            residue(4 * j + k, v[32 * k : 32 * k + 32])
    own = folded[:, 8, 0, :]
    z = jnp.concatenate([own, pltpu.roll(own, 96, 1)], axis=0)
    residue(16, mm(spread(z, LEFT[3], 0), w[...], TN)[0:32])

    def rows(i, _):
        at = pl.ds(pl.multiple_of(i * 8, 8), 8)
        first = [(mid[c, at, 0:128], mid[c, at, 128:256]) for c in range(17)] + [None] * 15
        for b, (re, im) in enumerate(fft_list(first)):
            to = slice(128 * b, 128 * b + 128)
            out[at, to] = amplitude[at, to] * (re + im) * (1.0 / IMG)
        return 0

    lax.fori_loop(0, 4, rows, 0)


def per_device(residual, position, owner, tile_local, xi, amplitude):
    n_base = lax.axis_size("base")
    n_slab = lax.axis_size("slab")
    devices = n_base * n_slab
    everywhere = ("base", "slab")
    t = {k: jnp.asarray(v) for k, v in tables(n_base, n_slab).items()}

    def exchange(a, axis):
        return lax.all_to_all(a, axis, split_axis=0, concat_axis=0, tiled=True)

    rows, width = xi.shape
    blocks = residual.shape[0]
    me = jnp.stack([lax.axis_index("base"), lax.axis_index("slab") & 1]).astype(jnp.int32)
    packed = call(
        first_kernel,
        (devices, 17, 1, 128),
        [SM, SM] + [VM] * 6,
        [SM((devices,), jnp.int32), VM((20, 32, 256), f32), VM((devices, 1, 128), f32)],
        2e9,
        [
            (0, SM((blocks,), jnp.int32)),
            (1, SM((blocks,), jnp.int32)),
            (2, VM(residual.shape, f32)),
            (3, VM(position.shape, f32)),
            (4, VM((rows, width), f32)),
            (5, VM((rows, width), f32)),
            (6, VM((2, 32, 128), f32)),
            (7, VM((256, 768), bf16)),
        ],
    )(owner[:, 0], tile_local, residual, position, xi, amplitude, t["tw_row"], t["w128"])
    data = exchange(packed, everywhere)
    mate = lax.ppermute(data, "slab", [(i, i ^ 1) for i in range(n_slab)])
    tags = tuple(a[:, 16, 0, 64:66].reshape(2 * devices).astype(jnp.int32) for a in (data, mate))
    spare = [VM((4, TILE, TILE), f32), SM((4 * devices + REST,), jnp.int32)]
    whole = call(
        functools.partial(grid_whole_kernel, 0), (n_base, 2, CUT, 32, 128), [SM, SM, SM, VM, VM], spare, 2e10
    )(me, *tags, data, mate)
    whole, tags = lax.optimization_barrier((whole, tags))
    whole = exchange(whole, "base")
    shape = (2, 16 - CUT, 32, 128)
    parts = call(
        functools.partial(grid_parts_kernel, CUT),
        [shape] * n_base,
        [SM, SM, SM, VM, VM],
        [*spare, VM((n_base, *shape), f32)],
        2e10,
    )(me, *tags, data, mate)
    parts, field = lax.optimization_barrier((parts, data))
    parts = [parts[0]] + [
        lax.ppermute(parts[k], "base", [(i, (i + k) % n_base) for i in range(n_base)]) for k in range(1, n_base)
    ]
    sky = call(
        sky_kernel,
        (4, 256, 128),
        [VM] * 4,
        (),
        4e9,
        [(1, VM((256, 768), bf16)), (2, VM((2, 128, 128), f32)), (3, VM((768, 128), bf16))],
        True,
    )(field, t["w128"], t["tw_f"], t["r_f"])
    parts[0], sky = lax.optimization_barrier((parts[0], sky))
    cols = call(
        cols_kernel,
        (devices // 2, 2, 16, 128),
        [SM] + [VM] * 8,
        [VM((64, 32, 256), f32)],
        4e9,
        [
            (2, VM(shape, f32)),
            (6, VM((n_base, 2, 64, 128), f32)),
            (7, VM((128, 1536), bf16)),
            (8, VM((128, 1536), bf16)),
        ],
    )(me, whole, *parts, t["tw_cols"], t["w_cols"], t["w_back"])
    cols = exchange(cols.reshape(devices, 16, 128), everywhere)
    fold = call(
        image_kernel,
        (devices, 9, 1, 128),
        [VM] * 8,
        (),
        8e9,
        [
            (0, VM((4, 256, 128), f32)),
            (5, VM((512, 768), bf16)),
            (7, VM((1536, 128), bf16)),
        ],
    )(sky, cols, t["w128"], t["tw_f"], t["r_y"], t["w_b"], t["tw_b"], t["r_b"])
    fold = exchange(fold, everywhere)
    return call(last_kernel, (32, IMG), [VM] * 4, [VM((32, 32, 256), f32)], 3e9)(
        fold, amplitude, t["tw_row"], t["w128t"]
    )


def solution(mesh):
    placed = (
        P(("base", "slab"), None, None),
        P(("base", "slab"), None, None),
        P(("base", "slab"), None),
        P(("base", "slab")),
        P(("base", "slab"), None),
        P(("base", "slab"), None),
    )
    return jax.shard_map(
        per_device, mesh=mesh, in_specs=placed, out_specs=P(("base", "slab"), None), check_vma=False
    )
```

```python
import functools
import math

import jax
import jax.numpy as jnp
import ml_dtypes
import numpy as np
from jax import lax
from jax.experimental import pallas as pl
from jax.experimental.pallas import tpu as pltpu
from jax.sharding import PartitionSpec as P

G = 8192
IMG = 4096
TILE = 128
GROUP = 24
REST = 8
GRANT = 20 * 2**20

NN = (((1,), (0,)), ((), ()))
NT = (((1,), (1,)), ((), ()))
TN = (((0,), (0,)), ((), ()))
f32 = jnp.float32
bf16 = jnp.bfloat16


LEFT = {6: (0, 0, 1, 1, 0, 2), 3: (0, 0, 1)}
RIGHT = {6: (0, 1, 0, 1, 2, 0), 3: (0, 1, 0)}


def pieces(x, count=3):
    out, rest = [], x
    for k in range(count):
        out.append(rest.astype(bf16))
        if k + 1 < count:
            rest = rest - out[-1].astype(f32)
    return out


def spread(x, order, axis):
    cut = pieces(x, max(order) + 1)
    return jnp.concatenate([cut[k] for k in order], axis=axis)


def mm(a, b, dims=NN):
    return lax.dot_general(a, b, dims, preferred_element_type=f32)


def spread_table(x, order, axis):
    cut, rest = [], x.astype(np.float64)
    for _ in range(max(order) + 1):
        cut.append(rest.astype(np.float32).astype(ml_dtypes.bfloat16))
        rest = rest - cut[-1].astype(np.float64)
    return np.concatenate([cut[k] for k in order], axis=axis)


def wave(rows, cols, modulus):
    turn = np.outer(rows, cols).astype(np.int64) % modulus
    angle = turn * (2.0 * np.pi / modulus)
    return np.cos(angle), np.sin(angle)


def turned(c, s):
    return np.block([[c, -s], [s, c]])


@functools.lru_cache(None)
def tables(n_base, n_slab):
    n = np.arange
    devices = n_base * n_slab
    out = {}
    c, s = wave(n(128), n(128), 128)
    out["w128"] = spread_table(turned(c, s), LEFT[3], 1)
    out["w128t"] = spread_table(turned(c, s).T, RIGHT[3], 0)
    out["tw_row"] = np.stack(wave(n(32), n(128), IMG))
    c, s = wave(n(64) + 32, n(128), 128)
    out["w_cols"] = spread_table(turned(c, s), LEFT[6], 1)
    out["w_back"] = spread_table(turned(c[::-1], s[::-1]), LEFT[6], 1)
    out["tw_cols"] = np.stack([np.stack(wave(n(64), n(128) + G // n_base * me, G)) for me in range(n_base)])
    eye = np.eye(4)
    c, s = wave(n(128), n(32), IMG)
    out["tw_f"] = np.stack([np.tile(c, (1, 4)), np.tile(s, (1, 4))])
    c, s = wave(n(32), n(32), 32)
    out["r_f"] = spread_table(np.concatenate([np.kron(eye, c + s), np.kron(eye, c - s)]) / IMG, RIGHT[3], 0)
    out["r_y"] = spread_table(np.concatenate([np.kron(eye, c), np.kron(eye, s)], axis=1), RIGHT[3], 0)
    src = n(devices)
    place = (src % n_slab) * n_base + src // n_slab
    wb, twb, rb = [], [], []
    for half in range(2):
        c, s = wave(n(128) + 128 * half, place, 256)
        wb.append(turned(c, s))
        c, s = wave(n(128) + 128 * half, n(32), G)
        twb.append(np.stack([np.tile(c, (1, 4)), np.tile(s, (1, 4))]))
        c, s = wave(n(32), n(32) // 2 + 8, 32)
        keep = (n(32) % 2 == half)[None, :]
        rb += [np.kron(eye, c * keep) / G, np.kron(eye, -s * keep) / G]
    out["w_b"] = spread_table(np.concatenate(wb), LEFT[3], 1)
    out["tw_b"] = np.stack(twb)
    out["r_b"] = spread_table(np.concatenate(rb), RIGHT[3], 0)
    return {k: v if v.dtype == ml_dtypes.bfloat16 else v.astype(np.float32) for k, v in out.items()}


def times(z, k, n):
    re, im = z
    k %= n
    if k == 0:
        return z
    if 4 * k == n:
        return -im, re
    c, s = math.cos(2 * math.pi * k / n), math.sin(2 * math.pi * k / n)
    if 8 * k == n:
        return (re - im) * c, (re + im) * c
    if 8 * k == 3 * n:
        return (re + im) * -s, (re - im) * s
    return re * c - im * s, re * s + im * c


def fft_list(xs):
    n = len(xs)
    if n == 1:
        return xs
    even, odd = fft_list(xs[0::2]), fft_list(xs[1::2])
    low, high = [], []
    for k in range(n // 2):
        if odd[k] is None:
            low.append(even[k])
            high.append(even[k])
            continue
        (a, b), (c, d) = even[k], times(odd[k], k, n)
        low.append((a + c, b + d))
        high.append((a - c, b - d))
    return low + high


def rfft_list(xs):
    n = len(xs)
    if n == 2:
        return [(xs[0] + xs[1], None), (xs[0] - xs[1], None)]
    even, odd = rfft_list(xs[0::2]), rfft_list(xs[1::2])
    out = [None] * (n // 2 + 1)
    out[0] = (even[0][0] + odd[0][0], None)
    out[n // 2] = (even[0][0] - odd[0][0], None)
    out[n // 4] = (even[n // 4][0], odd[n // 4][0])
    for k in range(1, n // 4):
        (a, b), (c, d) = even[k], times(odd[k], k, n)
        out[k] = (a + c, b + d)
        out[n // 2 - k] = (a - c, d - b)
    return out


class Late:
    def __init__(self, ref, copy):
        self.ref, self.copy, self.shape = ref, copy, ref.shape

    def ready(self):
        if self.copy is not None:
            self.copy.wait()
            self.copy = None
        return self.ref

    def __getitem__(self, at):
        return self.ready()[at]


def call(body, out_shapes, in_specs, scratch=(), flops=0, far=(), far_out=False):
    outs = [out_shapes] if isinstance(out_shapes[0], int) else list(out_shapes)
    count, own, made = len(in_specs), len(scratch), len(outs)
    specs = [pl.BlockSpec(memory_space=m) for m in in_specs]
    for i, _ in far:
        specs[i] = pl.BlockSpec(memory_space=pltpu.HBM)

    def kernel(*refs):
        ins, results = list(refs[:count]), list(refs[count : count + made])
        rest = refs[count + made : count + made + own]
        spare = refs[count + made + own :]
        copies = []
        for k, (i, _) in enumerate(far):
            copies.append(pltpu.make_async_copy(ins[i], spare[k], spare[-1].at[k]))
            copies[-1].start()
            ins[i] = Late(spare[k], copies[-1])
        if not far_out:
            body(*ins, *results, *rest)
            return
        body(*ins, spare[len(far)], *rest)
        last = pltpu.make_async_copy(spare[len(far)], results[0], spare[-1].at[len(far)])
        last.start()
        last.wait()

    more = [shape for _, shape in far] + ([VM(outs[0], f32)] if far_out else [])
    if more:
        more.append(pltpu.SemaphoreType.DMA((len(more),)))
    made_in = pltpu.HBM if far_out else pltpu.VMEM
    got = pl.pallas_call(
        kernel,
        out_shape=[(pltpu.HBM if far_out else jax.ShapeDtypeStruct)(shape, f32) for shape in outs],
        in_specs=specs,
        out_specs=[pl.BlockSpec(memory_space=made_in)] * made,
        scratch_shapes=list(scratch) + more,
        compiler_params=pltpu.CompilerParams(vmem_limit_bytes=GRANT),
        cost_estimate=pl.CostEstimate(
            flops=int(flops), bytes_accessed=8 * sum(map(math.prod, outs)), transcendentals=0
        ),
    )

    def placed(*arrays):
        arrays = list(arrays)
        for i, _ in far:
            arrays[i] = pltpu.with_memory_space_constraint(arrays[i], pltpu.HBM)
        results = got(*arrays)
        return results[0] if isinstance(out_shapes[0], int) else results

    return placed


VM = pltpu.VMEM
SM = pltpu.SMEM


def first_kernel(owner, tile, residual, position, xi, amplitude, tw, w, out, count, mid, tags):
    n_base, n_slab = 4, 32

    def clear(i, _):
        count[i] = 0
        return 0

    lax.fori_loop(0, count.shape[0], clear, 0, unroll=8)
    owner, tile, residual, position = (a.ready() for a in (owner, tile, residual, position))
    lane = lax.broadcasted_iota(jnp.int32, (1, 128), 1)
    tags[...] = jnp.zeros_like(tags)

    def step(i, _):
        placed = []
        for u in range(8):
            at = i * 8 + u
            o, t = owner[at], tile[at]
            row = (o & (n_slab - 1)) * 2 + (t >> 4)
            group, col = o >> 5, t & 15
            flip = (row >= n_slab).astype(jnp.int32)
            row = jnp.where(flip == 1, 2 * n_slab - 1 - row, row)
            group = jnp.where(flip == 1, n_base - 1 - group, group)
            col = jnp.where(flip == 1, 15 - col, col)
            k = count[o]
            count[o] = k + 1
            to = group * n_slab + (row & ~1) + flip
            k = k & 1
            placed.append((at, to, k, (col + 1).astype(f32), 66 + 2 * (row & 1) + k, (1 + (col >> 3)).astype(f32)))
        parts = [(residual[at], position[at]) for at, *_ in placed]
        for (at, to, slot, tag, spot, phase), (value, place) in zip(placed, parts):
            for part in range(2):
                out[to, slot * 4 + part] = value[part : part + 1]
                out[to, slot * 4 + 2 + part] = place[part : part + 1]
            tags[to] = jnp.where(lane == 64 + slot, tag, jnp.where(lane == spot, phase, tags[to]))
        return 0

    lax.fori_loop(0, owner.shape[0] // 8, step, 0)
    row_transform(*(a.ready() for a in (xi, amplitude, tw, w)), out, mid, tags)


def taps(d):
    x = jnp.maximum(1.0 - d * d, 0.0)
    return x * x * x


def grid_whole_kernel(first, me, own, others, data, mate, total, cells, order):
    grid_into(first, 0, me[1], own, others, data, mate, total, cells, order)


def grid_parts_kernel(first, me, own, others, data, mate, out0, out1, out2, out3, cells, order, total):
    grid_into(first, me[0], me[1], own, others, data, mate, total, cells, order)
    for k, out in enumerate((out0, out1, out2, out3)):
        out[...] = total[k]


def grid_into(first, me, core, own, others, data, mate, total, cells, order):
    sources, wide = own.shape[0] // 6, total.shape[2]
    slots = 2 * sources
    for axis in range(2):
        at = lax.broadcasted_iota(jnp.int32, (TILE, TILE), axis).astype(f32)
        cells[2 * axis] = at * 0.25
        cells[2 * axis + 1] = (float(TILE) - at) * 0.25
    total[...] = jnp.zeros_like(total)

    def scan(tags, begin):
        def step(src, n):
            for slot in range(2):
                order[n] = begin + 2 * src + slot
                phase = tags[6 * src + 2 + 2 * core + slot]
                n = n + (phase & 1 if first == 0 else phase >> 1)
            return n

        return step

    n = lax.fori_loop(0, sources, scan(own, 0), jnp.int32(0), unroll=8)
    n = lax.fori_loop(0, sources, scan(others, slots), n, unroll=8)
    for extra in range(REST):
        order[n + extra] = order[jnp.maximum(n - 1, 0)]

    def down(row):
        return jnp.transpose(jnp.broadcast_to(row, (TILE, TILE)))

    def add(at):
        s = order[at]
        used = (at < n).astype(f32)
        far = (s >= slots).astype(jnp.int32)
        s = s - far * slots
        src, slot = s >> 1, s & 1
        flip = (core + far) & 1
        tag = 6 * src + slot
        t = jnp.clip(jnp.where(far == 1, others[tag], own[tag]) - first - 1, 0, wide - 1)
        value_re, value_im, row, col = (
            jnp.where(far == 1, mate[src, slot * 4 + i], data[src, slot * 4 + i]) for i in range(4)
        )
        value_re = value_re * used
        value_im = value_im * (used * (1.0 - 2.0 * flip.astype(f32)))
        rows = taps(cells[flip] - row * 0.25)
        cols = taps(cells[2 + flip] - down(col * 0.25))
        weighted = jnp.concatenate([cols * down(value_re), cols * down(value_im)], axis=1)
        sub = mm(spread(rows, LEFT[6], 1), spread(weighted, RIGHT[6], 0))
        for q in range(4):
            for ri in range(2):
                total[(q - me) & 3, ri, t] += sub[32 * q : 32 * q + 32, 128 * ri : 128 * ri + 128]

    def turn(start, count):
        def body(g, _):
            for u in range(count):
                add(start + g * count + u)
            return 0

        return body

    whole = n // GROUP
    lax.fori_loop(0, whole, turn(0, GROUP), 0)
    begun = whole * GROUP
    lax.fori_loop(0, (n - begun + REST - 1) // REST, turn(begun, REST), 0)


def cols_kernel(*refs):
    me, whole, parts, (tw, w, w_back, out, mid) = refs[0], refs[1], refs[2:6], refs[6:]

    def tile(b, ri, at):
        group = b // 16
        if b % 16 < 8:
            return whole[(me[0] + group) & 3, ri, b % 8, at, :]
        return parts[-group % 4][ri, b % 8, at, :]

    def rows(i, _):
        at = pl.ds(pl.multiple_of(i * 8, 8), 8)
        first = [(tile(b, 0, at), tile(b, 1, at)) for b in range(64)]
        for c, (re, im) in enumerate(fft_list(first)):
            half, c = c // 32, c % 32
            to = 32 * half + c if c <= 16 else 32 * (1 - half) + 48 - c
            mid[to, at, 0:128] = re
            mid[to, at, 128:256] = im
        return 0

    def turned_rows(to):
        half, c = to // 32, to % 32
        c = 32 * half + c if c <= 16 else 32 * (1 - half) + 48 - c
        cos, sin = tw[me[0], 0, c : c + 1, :], tw[me[0], 1, c : c + 1, :]
        re, im = mid[to, :, 0:128], mid[to, :, 128:256]
        return jnp.concatenate([re * cos - im * sin, re * sin + im * cos], axis=1)

    lax.fori_loop(0, 4, rows, 0)
    for pair in range(8):
        part = jnp.concatenate([turned_rows(8 * pair + k) for k in range(8)], axis=0)
        part = spread(part, RIGHT[6], 1)
        res = mm((w if pair % 4 < 2 else w_back)[...], part, NT)
        if pair % 4 == 2:
            own = mm(w[...], part[0:128], NT)
            own = jnp.concatenate([jnp.where(low_lanes(), own, res[:, 0:128]), res[:, 128:256]], axis=1)
            res = own
        for k in range(2):
            chunk = 2 * pair + k
            for ri in range(2):
                out[:, chunk // 8, ri * 8 + chunk % 8, :] = res[64 * ri : 64 * ri + 64, 128 * k : 128 * k + 128]


def row_transform(xi, amplitude, tw, w, out, mid, tags):
    def rows(i, _):
        at = pl.ds(pl.multiple_of(i * 8, 8), 8)
        first = [
            xi[at, 128 * b : 128 * b + 128] * amplitude[at, 128 * b : 128 * b + 128] for b in range(32)
        ]
        for c, (re, im) in enumerate(rfft_list(first)):
            cos, sin = tw[0, c : c + 1, :], tw[1, c : c + 1, :]
            if im is None:
                mid[c, at, 0:128] = re * cos
                mid[c, at, 128:256] = re * sin
            else:
                mid[c, at, 0:128] = re * cos - im * sin
                mid[c, at, 128:256] = re * sin + im * cos
        return 0

    lax.fori_loop(0, 4, rows, 0)
    for pair in range(2):
        part = spread(mid[8 * pair : 8 * pair + 8].reshape(256, 256), RIGHT[3], 1)
        res = mm(w[...], part, NT)
        for k in range(2):
            for ri in range(2):
                out[:, 8 + ri * 4 + 2 * pair + k, 0, :] = res[128 * ri : 128 * ri + 128, 128 * k : 128 * k + 128]
    part = spread(mid[16:20].reshape(128, 256), RIGHT[3], 1)
    res = mm(w[...], part, NT)
    out[:, 16, 0, :] = beside(res[0:128], res[128:256]) + tags[:, 0, :]


def low_lanes():
    return lax.broadcasted_iota(jnp.int32, (128, 128), 1) < 32


def beside(a, b):
    lane = lax.broadcasted_iota(jnp.int32, (128, 128), 1)
    return jnp.where(lane < 32, a, jnp.where(lane < 64, pltpu.roll(b, 32, 1), 0.0))


def column_pairs(field, pair):
    chunk = []
    for k in range(2):
        j = 2 * pair + k
        re, im = field[:, 8 + j % 4, 0, :], field[:, 12 + j % 4, 0, :]
        if j >= 4:
            im = -im
        if j == 4:
            own = field[:, 16, 0, :]
            re, im = jnp.where(low_lanes(), own, re), jnp.where(low_lanes(), pltpu.roll(own, 96, 1), im)
        chunk.append((re, im))
    return jnp.concatenate(
        [jnp.concatenate([chunk[k][ri] for k in range(2)], axis=1) for ri in range(2)], axis=0
    )


def chunks(ref, pair):
    return jnp.concatenate(
        [jnp.concatenate([ref[:, ri * 8 + 2 * pair + k, :] for k in range(2)], axis=1) for ri in range(2)],
        axis=0,
    )


def twist(re, im, tw):
    return re * tw[0] - im * tw[1], re * tw[1] + im * tw[0]


def halves(a, at):
    return [a[at : at + 128, 128 * k : 128 * k + 128] for k in range(2)]


def stacked(rows):
    return jnp.concatenate([jnp.concatenate(r, axis=1) for r in rows], axis=0)


def sky_kernel(field, w, tw, r, out):
    for pair in range(4):
        a = mm(w[...], spread(column_pairs(field, pair), RIGHT[3], 0))
        turn = stacked([twist(re, im, tw) for re, im in zip(halves(a, 0), halves(a, 128))])
        out[pair] = jnp.exp(mm(spread(turn, LEFT[3], 1), r[...]))


def image_kernel(sky, uv, w, tw_f, r_y, w_b, tw_b, r_b, out):
    done = []
    for pair in range(4):
        a = mm(w_b[...], spread(chunks(uv, pair), RIGHT[3], 0))
        parts = [[], []]
        for h in range(2):
            for k, (re, im) in enumerate(zip(halves(a, 256 * h), halves(a, 256 * h + 128))):
                parts[k] += twist(re, im, tw_b[h])
        back = mm(spread(stacked(parts), LEFT[3], 1), r_b[...])
        a = mm(spread(sky[pair] * back, LEFT[3], 1), r_y[...])
        turn = [twist(a[128 * k : 128 * k + 128, 0:128], a[128 * k : 128 * k + 128, 128:256], tw_f) for k in range(2)]
        turn = jnp.concatenate([jnp.concatenate([turn[k][ri] for k in range(2)], axis=1) for ri in range(2)], axis=0)
        done.append(mm(w[...], spread(turn, RIGHT[3], 0)))
    for j in range(4):
        at = slice(128 * (j % 2), 128 * (j % 2) + 128)
        straight, mirrored = done[j // 2][:, at], done[2 + j // 2][:, at]
        re, im = mirrored[0:128], mirrored[128:256]
        if j == 0:
            out[:, 8, 0, :] = beside(re, im)
            re, im = jnp.where(low_lanes(), 0.0, re), jnp.where(low_lanes(), 0.0, im)
        out[:, j, 0, :] = straight[0:128] + im
        out[:, 4 + j, 0, :] = straight[128:256] + re


def last_kernel(folded, amplitude, tw, w, out, mid):
    def residue(c, v):
        cos, sin = tw[0, c : c + 1, :], tw[1, c : c + 1, :]
        re, im = v[:, 0:128], v[:, 128:256]
        mid[c, :, 0:128] = re * cos - im * sin
        mid[c, :, 128:256] = re * sin + im * cos

    for j in range(4):
        z = jnp.concatenate([folded[:, j, 0, :], folded[:, 4 + j, 0, :]], axis=0)
        v = mm(spread(z, LEFT[3], 0), w[...], TN)
        for k in range(4):
            residue(4 * j + k, v[32 * k : 32 * k + 32])
    own = folded[:, 8, 0, :]
    z = jnp.concatenate([own, pltpu.roll(own, 96, 1)], axis=0)
    residue(16, mm(spread(z, LEFT[3], 0), w[...], TN)[0:32])

    def rows(i, _):
        at = pl.ds(pl.multiple_of(i * 8, 8), 8)
        first = [(mid[c, at, 0:128], mid[c, at, 128:256]) for c in range(17)] + [None] * 15
        for b, (re, im) in enumerate(fft_list(first)):
            to = slice(128 * b, 128 * b + 128)
            out[at, to] = amplitude[at, to] * (re + im) * (1.0 / IMG)
        return 0

    lax.fori_loop(0, 4, rows, 0)


def per_device(residual, position, owner, tile_local, xi, amplitude):
    n_base = lax.axis_size("base")
    n_slab = lax.axis_size("slab")
    devices = n_base * n_slab
    everywhere = ("base", "slab")
    t = {k: jnp.asarray(v) for k, v in tables(n_base, n_slab).items()}

    def exchange(a, axis):
        return lax.all_to_all(a, axis, split_axis=0, concat_axis=0, tiled=True)

    rows, width = xi.shape
    blocks = residual.shape[0]
    me = jnp.stack([lax.axis_index("base"), lax.axis_index("slab") & 1]).astype(jnp.int32)
    packed = call(
        first_kernel,
        (devices, 17, 1, 128),
        [SM, SM] + [VM] * 6,
        [SM((devices,), jnp.int32), VM((20, 32, 256), f32), VM((devices, 1, 128), f32)],
        2e9,
        [
            (0, SM((blocks,), jnp.int32)),
            (1, SM((blocks,), jnp.int32)),
            (2, VM(residual.shape, f32)),
            (3, VM(position.shape, f32)),
            (4, VM((rows, width), f32)),
            (5, VM((rows, width), f32)),
            (6, VM((2, 32, 128), f32)),
            (7, VM((256, 768), bf16)),
        ],
    )(owner[:, 0], tile_local, residual, position, xi, amplitude, t["tw_row"], t["w128"])
    data = exchange(packed, everywhere)
    mate = lax.ppermute(data, "slab", [(i, i ^ 1) for i in range(n_slab)])
    tags = tuple(a[:, 16, 0, 64:70].reshape(6 * devices).astype(jnp.int32) for a in (data, mate))
    spare = [VM((4, TILE, TILE), f32), SM((4 * devices + REST,), jnp.int32)]
    shape = (2, 8, 32, 128)
    whole = call(
        functools.partial(grid_whole_kernel, 0), (n_base, *shape), [SM, SM, SM, VM, VM], spare, 2e10
    )(me, *tags, data, mate)
    whole, tags = lax.optimization_barrier((whole, tags))
    whole = exchange(whole, "base")
    parts = call(
        functools.partial(grid_parts_kernel, 8),
        [shape] * n_base,
        [SM, SM, SM, VM, VM],
        [*spare, VM((n_base, *shape), f32)],
        2e10,
    )(me, *tags, data, mate)
    parts, field = lax.optimization_barrier((parts, data))
    parts = [parts[0]] + [
        lax.ppermute(parts[k], "base", [(i, (i + k) % n_base) for i in range(n_base)]) for k in range(1, n_base)
    ]
    sky = call(
        sky_kernel,
        (4, 256, 128),
        [VM] * 4,
        (),
        4e9,
        [(1, VM((256, 768), bf16)), (2, VM((2, 128, 128), f32)), (3, VM((768, 128), bf16))],
        True,
    )(field, t["w128"], t["tw_f"], t["r_f"])
    parts[0], sky = lax.optimization_barrier((parts[0], sky))
    cols = call(
        cols_kernel,
        (devices // 2, 2, 16, 128),
        [SM] + [VM] * 8,
        [VM((64, 32, 256), f32)],
        4e9,
        [
            (6, VM((n_base, 2, 64, 128), f32)),
            (7, VM((128, 1536), bf16)),
            (8, VM((128, 1536), bf16)),
        ],
    )(me, whole, *parts, t["tw_cols"], t["w_cols"], t["w_back"])
    cols = exchange(cols.reshape(devices, 16, 128), everywhere)
    fold = call(
        image_kernel,
        (devices, 9, 1, 128),
        [VM] * 8,
        (),
        8e9,
        [
            (0, VM((4, 256, 128), f32)),
            (5, VM((512, 768), bf16)),
            (7, VM((1536, 128), bf16)),
        ],
    )(sky, cols, t["w128"], t["tw_f"], t["r_y"], t["w_b"], t["tw_b"], t["r_b"])
    fold = exchange(fold, everywhere)
    return call(last_kernel, (32, IMG), [VM] * 4, [VM((32, 32, 256), f32)], 3e9)(
        fold, amplitude, t["tw_row"], t["w128t"]
    )


def solution(mesh):
    placed = (
        P(("base", "slab"), None, None),
        P(("base", "slab"), None, None),
        P(("base", "slab"), None),
        P(("base", "slab")),
        P(("base", "slab"), None),
        P(("base", "slab"), None),
    )
    return jax.shard_map(
        per_device, mesh=mesh, in_specs=placed, out_specs=P(("base", "slab"), None), check_vma=False
    )
```

```python
import functools
import math

import jax
import jax.numpy as jnp
import ml_dtypes
import numpy as np
from jax import lax
from jax.experimental import pallas as pl
from jax.experimental.pallas import tpu as pltpu
from jax.sharding import PartitionSpec as P

G = 8192
IMG = 4096
TILE = 128
GROUP = 24
REST = 8
GRANT = 20 * 2**20

NN = (((1,), (0,)), ((), ()))
NT = (((1,), (1,)), ((), ()))
TN = (((0,), (0,)), ((), ()))
f32 = jnp.float32
bf16 = jnp.bfloat16


LEFT = {6: (0, 0, 1, 1, 0, 2), 3: (0, 0, 1)}
RIGHT = {6: (0, 1, 0, 1, 2, 0), 3: (0, 1, 0)}


def pieces(x, count=3):
    out, rest = [], x
    for k in range(count):
        out.append(rest.astype(bf16))
        if k + 1 < count:
            rest = rest - out[-1].astype(f32)
    return out


def spread(x, order, axis):
    cut = pieces(x, max(order) + 1)
    return jnp.concatenate([cut[k] for k in order], axis=axis)


def mm(a, b, dims=NN):
    return lax.dot_general(a, b, dims, preferred_element_type=f32)


def spread_table(x, order, axis):
    cut, rest = [], x.astype(np.float64)
    for _ in range(max(order) + 1):
        cut.append(rest.astype(np.float32).astype(ml_dtypes.bfloat16))
        rest = rest - cut[-1].astype(np.float64)
    return np.concatenate([cut[k] for k in order], axis=axis)


def wave(rows, cols, modulus):
    turn = np.outer(rows, cols).astype(np.int64) % modulus
    angle = turn * (2.0 * np.pi / modulus)
    return np.cos(angle), np.sin(angle)


def turned(c, s):
    return np.block([[c, -s], [s, c]])


@functools.lru_cache(None)
def tables(n_base, n_slab):
    n = np.arange
    devices = n_base * n_slab
    out = {}
    c, s = wave(n(128), n(128), 128)
    out["w128"] = spread_table(turned(c, s), LEFT[3], 1)
    out["w128t"] = spread_table(turned(c, s).T, RIGHT[3], 0)
    out["tw_row"] = np.stack(wave(n(32), n(128), IMG))
    c, s = wave(n(64) + 32, n(128), 128)
    out["w_cols"] = spread_table(turned(c, s), LEFT[6], 1)
    out["w_back"] = spread_table(turned(c[::-1], s[::-1]), LEFT[6], 1)
    out["tw_cols"] = np.stack([np.stack(wave(n(64), n(128) + G // n_base * me, G)) for me in range(n_base)])
    eye = np.eye(4)
    c, s = wave(n(128), n(32), IMG)
    out["tw_f"] = np.stack([np.tile(c, (1, 4)), np.tile(s, (1, 4))])
    c, s = wave(n(32), n(32), 32)
    out["r_f"] = spread_table(np.concatenate([np.kron(eye, c + s), np.kron(eye, c - s)]) / IMG, RIGHT[3], 0)
    out["r_y"] = spread_table(np.concatenate([np.kron(eye, c), np.kron(eye, s)], axis=1), RIGHT[3], 0)
    src = n(devices)
    place = (src % n_slab) * n_base + src // n_slab
    wb, twb, rb = [], [], []
    for half in range(2):
        c, s = wave(n(128) + 128 * half, place, 256)
        wb.append(turned(c, s))
        c, s = wave(n(128) + 128 * half, n(32), G)
        twb.append(np.stack([np.tile(c, (1, 4)), np.tile(s, (1, 4))]))
        c, s = wave(n(32), n(32) // 2 + 8, 32)
        keep = (n(32) % 2 == half)[None, :]
        rb += [np.kron(eye, c * keep) / G, np.kron(eye, -s * keep) / G]
    out["w_b"] = spread_table(np.concatenate(wb), LEFT[3], 1)
    out["tw_b"] = np.stack(twb)
    out["r_b"] = spread_table(np.concatenate(rb), RIGHT[3], 0)
    return {k: v if v.dtype == ml_dtypes.bfloat16 else v.astype(np.float32) for k, v in out.items()}


def times(z, k, n):
    re, im = z
    k %= n
    if k == 0:
        return z
    if 4 * k == n:
        return -im, re
    c, s = math.cos(2 * math.pi * k / n), math.sin(2 * math.pi * k / n)
    if 8 * k == n:
        return (re - im) * c, (re + im) * c
    if 8 * k == 3 * n:
        return (re + im) * -s, (re - im) * s
    return re * c - im * s, re * s + im * c


def fft_list(xs):
    n = len(xs)
    if n == 1:
        return xs
    even, odd = fft_list(xs[0::2]), fft_list(xs[1::2])
    low, high = [], []
    for k in range(n // 2):
        if odd[k] is None:
            low.append(even[k])
            high.append(even[k])
            continue
        (a, b), (c, d) = even[k], times(odd[k], k, n)
        low.append((a + c, b + d))
        high.append((a - c, b - d))
    return low + high


def rfft_list(xs):
    n = len(xs)
    if n == 2:
        return [(xs[0] + xs[1], None), (xs[0] - xs[1], None)]
    even, odd = rfft_list(xs[0::2]), rfft_list(xs[1::2])
    out = [None] * (n // 2 + 1)
    out[0] = (even[0][0] + odd[0][0], None)
    out[n // 2] = (even[0][0] - odd[0][0], None)
    out[n // 4] = (even[n // 4][0], odd[n // 4][0])
    for k in range(1, n // 4):
        (a, b), (c, d) = even[k], times(odd[k], k, n)
        out[k] = (a + c, b + d)
        out[n // 2 - k] = (a - c, d - b)
    return out


class Late:
    def __init__(self, ref, copy):
        self.ref, self.copy, self.shape = ref, copy, ref.shape

    def ready(self):
        if self.copy is not None:
            self.copy.wait()
            self.copy = None
        return self.ref

    def __getitem__(self, at):
        return self.ready()[at]


def call(body, out_shapes, in_specs, scratch=(), flops=0, far=(), far_out=False):
    outs = [out_shapes] if isinstance(out_shapes[0], int) else list(out_shapes)
    count, own, made = len(in_specs), len(scratch), len(outs)
    specs = [pl.BlockSpec(memory_space=m) for m in in_specs]
    for i, _ in far:
        specs[i] = pl.BlockSpec(memory_space=pltpu.HBM)

    def kernel(*refs):
        ins, results = list(refs[:count]), list(refs[count : count + made])
        rest = refs[count + made : count + made + own]
        spare = refs[count + made + own :]
        copies = []
        for k, (i, _) in enumerate(far):
            copies.append(pltpu.make_async_copy(ins[i], spare[k], spare[-1].at[k]))
            copies[-1].start()
            ins[i] = Late(spare[k], copies[-1])
        if not far_out:
            body(*ins, *results, *rest)
            return
        body(*ins, spare[len(far)], *rest)
        last = pltpu.make_async_copy(spare[len(far)], results[0], spare[-1].at[len(far)])
        last.start()
        last.wait()

    more = [shape for _, shape in far] + ([VM(outs[0], f32)] if far_out else [])
    if more:
        more.append(pltpu.SemaphoreType.DMA((len(more),)))
    made_in = pltpu.HBM if far_out else pltpu.VMEM
    got = pl.pallas_call(
        kernel,
        out_shape=[(pltpu.HBM if far_out else jax.ShapeDtypeStruct)(shape, f32) for shape in outs],
        in_specs=specs,
        out_specs=[pl.BlockSpec(memory_space=made_in)] * made,
        scratch_shapes=list(scratch) + more,
        compiler_params=pltpu.CompilerParams(vmem_limit_bytes=GRANT),
        cost_estimate=pl.CostEstimate(
            flops=int(flops), bytes_accessed=8 * sum(map(math.prod, outs)), transcendentals=0
        ),
    )

    def placed(*arrays):
        arrays = list(arrays)
        for i, _ in far:
            arrays[i] = pltpu.with_memory_space_constraint(arrays[i], pltpu.HBM)
        results = got(*arrays)
        return results[0] if isinstance(out_shapes[0], int) else results

    return placed


VM = pltpu.VMEM
SM = pltpu.SMEM


def first_kernel(owner, tile, residual, position, xi, amplitude, tw, w, out, count, mid, tags):
    n_base, n_slab = 4, 32

    def clear(i, _):
        count[i] = 0
        return 0

    lax.fori_loop(0, count.shape[0], clear, 0, unroll=8)
    owner, tile, residual, position = (a.ready() for a in (owner, tile, residual, position))
    lane = lax.broadcasted_iota(jnp.int32, (1, 128), 1)
    tags[...] = jnp.zeros_like(tags)

    def step(i, _):
        placed = []
        for u in range(8):
            at = i * 8 + u
            o, t = owner[at], tile[at]
            row = (o & (n_slab - 1)) * 2 + (t >> 4)
            group, col = o >> 5, t & 15
            flip = (row >= n_slab).astype(jnp.int32)
            row = jnp.where(flip == 1, 2 * n_slab - 1 - row, row)
            group = jnp.where(flip == 1, n_base - 1 - group, group)
            col = jnp.where(flip == 1, 15 - col, col)
            k = count[o]
            count[o] = k + 1
            to = group * n_slab + (row & ~1) + flip
            k = k & 1
            placed.append((at, to, k, (col + 1).astype(f32), 66 + 2 * (row & 1) + k, (1 + (col >> 3)).astype(f32)))
        parts = [(residual[at], position[at]) for at, *_ in placed]
        for (at, to, slot, tag, spot, phase), (value, place) in zip(placed, parts):
            for part in range(2):
                out[to, slot * 4 + part] = value[part : part + 1]
                out[to, slot * 4 + 2 + part] = place[part : part + 1]
            tags[to] = jnp.where(lane == 64 + slot, tag, jnp.where(lane == spot, phase, tags[to]))
        return 0

    lax.fori_loop(0, owner.shape[0] // 8, step, 0)
    row_transform(*(a.ready() for a in (xi, amplitude, tw, w)), out, mid, tags)


def taps(d):
    x = jnp.maximum(1.0 - d * d, 0.0)
    return x * x * x


def grid_parts_kernel(first, me, own, others, data, mate, out0, out1, out2, out3, cells, order, total):
    grid_into(first, me[0], me[1], own, others, data, mate, total, cells, order)
    for k, out in enumerate((out0, out1, out2, out3)):
        out[...] = total[k]


def grid_into(first, me, core, own, others, data, mate, total, cells, order):
    sources, wide = own.shape[0] // 6, total.shape[2]
    slots = 2 * sources
    for axis in range(2):
        at = lax.broadcasted_iota(jnp.int32, (TILE, TILE), axis).astype(f32)
        cells[2 * axis] = at * 0.25
        cells[2 * axis + 1] = (float(TILE) - at) * 0.25
    total[...] = jnp.zeros_like(total)

    def scan(tags, begin):
        def step(src, n):
            for slot in range(2):
                order[n] = begin + 2 * src + slot
                phase = tags[6 * src + 2 + 2 * core + slot]
                n = n + (phase & 1 if first == 0 else phase >> 1)
            return n

        return step

    n = lax.fori_loop(0, sources, scan(own, 0), jnp.int32(0), unroll=8)
    n = lax.fori_loop(0, sources, scan(others, slots), n, unroll=8)
    for extra in range(REST):
        order[n + extra] = order[jnp.maximum(n - 1, 0)]

    def down(row):
        return jnp.transpose(jnp.broadcast_to(row, (TILE, TILE)))

    def add(at):
        s = order[at]
        used = (at < n).astype(f32)
        far = (s >= slots).astype(jnp.int32)
        s = s - far * slots
        src, slot = s >> 1, s & 1
        flip = (core + far) & 1
        tag = 6 * src + slot
        t = jnp.clip(jnp.where(far == 1, others[tag], own[tag]) - first - 1, 0, wide - 1)
        value_re, value_im, row, col = (
            jnp.where(far == 1, mate[src, slot * 4 + i], data[src, slot * 4 + i]) for i in range(4)
        )
        value_re = value_re * used
        value_im = value_im * (used * (1.0 - 2.0 * flip.astype(f32)))
        rows = taps(cells[flip] - row * 0.25)
        cols = taps(cells[2 + flip] - down(col * 0.25))
        weighted = jnp.concatenate([cols * down(value_re), cols * down(value_im)], axis=1)
        sub = mm(spread(rows, LEFT[6], 1), spread(weighted, RIGHT[6], 0))
        for q in range(4):
            for ri in range(2):
                total[(q - me) & 3, ri, t] += sub[32 * q : 32 * q + 32, 128 * ri : 128 * ri + 128]

    def turn(start, count):
        def body(g, _):
            for u in range(count):
                add(start + g * count + u)
            return 0

        return body

    whole = n // GROUP
    lax.fori_loop(0, whole, turn(0, GROUP), 0)
    begun = whole * GROUP
    lax.fori_loop(0, (n - begun + REST - 1) // REST, turn(begun, REST), 0)


def cols_kernel(*refs):
    me, parts, (tw, w, w_back, out, mid) = refs[0], refs[1:9], refs[9:]

    def tile(b, ri, at):
        return parts[b % 16 // 8 * 4 + -(b // 16) % 4][ri, b % 8, at, :]

    def rows(i, _):
        at = pl.ds(pl.multiple_of(i * 8, 8), 8)
        first = [(tile(b, 0, at), tile(b, 1, at)) for b in range(64)]
        for c, (re, im) in enumerate(fft_list(first)):
            half, c = c // 32, c % 32
            to = 32 * half + c if c <= 16 else 32 * (1 - half) + 48 - c
            mid[to, at, 0:128] = re
            mid[to, at, 128:256] = im
        return 0

    def turned_rows(to):
        half, c = to // 32, to % 32
        c = 32 * half + c if c <= 16 else 32 * (1 - half) + 48 - c
        cos, sin = tw[me[0], 0, c : c + 1, :], tw[me[0], 1, c : c + 1, :]
        re, im = mid[to, :, 0:128], mid[to, :, 128:256]
        return jnp.concatenate([re * cos - im * sin, re * sin + im * cos], axis=1)

    lax.fori_loop(0, 4, rows, 0)
    for pair in range(8):
        part = jnp.concatenate([turned_rows(8 * pair + k) for k in range(8)], axis=0)
        part = spread(part, RIGHT[6], 1)
        res = mm((w if pair % 4 < 2 else w_back)[...], part, NT)
        if pair % 4 == 2:
            own = mm(w[...], part[0:128], NT)
            own = jnp.concatenate([jnp.where(low_lanes(), own, res[:, 0:128]), res[:, 128:256]], axis=1)
            res = own
        for k in range(2):
            chunk = 2 * pair + k
            for ri in range(2):
                out[:, chunk // 8, ri * 8 + chunk % 8, :] = res[64 * ri : 64 * ri + 64, 128 * k : 128 * k + 128]


def row_transform(xi, amplitude, tw, w, out, mid, tags):
    def rows(i, _):
        at = pl.ds(pl.multiple_of(i * 8, 8), 8)
        first = [
            xi[at, 128 * b : 128 * b + 128] * amplitude[at, 128 * b : 128 * b + 128] for b in range(32)
        ]
        for c, (re, im) in enumerate(rfft_list(first)):
            cos, sin = tw[0, c : c + 1, :], tw[1, c : c + 1, :]
            if im is None:
                mid[c, at, 0:128] = re * cos
                mid[c, at, 128:256] = re * sin
            else:
                mid[c, at, 0:128] = re * cos - im * sin
                mid[c, at, 128:256] = re * sin + im * cos
        return 0

    lax.fori_loop(0, 4, rows, 0)
    for pair in range(2):
        part = spread(mid[8 * pair : 8 * pair + 8].reshape(256, 256), RIGHT[3], 1)
        res = mm(w[...], part, NT)
        for k in range(2):
            for ri in range(2):
                out[:, 8 + ri * 4 + 2 * pair + k, 0, :] = res[128 * ri : 128 * ri + 128, 128 * k : 128 * k + 128]
    part = spread(mid[16:20].reshape(128, 256), RIGHT[3], 1)
    res = mm(w[...], part, NT)
    out[:, 16, 0, :] = beside(res[0:128], res[128:256]) + tags[:, 0, :]


def low_lanes():
    return lax.broadcasted_iota(jnp.int32, (128, 128), 1) < 32


def beside(a, b):
    lane = lax.broadcasted_iota(jnp.int32, (128, 128), 1)
    return jnp.where(lane < 32, a, jnp.where(lane < 64, pltpu.roll(b, 32, 1), 0.0))


def column_pairs(field, pair):
    chunk = []
    for k in range(2):
        j = 2 * pair + k
        re, im = field[:, 8 + j % 4, 0, :], field[:, 12 + j % 4, 0, :]
        if j >= 4:
            im = -im
        if j == 4:
            own = field[:, 16, 0, :]
            re, im = jnp.where(low_lanes(), own, re), jnp.where(low_lanes(), pltpu.roll(own, 96, 1), im)
        chunk.append((re, im))
    return jnp.concatenate(
        [jnp.concatenate([chunk[k][ri] for k in range(2)], axis=1) for ri in range(2)], axis=0
    )


def chunks(ref, pair):
    return jnp.concatenate(
        [jnp.concatenate([ref[:, ri * 8 + 2 * pair + k, :] for k in range(2)], axis=1) for ri in range(2)],
        axis=0,
    )


def twist(re, im, tw):
    return re * tw[0] - im * tw[1], re * tw[1] + im * tw[0]


def halves(a, at):
    return [a[at : at + 128, 128 * k : 128 * k + 128] for k in range(2)]


def stacked(rows):
    return jnp.concatenate([jnp.concatenate(r, axis=1) for r in rows], axis=0)


def sky_kernel(field, w, tw, r, out):
    for pair in range(4):
        a = mm(w[...], spread(column_pairs(field, pair), RIGHT[3], 0))
        turn = stacked([twist(re, im, tw) for re, im in zip(halves(a, 0), halves(a, 128))])
        out[pair] = jnp.exp(mm(spread(turn, LEFT[3], 1), r[...]))


def image_kernel(sky, uv, w, tw_f, r_y, w_b, tw_b, r_b, out):
    done = []
    for pair in range(4):
        a = mm(w_b[...], spread(chunks(uv, pair), RIGHT[3], 0))
        parts = [[], []]
        for h in range(2):
            for k, (re, im) in enumerate(zip(halves(a, 256 * h), halves(a, 256 * h + 128))):
                parts[k] += twist(re, im, tw_b[h])
        back = mm(spread(stacked(parts), LEFT[3], 1), r_b[...])
        a = mm(spread(sky[pair] * back, LEFT[3], 1), r_y[...])
        turn = [twist(a[128 * k : 128 * k + 128, 0:128], a[128 * k : 128 * k + 128, 128:256], tw_f) for k in range(2)]
        turn = jnp.concatenate([jnp.concatenate([turn[k][ri] for k in range(2)], axis=1) for ri in range(2)], axis=0)
        done.append(mm(w[...], spread(turn, RIGHT[3], 0)))
    for j in range(4):
        at = slice(128 * (j % 2), 128 * (j % 2) + 128)
        straight, mirrored = done[j // 2][:, at], done[2 + j // 2][:, at]
        re, im = mirrored[0:128], mirrored[128:256]
        if j == 0:
            out[:, 8, 0, :] = beside(re, im)
            re, im = jnp.where(low_lanes(), 0.0, re), jnp.where(low_lanes(), 0.0, im)
        out[:, j, 0, :] = straight[0:128] + im
        out[:, 4 + j, 0, :] = straight[128:256] + re


def last_kernel(folded, amplitude, tw, w, out, mid):
    def residue(c, v):
        cos, sin = tw[0, c : c + 1, :], tw[1, c : c + 1, :]
        re, im = v[:, 0:128], v[:, 128:256]
        mid[c, :, 0:128] = re * cos - im * sin
        mid[c, :, 128:256] = re * sin + im * cos

    for j in range(4):
        z = jnp.concatenate([folded[:, j, 0, :], folded[:, 4 + j, 0, :]], axis=0)
        v = mm(spread(z, LEFT[3], 0), w[...], TN)
        for k in range(4):
            residue(4 * j + k, v[32 * k : 32 * k + 32])
    own = folded[:, 8, 0, :]
    z = jnp.concatenate([own, pltpu.roll(own, 96, 1)], axis=0)
    residue(16, mm(spread(z, LEFT[3], 0), w[...], TN)[0:32])

    def rows(i, _):
        at = pl.ds(pl.multiple_of(i * 8, 8), 8)
        first = [(mid[c, at, 0:128], mid[c, at, 128:256]) for c in range(17)] + [None] * 15
        for b, (re, im) in enumerate(fft_list(first)):
            to = slice(128 * b, 128 * b + 128)
            out[at, to] = amplitude[at, to] * (re + im) * (1.0 / IMG)
        return 0

    lax.fori_loop(0, 4, rows, 0)


def per_device(residual, position, owner, tile_local, xi, amplitude):
    n_base = lax.axis_size("base")
    n_slab = lax.axis_size("slab")
    devices = n_base * n_slab
    everywhere = ("base", "slab")
    t = {k: jnp.asarray(v) for k, v in tables(n_base, n_slab).items()}

    def exchange(a, axis):
        return lax.all_to_all(a, axis, split_axis=0, concat_axis=0, tiled=True)

    rows, width = xi.shape
    blocks = residual.shape[0]
    me = jnp.stack([lax.axis_index("base"), lax.axis_index("slab") & 1]).astype(jnp.int32)
    packed = call(
        first_kernel,
        (devices, 17, 1, 128),
        [SM, SM] + [VM] * 6,
        [SM((devices,), jnp.int32), VM((20, 32, 256), f32), VM((devices, 1, 128), f32)],
        2e9,
        [
            (0, SM((blocks,), jnp.int32)),
            (1, SM((blocks,), jnp.int32)),
            (2, VM(residual.shape, f32)),
            (3, VM(position.shape, f32)),
            (4, VM((rows, width), f32)),
            (5, VM((rows, width), f32)),
            (6, VM((2, 32, 128), f32)),
            (7, VM((256, 768), bf16)),
        ],
    )(owner[:, 0], tile_local, residual, position, xi, amplitude, t["tw_row"], t["w128"])
    data = exchange(packed, everywhere)
    mate = lax.ppermute(data, "slab", [(i, i ^ 1) for i in range(n_slab)])
    tags = tuple(a[:, 16, 0, 64:70].reshape(6 * devices).astype(jnp.int32) for a in (data, mate))
    spare = [VM((4, TILE, TILE), f32), SM((4 * devices + REST,), jnp.int32)]
    shape = (2, 8, 32, 128)
    grids = []
    for phase in range(2):
        parts = call(
            functools.partial(grid_parts_kernel, 8 * phase),
            [shape] * n_base,
            [SM, SM, SM, VM, VM],
            [*spare, VM((n_base, *shape), f32)],
            2e10,
        )(me, *tags, data, mate)
        if phase == 0:
            parts, tags = lax.optimization_barrier((parts, tags))
        else:
            parts, grids, field = lax.optimization_barrier((parts, grids, data))
        grids = [*grids, parts[0]] + [
            lax.ppermute(parts[k], "base", [(i, (i + k) % n_base) for i in range(n_base)]) for k in range(1, n_base)
        ]
    sky = call(
        sky_kernel,
        (4, 256, 128),
        [VM] * 4,
        (),
        4e9,
        [(1, VM((256, 768), bf16)), (2, VM((2, 128, 128), f32)), (3, VM((768, 128), bf16))],
        True,
    )(field, t["w128"], t["tw_f"], t["r_f"])
    grids[0], sky = lax.optimization_barrier((grids[0], sky))
    cols = call(
        cols_kernel,
        (devices // 2, 2, 16, 128),
        [SM] + [VM] * 11,
        [VM((64, 32, 256), f32)],
        4e9,
        [
            (9, VM((n_base, 2, 64, 128), f32)),
            (10, VM((128, 1536), bf16)),
            (11, VM((128, 1536), bf16)),
        ],
    )(me, *grids, t["tw_cols"], t["w_cols"], t["w_back"])
    cols = exchange(cols.reshape(devices, 16, 128), everywhere)
    fold = call(
        image_kernel,
        (devices, 9, 1, 128),
        [VM] * 8,
        (),
        8e9,
        [
            (0, VM((4, 256, 128), f32)),
            (5, VM((512, 768), bf16)),
            (7, VM((1536, 128), bf16)),
        ],
    )(sky, cols, t["w128"], t["tw_f"], t["r_y"], t["w_b"], t["tw_b"], t["r_b"])
    fold = exchange(fold, everywhere)
    return call(last_kernel, (32, IMG), [VM] * 4, [VM((32, 32, 256), f32)], 3e9)(
        fold, amplitude, t["tw_row"], t["w128t"]
    )


def solution(mesh):
    placed = (
        P(("base", "slab"), None, None),
        P(("base", "slab"), None, None),
        P(("base", "slab"), None),
        P(("base", "slab")),
        P(("base", "slab"), None),
        P(("base", "slab"), None),
    )
    return jax.shard_map(
        per_device, mesh=mesh, in_specs=placed, out_specs=P(("base", "slab"), None), check_vma=False
    )
```

```python
import functools
import math

import jax
import jax.numpy as jnp
import ml_dtypes
import numpy as np
from jax import lax
from jax.experimental import pallas as pl
from jax.experimental.pallas import tpu as pltpu
from jax.sharding import PartitionSpec as P

G = 8192
IMG = 4096
TILE = 128
GROUP = 32
REST = 8
GRANT = 20 * 2**20

NN = (((1,), (0,)), ((), ()))
NT = (((1,), (1,)), ((), ()))
TN = (((0,), (0,)), ((), ()))
f32 = jnp.float32
bf16 = jnp.bfloat16


LEFT = {6: (0, 0, 1, 1, 0, 2), 3: (0, 0, 1)}
RIGHT = {6: (0, 1, 0, 1, 2, 0), 3: (0, 1, 0)}


def pieces(x, count=3):
    out, rest = [], x
    for k in range(count):
        out.append(rest.astype(bf16))
        if k + 1 < count:
            rest = rest - out[-1].astype(f32)
    return out


def spread(x, order, axis):
    cut = pieces(x, max(order) + 1)
    return jnp.concatenate([cut[k] for k in order], axis=axis)


def mm(a, b, dims=NN):
    return lax.dot_general(a, b, dims, preferred_element_type=f32)


def spread_table(x, order, axis):
    cut, rest = [], x.astype(np.float64)
    for _ in range(max(order) + 1):
        cut.append(rest.astype(np.float32).astype(ml_dtypes.bfloat16))
        rest = rest - cut[-1].astype(np.float64)
    return np.concatenate([cut[k] for k in order], axis=axis)


def wave(rows, cols, modulus):
    turn = np.outer(rows, cols).astype(np.int64) % modulus
    angle = turn * (2.0 * np.pi / modulus)
    return np.cos(angle), np.sin(angle)


def turned(c, s):
    return np.block([[c, -s], [s, c]])


@functools.lru_cache(None)
def tables(n_base, n_slab):
    n = np.arange
    devices = n_base * n_slab
    out = {}
    c, s = wave(n(128), n(128), 128)
    out["w128"] = spread_table(turned(c, s), LEFT[3], 1)
    out["w128t"] = spread_table(turned(c, s).T, RIGHT[3], 0)
    out["tw_row"] = np.stack(wave(n(32), n(128), IMG))
    c, s = wave(n(64) + 32, n(128), 128)
    out["w_cols"] = spread_table(turned(c, s), LEFT[6], 1)
    out["w_back"] = spread_table(turned(c[::-1], s[::-1]), LEFT[6], 1)
    out["tw_cols"] = np.stack([np.stack(wave(n(64), n(128) + G // n_base * me, G)) for me in range(n_base)])
    eye = np.eye(4)
    c, s = wave(n(128), n(32), IMG)
    out["tw_f"] = np.stack([np.tile(c, (1, 4)), np.tile(s, (1, 4))])
    c, s = wave(n(32), n(32), 32)
    out["r_f"] = spread_table(np.concatenate([np.kron(eye, c + s), np.kron(eye, c - s)]) / IMG, RIGHT[3], 0)
    out["r_y"] = spread_table(np.concatenate([np.kron(eye, c), np.kron(eye, s)], axis=1), RIGHT[3], 0)
    src = n(devices)
    place = (src % n_slab) * n_base + src // n_slab
    wb, twb, rb = [], [], []
    for half in range(2):
        c, s = wave(n(128) + 128 * half, place, 256)
        wb.append(turned(c, s))
        c, s = wave(n(128) + 128 * half, n(32), G)
        twb.append(np.stack([np.tile(c, (1, 4)), np.tile(s, (1, 4))]))
        c, s = wave(n(32), n(32) // 2 + 8, 32)
        keep = (n(32) % 2 == half)[None, :]
        rb += [np.kron(eye, c * keep) / G, np.kron(eye, -s * keep) / G]
    out["w_b"] = spread_table(np.concatenate(wb), LEFT[3], 1)
    out["tw_b"] = np.stack(twb)
    out["r_b"] = spread_table(np.concatenate(rb), RIGHT[3], 0)
    return {k: v if v.dtype == ml_dtypes.bfloat16 else v.astype(np.float32) for k, v in out.items()}


def times(z, k, n):
    re, im = z
    k %= n
    if k == 0:
        return z
    if 4 * k == n:
        return -im, re
    c, s = math.cos(2 * math.pi * k / n), math.sin(2 * math.pi * k / n)
    if 8 * k == n:
        return (re - im) * c, (re + im) * c
    if 8 * k == 3 * n:
        return (re + im) * -s, (re - im) * s
    return re * c - im * s, re * s + im * c


def fft_list(xs):
    n = len(xs)
    if n == 1:
        return xs
    even, odd = fft_list(xs[0::2]), fft_list(xs[1::2])
    low, high = [], []
    for k in range(n // 2):
        if odd[k] is None:
            low.append(even[k])
            high.append(even[k])
            continue
        (a, b), (c, d) = even[k], times(odd[k], k, n)
        low.append((a + c, b + d))
        high.append((a - c, b - d))
    return low + high


def rfft_list(xs):
    n = len(xs)
    if n == 2:
        return [(xs[0] + xs[1], None), (xs[0] - xs[1], None)]
    even, odd = rfft_list(xs[0::2]), rfft_list(xs[1::2])
    out = [None] * (n // 2 + 1)
    out[0] = (even[0][0] + odd[0][0], None)
    out[n // 2] = (even[0][0] - odd[0][0], None)
    out[n // 4] = (even[n // 4][0], odd[n // 4][0])
    for k in range(1, n // 4):
        (a, b), (c, d) = even[k], times(odd[k], k, n)
        out[k] = (a + c, b + d)
        out[n // 2 - k] = (a - c, d - b)
    return out


class Late:
    def __init__(self, ref, copy):
        self.ref, self.copy, self.shape = ref, copy, ref.shape

    def ready(self):
        if self.copy is not None:
            self.copy.wait()
            self.copy = None
        return self.ref

    def __getitem__(self, at):
        return self.ready()[at]


def call(body, out_shapes, in_specs, scratch=(), flops=0, far=(), far_out=False):
    outs = [out_shapes] if isinstance(out_shapes[0], int) else list(out_shapes)
    count, own, made = len(in_specs), len(scratch), len(outs)
    specs = [pl.BlockSpec(memory_space=m) for m in in_specs]
    for i, _ in far:
        specs[i] = pl.BlockSpec(memory_space=pltpu.HBM)

    def kernel(*refs):
        ins, results = list(refs[:count]), list(refs[count : count + made])
        rest = refs[count + made : count + made + own]
        spare = refs[count + made + own :]
        copies = []
        for k, (i, _) in enumerate(far):
            copies.append(pltpu.make_async_copy(ins[i], spare[k], spare[-1].at[k]))
            copies[-1].start()
            ins[i] = Late(spare[k], copies[-1])
        if not far_out:
            body(*ins, *results, *rest)
            return
        body(*ins, spare[len(far)], *rest)
        last = pltpu.make_async_copy(spare[len(far)], results[0], spare[-1].at[len(far)])
        last.start()
        last.wait()

    more = [shape for _, shape in far] + ([VM(outs[0], f32)] if far_out else [])
    if more:
        more.append(pltpu.SemaphoreType.DMA((len(more),)))
    made_in = pltpu.HBM if far_out else pltpu.VMEM
    got = pl.pallas_call(
        kernel,
        out_shape=[(pltpu.HBM if far_out else jax.ShapeDtypeStruct)(shape, f32) for shape in outs],
        in_specs=specs,
        out_specs=[pl.BlockSpec(memory_space=made_in)] * made,
        scratch_shapes=list(scratch) + more,
        compiler_params=pltpu.CompilerParams(vmem_limit_bytes=GRANT),
        cost_estimate=pl.CostEstimate(
            flops=int(flops), bytes_accessed=8 * sum(map(math.prod, outs)), transcendentals=0
        ),
    )

    def placed(*arrays):
        arrays = list(arrays)
        for i, _ in far:
            arrays[i] = pltpu.with_memory_space_constraint(arrays[i], pltpu.HBM)
        results = got(*arrays)
        return results[0] if isinstance(out_shapes[0], int) else results

    return placed


VM = pltpu.VMEM
SM = pltpu.SMEM


def first_kernel(owner, tile, residual, position, xi, amplitude, tw, w, out, count, mid, tags):
    n_base, n_slab = 4, 32

    def clear(i, _):
        count[i] = 0
        return 0

    lax.fori_loop(0, count.shape[0], clear, 0, unroll=8)
    owner, tile, residual, position = (a.ready() for a in (owner, tile, residual, position))
    lane = lax.broadcasted_iota(jnp.int32, (1, 128), 1)
    tags[...] = jnp.zeros_like(tags)

    def step(i, _):
        placed = []
        for u in range(8):
            at = i * 8 + u
            o, t = owner[at], tile[at]
            row = (o & (n_slab - 1)) * 2 + (t >> 4)
            group, col = o >> 5, t & 15
            flip = (row >= n_slab).astype(jnp.int32)
            row = jnp.where(flip == 1, 2 * n_slab - 1 - row, row)
            group = jnp.where(flip == 1, n_base - 1 - group, group)
            col = jnp.where(flip == 1, 15 - col, col)
            k = count[o]
            count[o] = k + 1
            to = group * n_slab + (row & ~1) + flip
            k = k & 1
            placed.append((at, to, k, (col + 1).astype(f32), 66 + 2 * (row & 1) + k, (1 + (col >> 3)).astype(f32)))
        parts = [(residual[at], position[at]) for at, *_ in placed]
        for (at, to, slot, tag, spot, phase), (value, place) in zip(placed, parts):
            for part in range(2):
                out[to, slot * 4 + part] = value[part : part + 1]
                out[to, slot * 4 + 2 + part] = place[part : part + 1]
            tags[to] = jnp.where(lane == 64 + slot, tag, jnp.where(lane == spot, phase, tags[to]))
        return 0

    lax.fori_loop(0, owner.shape[0] // 8, step, 0)
    row_transform(*(a.ready() for a in (xi, amplitude, tw, w)), out, mid, tags)


def taps(d):
    x = jnp.maximum(1.0 - d * d, 0.0)
    return x * x * x


def grid_parts_kernel(first, me, own, others, data, mate, out0, out1, out2, out3, cells, order, total):
    grid_into(first, me[0], me[1], own, others, data, mate, total, cells, order)
    for k, out in enumerate((out0, out1, out2, out3)):
        out[...] = total[k]


def grid_into(first, me, core, own, others, data, mate, total, cells, order):
    sources, wide = own.shape[0] // 6, total.shape[2]
    slots = 2 * sources
    for axis in range(2):
        at = lax.broadcasted_iota(jnp.int32, (TILE, TILE), axis).astype(f32)
        cells[2 * axis] = at * 0.25
        cells[2 * axis + 1] = (float(TILE) - at) * 0.25
    total[...] = jnp.zeros_like(total)

    def scan(tags, begin):
        def step(src, n):
            for slot in range(2):
                order[n] = begin + 2 * src + slot
                phase = tags[6 * src + 2 + 2 * core + slot]
                n = n + (phase & 1 if first == 0 else phase >> 1)
            return n

        return step

    n = lax.fori_loop(0, sources, scan(own, 0), jnp.int32(0), unroll=8)
    n = lax.fori_loop(0, sources, scan(others, slots), n, unroll=8)
    for extra in range(REST):
        order[n + extra] = order[jnp.maximum(n - 1, 0)]

    def down(row):
        return jnp.transpose(jnp.broadcast_to(row, (TILE, TILE)))

    def add(at):
        s = order[at]
        used = (at < n).astype(f32)
        far = (s >= slots).astype(jnp.int32)
        s = s - far * slots
        src, slot = s >> 1, s & 1
        flip = (core + far) & 1
        tag = 6 * src + slot
        t = jnp.clip(jnp.where(far == 1, others[tag], own[tag]) - first - 1, 0, wide - 1)
        value_re, value_im, row, col = (
            jnp.where(far == 1, mate[src, slot * 4 + i], data[src, slot * 4 + i]) for i in range(4)
        )
        value_re = value_re * used
        value_im = value_im * (used * (1.0 - 2.0 * flip.astype(f32)))
        rows = taps(cells[flip] - row * 0.25)
        cols = taps(cells[2 + flip] - down(col * 0.25))
        weighted = jnp.concatenate([cols * down(value_re), cols * down(value_im)], axis=1)
        sub = mm(spread(rows, LEFT[6], 1), spread(weighted, RIGHT[6], 0))
        for q in range(4):
            for ri in range(2):
                total[(q - me) & 3, ri, t] += sub[32 * q : 32 * q + 32, 128 * ri : 128 * ri + 128]

    def turn(start, count):
        def body(g, _):
            for u in range(count):
                add(start + g * count + u)
            return 0

        return body

    whole = n // GROUP
    lax.fori_loop(0, whole, turn(0, GROUP), 0)
    begun = whole * GROUP
    lax.fori_loop(0, (n - begun + REST - 1) // REST, turn(begun, REST), 0)


def cols_kernel(*refs):
    me, parts, (tw, w, w_back, out, mid) = refs[0], refs[1:9], refs[9:]

    def tile(b, ri, at):
        return parts[b % 16 // 8 * 4 + -(b // 16) % 4][ri, b % 8, at, :]

    def rows(i, _):
        at = pl.ds(pl.multiple_of(i * 8, 8), 8)
        first = [(tile(b, 0, at), tile(b, 1, at)) for b in range(64)]
        for c, (re, im) in enumerate(fft_list(first)):
            half, c = c // 32, c % 32
            to = 32 * half + c if c <= 16 else 32 * (1 - half) + 48 - c
            mid[to, at, 0:128] = re
            mid[to, at, 128:256] = im
        return 0

    def turned_rows(to):
        half, c = to // 32, to % 32
        c = 32 * half + c if c <= 16 else 32 * (1 - half) + 48 - c
        cos, sin = tw[me[0], 0, c : c + 1, :], tw[me[0], 1, c : c + 1, :]
        re, im = mid[to, :, 0:128], mid[to, :, 128:256]
        return jnp.concatenate([re * cos - im * sin, re * sin + im * cos], axis=1)

    lax.fori_loop(0, 4, rows, 0)
    for pair in range(8):
        part = jnp.concatenate([turned_rows(8 * pair + k) for k in range(8)], axis=0)
        part = spread(part, RIGHT[6], 1)
        res = mm((w if pair % 4 < 2 else w_back)[...], part, NT)
        if pair % 4 == 2:
            own = mm(w[...], part[0:128], NT)
            own = jnp.concatenate([jnp.where(low_lanes(), own, res[:, 0:128]), res[:, 128:256]], axis=1)
            res = own
        for k in range(2):
            chunk = 2 * pair + k
            for ri in range(2):
                out[:, chunk // 8, ri * 8 + chunk % 8, :] = res[64 * ri : 64 * ri + 64, 128 * k : 128 * k + 128]


def row_transform(xi, amplitude, tw, w, out, mid, tags):
    def rows(i, _):
        at = pl.ds(pl.multiple_of(i * 8, 8), 8)
        first = [
            xi[at, 128 * b : 128 * b + 128] * amplitude[at, 128 * b : 128 * b + 128] for b in range(32)
        ]
        for c, (re, im) in enumerate(rfft_list(first)):
            cos, sin = tw[0, c : c + 1, :], tw[1, c : c + 1, :]
            if im is None:
                mid[c, at, 0:128] = re * cos
                mid[c, at, 128:256] = re * sin
            else:
                mid[c, at, 0:128] = re * cos - im * sin
                mid[c, at, 128:256] = re * sin + im * cos
        return 0

    lax.fori_loop(0, 4, rows, 0)
    for pair in range(2):
        part = spread(mid[8 * pair : 8 * pair + 8].reshape(256, 256), RIGHT[3], 1)
        res = mm(w[...], part, NT)
        for k in range(2):
            for ri in range(2):
                out[:, 8 + ri * 4 + 2 * pair + k, 0, :] = res[128 * ri : 128 * ri + 128, 128 * k : 128 * k + 128]
    part = spread(mid[16:20].reshape(128, 256), RIGHT[3], 1)
    res = mm(w[...], part, NT)
    out[:, 16, 0, :] = beside(res[0:128], res[128:256]) + tags[:, 0, :]


def low_lanes():
    return lax.broadcasted_iota(jnp.int32, (128, 128), 1) < 32


def beside(a, b):
    lane = lax.broadcasted_iota(jnp.int32, (128, 128), 1)
    return jnp.where(lane < 32, a, jnp.where(lane < 64, pltpu.roll(b, 32, 1), 0.0))


def column_pairs(field, pair):
    chunk = []
    for k in range(2):
        j = 2 * pair + k
        re, im = field[:, 8 + j % 4, 0, :], field[:, 12 + j % 4, 0, :]
        if j >= 4:
            im = -im
        if j == 4:
            own = field[:, 16, 0, :]
            re, im = jnp.where(low_lanes(), own, re), jnp.where(low_lanes(), pltpu.roll(own, 96, 1), im)
        chunk.append((re, im))
    return jnp.concatenate(
        [jnp.concatenate([chunk[k][ri] for k in range(2)], axis=1) for ri in range(2)], axis=0
    )


def chunks(ref, pair):
    return jnp.concatenate(
        [jnp.concatenate([ref[:, ri * 8 + 2 * pair + k, :] for k in range(2)], axis=1) for ri in range(2)],
        axis=0,
    )


def twist(re, im, tw):
    return re * tw[0] - im * tw[1], re * tw[1] + im * tw[0]


def halves(a, at):
    return [a[at : at + 128, 128 * k : 128 * k + 128] for k in range(2)]


def stacked(rows):
    return jnp.concatenate([jnp.concatenate(r, axis=1) for r in rows], axis=0)


def sky_kernel(field, w, tw, r, out):
    for pair in range(4):
        a = mm(w[...], spread(column_pairs(field, pair), RIGHT[3], 0))
        turn = stacked([twist(re, im, tw) for re, im in zip(halves(a, 0), halves(a, 128))])
        out[pair] = jnp.exp(mm(spread(turn, LEFT[3], 1), r[...]))


def image_kernel(sky, uv, w, tw_f, r_y, w_b, tw_b, r_b, out):
    done = []
    for pair in range(4):
        kept = spread(chunks(uv, pair), RIGHT[3], 0)
        a = mm(w_b[...], kept)
        parts = [[], []]
        for h in range(2):
            for k, (re, im) in enumerate(zip(halves(a, 256 * h), halves(a, 256 * h + 128))):
                parts[k] += twist(re, im, tw_b[h])
        back = mm(spread(stacked(parts), LEFT[3], 1), r_b[...])
        a = mm(spread(sky[pair] * back, LEFT[3], 1), r_y[...])
        turn = [twist(a[128 * k : 128 * k + 128, 0:128], a[128 * k : 128 * k + 128, 128:256], tw_f) for k in range(2)]
        turn = jnp.concatenate([jnp.concatenate([turn[k][ri] for k in range(2)], axis=1) for ri in range(2)], axis=0)
        done.append(mm(w[...], spread(turn, RIGHT[3], 0)))
    for j in range(4):
        at = slice(128 * (j % 2), 128 * (j % 2) + 128)
        straight, mirrored = done[j // 2][:, at], done[2 + j // 2][:, at]
        re, im = mirrored[0:128], mirrored[128:256]
        if j == 0:
            out[:, 8, 0, :] = beside(re, im)
            re, im = jnp.where(low_lanes(), 0.0, re), jnp.where(low_lanes(), 0.0, im)
        out[:, j, 0, :] = straight[0:128] + im
        out[:, 4 + j, 0, :] = straight[128:256] + re


def last_kernel(folded, amplitude, tw, w, out, mid):
    def residue(c, v):
        cos, sin = tw[0, c : c + 1, :], tw[1, c : c + 1, :]
        re, im = v[:, 0:128], v[:, 128:256]
        mid[c, :, 0:128] = re * cos - im * sin
        mid[c, :, 128:256] = re * sin + im * cos

    for j in range(4):
        z = jnp.concatenate([folded[:, j, 0, :], folded[:, 4 + j, 0, :]], axis=0)
        v = mm(spread(z, LEFT[3], 0), w[...], TN)
        for k in range(4):
            residue(4 * j + k, v[32 * k : 32 * k + 32])
    own = folded[:, 8, 0, :]
    z = jnp.concatenate([own, pltpu.roll(own, 96, 1)], axis=0)
    residue(16, mm(spread(z, LEFT[3], 0), w[...], TN)[0:32])

    def rows(i, _):
        at = pl.ds(pl.multiple_of(i * 8, 8), 8)
        first = [(mid[c, at, 0:128], mid[c, at, 128:256]) for c in range(17)] + [None] * 15
        for b, (re, im) in enumerate(fft_list(first)):
            to = slice(128 * b, 128 * b + 128)
            out[at, to] = amplitude[at, to] * (re + im) * (1.0 / IMG)
        return 0

    lax.fori_loop(0, 4, rows, 0)


def per_device(residual, position, owner, tile_local, xi, amplitude):
    n_base = lax.axis_size("base")
    n_slab = lax.axis_size("slab")
    devices = n_base * n_slab
    everywhere = ("base", "slab")
    t = {k: jnp.asarray(v) for k, v in tables(n_base, n_slab).items()}

    def exchange(a, axis):
        return lax.all_to_all(a, axis, split_axis=0, concat_axis=0, tiled=True)

    rows, width = xi.shape
    blocks = residual.shape[0]
    me = jnp.stack([lax.axis_index("base"), lax.axis_index("slab") & 1]).astype(jnp.int32)
    packed = call(
        first_kernel,
        (devices, 17, 1, 128),
        [SM, SM] + [VM] * 6,
        [SM((devices,), jnp.int32), VM((20, 32, 256), f32), VM((devices, 1, 128), f32)],
        2e9,
        [
            (0, SM((blocks,), jnp.int32)),
            (1, SM((blocks,), jnp.int32)),
            (2, VM(residual.shape, f32)),
            (3, VM(position.shape, f32)),
            (4, VM((rows, width), f32)),
            (5, VM((rows, width), f32)),
            (6, VM((2, 32, 128), f32)),
            (7, VM((256, 768), bf16)),
        ],
    )(owner[:, 0], tile_local, residual, position, xi, amplitude, t["tw_row"], t["w128"])
    data = exchange(packed, everywhere)
    mate = lax.ppermute(data, "slab", [(i, i ^ 1) for i in range(n_slab)])
    tags = tuple(a[:, 16, 0, 64:70].reshape(6 * devices).astype(jnp.int32) for a in (data, mate))
    spare = [VM((4, TILE, TILE), f32), SM((4 * devices + REST,), jnp.int32)]
    shape = (2, 8, 32, 128)
    grids = []
    for phase in range(2):
        parts = call(
            functools.partial(grid_parts_kernel, 8 * phase),
            [shape] * n_base,
            [SM, SM, SM, VM, VM],
            [*spare, VM((n_base, *shape), f32)],
            2e10,
        )(me, *tags, data, mate)
        if phase == 0:
            parts, tags = lax.optimization_barrier((parts, tags))
        else:
            parts, grids, field = lax.optimization_barrier((parts, grids, data))
        grids = [*grids, parts[0]] + [
            lax.ppermute(parts[k], "base", [(i, (i + k) % n_base) for i in range(n_base)]) for k in range(1, n_base)
        ]
    sky = call(
        sky_kernel,
        (4, 256, 128),
        [VM] * 4,
        (),
        4e9,
        [(1, VM((256, 768), bf16)), (2, VM((2, 128, 128), f32)), (3, VM((768, 128), bf16))],
        True,
    )(field, t["w128"], t["tw_f"], t["r_f"])
    grids[0], sky = lax.optimization_barrier((grids[0], sky))
    cols = call(
        cols_kernel,
        (devices // 2, 2, 16, 128),
        [SM] + [VM] * 11,
        [VM((64, 32, 256), f32)],
        4e9,
        [
            (9, VM((n_base, 2, 64, 128), f32)),
            (10, VM((128, 1536), bf16)),
            (11, VM((128, 1536), bf16)),
        ],
    )(me, *grids, t["tw_cols"], t["w_cols"], t["w_back"])
    cols = exchange(cols.reshape(devices, 16, 128), everywhere)
    fold = call(
        image_kernel,
        (devices, 9, 1, 128),
        [VM] * 8,
        (),
        8e9,
        [
            (0, VM((4, 256, 128), f32)),
            (5, VM((512, 768), bf16)),
            (7, VM((1536, 128), bf16)),
        ],
    )(sky, cols, t["w128"], t["tw_f"], t["r_y"], t["w_b"], t["tw_b"], t["r_b"])
    fold = exchange(fold, everywhere)
    return call(last_kernel, (32, IMG), [VM] * 4, [VM((32, 32, 256), f32)], 3e9)(
        fold, amplitude, t["tw_row"], t["w128t"]
    )


def solution(mesh):
    placed = (
        P(("base", "slab"), None, None),
        P(("base", "slab"), None, None),
        P(("base", "slab"), None),
        P(("base", "slab")),
        P(("base", "slab"), None),
        P(("base", "slab"), None),
    )
    return jax.shard_map(
        per_device, mesh=mesh, in_specs=placed, out_specs=P(("base", "slab"), None), check_vma=False
    )
```

```python
import functools
import math

import jax
import jax.numpy as jnp
import ml_dtypes
import numpy as np
from jax import lax
from jax.experimental import pallas as pl
from jax.experimental.pallas import tpu as pltpu
from jax.sharding import PartitionSpec as P

G = 8192
IMG = 4096
TILE = 128
GROUP = 32
REST = 8
GRANT = 20 * 2**20

NN = (((1,), (0,)), ((), ()))
NT = (((1,), (1,)), ((), ()))
TN = (((0,), (0,)), ((), ()))
f32 = jnp.float32
bf16 = jnp.bfloat16


LEFT = {6: (0, 0, 1, 1, 0, 2), 3: (0, 0, 1)}
RIGHT = {6: (0, 1, 0, 1, 2, 0), 3: (0, 1, 0)}


def pieces(x, count=3):
    out, rest = [], x
    for k in range(count):
        out.append(rest.astype(bf16))
        if k + 1 < count:
            rest = rest - out[-1].astype(f32)
    return out


def spread(x, order, axis):
    cut = pieces(x, max(order) + 1)
    return jnp.concatenate([cut[k] for k in order], axis=axis)


def mm(a, b, dims=NN):
    return lax.dot_general(a, b, dims, preferred_element_type=f32)


def spread_table(x, order, axis):
    cut, rest = [], x.astype(np.float64)
    for _ in range(max(order) + 1):
        cut.append(rest.astype(np.float32).astype(ml_dtypes.bfloat16))
        rest = rest - cut[-1].astype(np.float64)
    return np.concatenate([cut[k] for k in order], axis=axis)


def wave(rows, cols, modulus):
    turn = np.outer(rows, cols).astype(np.int64) % modulus
    angle = turn * (2.0 * np.pi / modulus)
    return np.cos(angle), np.sin(angle)


def turned(c, s):
    return np.block([[c, -s], [s, c]])


@functools.lru_cache(None)
def tables(n_base, n_slab):
    n = np.arange
    devices = n_base * n_slab
    out = {}
    c, s = wave(n(128), n(128), 128)
    out["w128"] = spread_table(turned(c, s), LEFT[3], 1)
    out["w128t"] = spread_table(turned(c, s).T, RIGHT[3], 0)
    out["tw_row"] = np.stack(wave(n(32), n(128), IMG))
    c, s = wave(n(64) + 32, n(128), 128)
    out["w_cols"] = spread_table(turned(c, s), LEFT[6], 1)
    out["w_back"] = spread_table(turned(c[::-1], s[::-1]), LEFT[6], 1)
    out["tw_cols"] = np.stack([np.stack(wave(n(64), n(128) + G // n_base * me, G)) for me in range(n_base)])
    eye = np.eye(4)
    c, s = wave(n(128), n(32), IMG)
    out["tw_f"] = np.stack([np.tile(c, (1, 4)), np.tile(s, (1, 4))])
    c, s = wave(n(32), n(32), 32)
    out["r_f"] = spread_table(np.concatenate([np.kron(eye, c + s), np.kron(eye, c - s)]) / IMG, RIGHT[3], 0)
    out["r_y"] = spread_table(np.concatenate([np.kron(eye, c), np.kron(eye, s)], axis=1), RIGHT[3], 0)
    src = n(devices)
    place = (src % n_slab) * n_base + src // n_slab
    wb, twb, rb = [], [], []
    for half in range(2):
        c, s = wave(n(128) + 128 * half, place, 256)
        wb.append(turned(c, s))
        c, s = wave(n(128) + 128 * half, n(32), G)
        twb.append(np.stack([np.tile(c, (1, 4)), np.tile(s, (1, 4))]))
        c, s = wave(n(32), n(32) // 2 + 8, 32)
        keep = (n(32) % 2 == half)[None, :]
        rb += [np.kron(eye, c * keep) / G, np.kron(eye, -s * keep) / G]
    out["w_b"] = spread_table(np.concatenate(wb), LEFT[3], 1)
    out["tw_b"] = np.stack(twb)
    out["r_b"] = spread_table(np.concatenate(rb), RIGHT[3], 0)
    return {k: v if v.dtype == ml_dtypes.bfloat16 else v.astype(np.float32) for k, v in out.items()}


def times(z, k, n):
    re, im = z
    k %= n
    if k == 0:
        return z
    if 4 * k == n:
        return -im, re
    c, s = math.cos(2 * math.pi * k / n), math.sin(2 * math.pi * k / n)
    if 8 * k == n:
        return (re - im) * c, (re + im) * c
    if 8 * k == 3 * n:
        return (re + im) * -s, (re - im) * s
    return re * c - im * s, re * s + im * c


def fft_list(xs):
    n = len(xs)
    if n == 1:
        return xs
    even, odd = fft_list(xs[0::2]), fft_list(xs[1::2])
    low, high = [], []
    for k in range(n // 2):
        if odd[k] is None:
            low.append(even[k])
            high.append(even[k])
            continue
        (a, b), (c, d) = even[k], times(odd[k], k, n)
        low.append((a + c, b + d))
        high.append((a - c, b - d))
    return low + high


def rfft_list(xs):
    n = len(xs)
    if n == 2:
        return [(xs[0] + xs[1], None), (xs[0] - xs[1], None)]
    even, odd = rfft_list(xs[0::2]), rfft_list(xs[1::2])
    out = [None] * (n // 2 + 1)
    out[0] = (even[0][0] + odd[0][0], None)
    out[n // 2] = (even[0][0] - odd[0][0], None)
    out[n // 4] = (even[n // 4][0], odd[n // 4][0])
    for k in range(1, n // 4):
        (a, b), (c, d) = even[k], times(odd[k], k, n)
        out[k] = (a + c, b + d)
        out[n // 2 - k] = (a - c, d - b)
    return out


class Late:
    def __init__(self, ref, copy):
        self.ref, self.copy, self.shape = ref, copy, ref.shape

    def ready(self):
        if self.copy is not None:
            self.copy.wait()
            self.copy = None
        return self.ref

    def __getitem__(self, at):
        return self.ready()[at]


def call(body, out_shapes, in_specs, scratch=(), flops=0, far=(), far_out=False):
    outs = [out_shapes] if isinstance(out_shapes[0], int) else list(out_shapes)
    count, own, made = len(in_specs), len(scratch), len(outs)
    specs = [pl.BlockSpec(memory_space=m) for m in in_specs]
    for i, _ in far:
        specs[i] = pl.BlockSpec(memory_space=pltpu.HBM)

    def kernel(*refs):
        ins, results = list(refs[:count]), list(refs[count : count + made])
        rest = refs[count + made : count + made + own]
        spare = refs[count + made + own :]
        copies = []
        for k, (i, _) in enumerate(far):
            copies.append(pltpu.make_async_copy(ins[i], spare[k], spare[-1].at[k]))
            copies[-1].start()
            ins[i] = Late(spare[k], copies[-1])
        if not far_out:
            body(*ins, *results, *rest)
            return
        body(*ins, spare[len(far)], *rest)
        last = pltpu.make_async_copy(spare[len(far)], results[0], spare[-1].at[len(far)])
        last.start()
        last.wait()

    more = [shape for _, shape in far] + ([VM(outs[0], f32)] if far_out else [])
    if more:
        more.append(pltpu.SemaphoreType.DMA((len(more),)))
    made_in = pltpu.HBM if far_out else pltpu.VMEM
    got = pl.pallas_call(
        kernel,
        out_shape=[(pltpu.HBM if far_out else jax.ShapeDtypeStruct)(shape, f32) for shape in outs],
        in_specs=specs,
        out_specs=[pl.BlockSpec(memory_space=made_in)] * made,
        scratch_shapes=list(scratch) + more,
        compiler_params=pltpu.CompilerParams(vmem_limit_bytes=GRANT),
        cost_estimate=pl.CostEstimate(
            flops=int(flops), bytes_accessed=8 * sum(map(math.prod, outs)), transcendentals=0
        ),
    )

    def placed(*arrays):
        arrays = list(arrays)
        for i, _ in far:
            arrays[i] = pltpu.with_memory_space_constraint(arrays[i], pltpu.HBM)
        results = got(*arrays)
        return results[0] if isinstance(out_shapes[0], int) else results

    return placed


VM = pltpu.VMEM
SM = pltpu.SMEM


def first_kernel(owner, tile, residual, position, xi, amplitude, tw, w, out, count, mid, tags):
    n_base, n_slab = 4, 32

    def clear(i, _):
        count[i] = 0
        return 0

    lax.fori_loop(0, count.shape[0], clear, 0, unroll=8)
    owner, tile, residual, position = (a.ready() for a in (owner, tile, residual, position))
    lane = lax.broadcasted_iota(jnp.int32, (1, 128), 1)
    tags[...] = jnp.zeros_like(tags)

    def step(i, _):
        placed = []
        for u in range(8):
            at = i * 8 + u
            o, t = owner[at], tile[at]
            row = (o & (n_slab - 1)) * 2 + (t >> 4)
            group, col = o >> 5, t & 15
            flip = (row >= n_slab).astype(jnp.int32)
            row = jnp.where(flip == 1, 2 * n_slab - 1 - row, row)
            group = jnp.where(flip == 1, n_base - 1 - group, group)
            col = jnp.where(flip == 1, 15 - col, col)
            k = count[o]
            count[o] = k + 1
            to = group * n_slab + (row & ~1) + flip
            k = k & 1
            placed.append((at, to, k, (col + 1).astype(f32), 66 + 2 * (row & 1) + k, (1 + (col >> 3)).astype(f32)))
        parts = [(residual[at], position[at]) for at, *_ in placed]
        for (at, to, slot, tag, spot, phase), (value, place) in zip(placed, parts):
            for part in range(2):
                out[to, slot * 4 + part] = value[part : part + 1]
                out[to, slot * 4 + 2 + part] = place[part : part + 1]
            tags[to] = jnp.where(lane == 64 + slot, tag, jnp.where(lane == spot, phase, tags[to]))
        return 0

    lax.fori_loop(0, owner.shape[0] // 8, step, 0)
    row_transform(*(a.ready() for a in (xi, amplitude, tw, w)), out, mid, tags)


def taps(d):
    x = jnp.maximum(1.0 - d * d, 0.0)
    return x * x * x


def grid_parts_kernel(first, me, own, others, data, mate, out0, out1, out2, out3, cells, order, total):
    grid_into(first, me[0], me[1], own, others, data, mate, total, cells, order)
    for k, out in enumerate((out0, out1, out2, out3)):
        out[...] = total[k]


def grid_into(first, me, core, own, others, data, mate, total, cells, order):
    sources, wide = own.shape[0] // 6, total.shape[2]
    slots = 2 * sources
    for axis in range(2):
        at = lax.broadcasted_iota(jnp.int32, (TILE, TILE), axis).astype(f32)
        cells[2 * axis] = at * 0.25
        cells[2 * axis + 1] = (float(TILE) - at) * 0.25
    total[...] = jnp.zeros_like(total)

    def scan(tags, begin):
        def step(src, n):
            for slot in range(2):
                order[n] = begin + 2 * src + slot
                phase = tags[6 * src + 2 + 2 * core + slot]
                n = n + (phase & 1 if first == 0 else phase >> 1)
            return n

        return step

    n = lax.fori_loop(0, sources, scan(own, 0), jnp.int32(0), unroll=8)
    n = lax.fori_loop(0, sources, scan(others, slots), n, unroll=8)
    for extra in range(REST):
        order[n + extra] = order[jnp.maximum(n - 1, 0)]

    def down(row):
        return jnp.transpose(jnp.broadcast_to(row, (TILE, TILE)))

    def add(at):
        s = order[at]
        used = (at < n).astype(f32)
        far = (s >= slots).astype(jnp.int32)
        s = s - far * slots
        src, slot = s >> 1, s & 1
        flip = (core + far) & 1
        tag = 6 * src + slot
        t = jnp.clip(jnp.where(far == 1, others[tag], own[tag]) - first - 1, 0, wide - 1)
        value_re, value_im, row, col = (
            jnp.where(far == 1, mate[src, slot * 4 + i], data[src, slot * 4 + i]) for i in range(4)
        )
        value_re = value_re * used
        value_im = value_im * (used * (1.0 - 2.0 * flip.astype(f32)))
        rows = taps(cells[flip] - row * 0.25)
        cols = taps(cells[2 + flip] - down(col * 0.25))
        weighted = jnp.concatenate([cols * down(value_re), cols * down(value_im)], axis=1)
        sub = mm(spread(rows, LEFT[6], 1), spread(weighted, RIGHT[6], 0))
        for q in range(4):
            for ri in range(2):
                total[(q - me) & 3, ri, t] += sub[32 * q : 32 * q + 32, 128 * ri : 128 * ri + 128]

    def turn(start, count):
        def body(g, _):
            for u in range(count):
                add(start + g * count + u)
            return 0

        return body

    whole = n // GROUP
    lax.fori_loop(0, whole, turn(0, GROUP), 0)
    begun = whole * GROUP
    lax.fori_loop(0, (n - begun + REST - 1) // REST, turn(begun, REST), 0)


def cols_kernel(*refs):
    me, parts, (tw, w, w_back, out, mid) = refs[0], refs[1:9], refs[9:]

    def tile(b, ri, at):
        return parts[b % 16 // 8 * 4 + -(b // 16) % 4][ri, b % 8, at, :]

    def rows(i, _):
        at = pl.ds(pl.multiple_of(i * 8, 8), 8)
        first = [(tile(b, 0, at), tile(b, 1, at)) for b in range(64)]
        for c, (re, im) in enumerate(fft_list(first)):
            half, c = c // 32, c % 32
            to = 32 * half + c if c <= 16 else 32 * (1 - half) + 48 - c
            mid[to, at, 0:128] = re
            mid[to, at, 128:256] = im
        return 0

    def turned_rows(to):
        half, c = to // 32, to % 32
        c = 32 * half + c if c <= 16 else 32 * (1 - half) + 48 - c
        cos, sin = tw[me[0], 0, c : c + 1, :], tw[me[0], 1, c : c + 1, :]
        re, im = mid[to, :, 0:128], mid[to, :, 128:256]
        return jnp.concatenate([re * cos - im * sin, re * sin + im * cos], axis=1)

    lax.fori_loop(0, 4, rows, 0)
    for pair in range(8):
        part = jnp.concatenate([turned_rows(8 * pair + k) for k in range(8)], axis=0)
        part = spread(part, RIGHT[6], 1)
        res = mm((w if pair % 4 < 2 else w_back)[...], part, NT)
        if pair % 4 == 2:
            own = mm(w[...], part[0:128], NT)
            own = jnp.concatenate([jnp.where(low_lanes(), own, res[:, 0:128]), res[:, 128:256]], axis=1)
            res = own
        for k in range(2):
            chunk = 2 * pair + k
            for ri in range(2):
                out[:, chunk // 8, ri * 8 + chunk % 8, :] = res[64 * ri : 64 * ri + 64, 128 * k : 128 * k + 128]


def row_transform(xi, amplitude, tw, w, out, mid, tags):
    def rows(i, _):
        at = pl.ds(pl.multiple_of(i * 8, 8), 8)
        first = [
            xi[at, 128 * b : 128 * b + 128] * amplitude[at, 128 * b : 128 * b + 128] for b in range(32)
        ]
        for c, (re, im) in enumerate(rfft_list(first)):
            cos, sin = tw[0, c : c + 1, :], tw[1, c : c + 1, :]
            if im is None:
                mid[c, at, 0:128] = re * cos
                mid[c, at, 128:256] = re * sin
            else:
                mid[c, at, 0:128] = re * cos - im * sin
                mid[c, at, 128:256] = re * sin + im * cos
        return 0

    lax.fori_loop(0, 4, rows, 0)
    for pair in range(2):
        part = spread(mid[8 * pair : 8 * pair + 8].reshape(256, 256), RIGHT[3], 1)
        res = mm(w[...], part, NT)
        for k in range(2):
            for ri in range(2):
                out[:, 8 + ri * 4 + 2 * pair + k, 0, :] = res[128 * ri : 128 * ri + 128, 128 * k : 128 * k + 128]
    part = spread(mid[16:20].reshape(128, 256), RIGHT[3], 1)
    res = mm(w[...], part, NT)
    out[:, 16, 0, :] = beside(res[0:128], res[128:256]) + tags[:, 0, :]


def low_lanes():
    return lax.broadcasted_iota(jnp.int32, (128, 128), 1) < 32


def beside(a, b):
    lane = lax.broadcasted_iota(jnp.int32, (128, 128), 1)
    return jnp.where(lane < 32, a, jnp.where(lane < 64, pltpu.roll(b, 32, 1), 0.0))


def column_pairs(field, pair):
    chunk = []
    for k in range(2):
        j = 2 * pair + k
        re, im = field[:, 8 + j % 4, 0, :], field[:, 12 + j % 4, 0, :]
        if j >= 4:
            im = -im
        if j == 4:
            own = field[:, 16, 0, :]
            re, im = jnp.where(low_lanes(), own, re), jnp.where(low_lanes(), pltpu.roll(own, 96, 1), im)
        chunk.append((re, im))
    return jnp.concatenate(
        [jnp.concatenate([chunk[k][ri] for k in range(2)], axis=1) for ri in range(2)], axis=0
    )


def chunks(ref, pair):
    return jnp.concatenate(
        [jnp.concatenate([ref[:, ri * 8 + 2 * pair + k, :] for k in range(2)], axis=1) for ri in range(2)],
        axis=0,
    )


def twist(re, im, tw):
    return re * tw[0] - im * tw[1], re * tw[1] + im * tw[0]


def halves(a, at):
    return [a[at : at + 128, 128 * k : 128 * k + 128] for k in range(2)]


def stacked(rows):
    return jnp.concatenate([jnp.concatenate(r, axis=1) for r in rows], axis=0)


def sky_kernel(field, w, tw, r, out):
    for pair in range(4):
        a = mm(w[...], spread(column_pairs(field, pair), RIGHT[3], 0))
        turn = stacked([twist(re, im, tw) for re, im in zip(halves(a, 0), halves(a, 128))])
        out[pair] = jnp.exp(mm(spread(turn, LEFT[3], 1), r[...]))


def image_kernel(sky, uv, w, tw_f, r_y, w_b, tw_b, r_b, out):
    done = []
    for pair in range(4):
        kept = spread(chunks(uv, pair), RIGHT[3], 0)
        a = mm(w_b[...], kept)
        parts = [[], []]
        for h in range(2):
            for k, (re, im) in enumerate(zip(halves(a, 256 * h), halves(a, 256 * h + 128))):
                parts[k] += twist(re, im, tw_b[h])
        back = mm(spread(stacked(parts), LEFT[3], 1), r_b[...])
        a = mm(spread(sky[pair] * back, LEFT[3], 1), r_y[...])
        turn = [twist(a[128 * k : 128 * k + 128, 0:128], a[128 * k : 128 * k + 128, 128:256], tw_f) for k in range(2)]
        turn = jnp.concatenate([jnp.concatenate([turn[k][ri] for k in range(2)], axis=1) for ri in range(2)], axis=0)
        done.append(mm(w[...], spread(turn, RIGHT[3], 0)))
    for j in range(4):
        at = slice(128 * (j % 2), 128 * (j % 2) + 128)
        straight, mirrored = done[j // 2][:, at], done[2 + j // 2][:, at]
        re, im = mirrored[0:128], mirrored[128:256]
        if j == 0:
            out[:, 8, 0, :] = beside(re, im)
            re, im = jnp.where(low_lanes(), 0.0, re), jnp.where(low_lanes(), 0.0, im)
        out[:, j, 0, :] = straight[0:128] + im
        out[:, 4 + j, 0, :] = straight[128:256] + re


def last_kernel(folded, amplitude, tw, w, out, mid):
    def residue(c, v):
        cos, sin = tw[0, c : c + 1, :], tw[1, c : c + 1, :]
        re, im = v[:, 0:128], v[:, 128:256]
        mid[c, :, 0:128] = re * cos - im * sin
        mid[c, :, 128:256] = re * sin + im * cos

    for j in range(4):
        z = jnp.concatenate([folded[:, j, 0, :], folded[:, 4 + j, 0, :]], axis=0)
        v = mm(spread(z, LEFT[3], 0), w[...], TN)
        for k in range(4):
            residue(4 * j + k, v[32 * k : 32 * k + 32])
    own = folded[:, 8, 0, :]
    z = jnp.concatenate([own, pltpu.roll(own, 96, 1)], axis=0)
    residue(16, mm(spread(z, LEFT[3], 0), w[...], TN)[0:32])

    def rows(i, _):
        at = pl.ds(pl.multiple_of(i * 8, 8), 8)
        first = [(mid[c, at, 0:128], mid[c, at, 128:256]) for c in range(17)] + [None] * 15
        for b, (re, im) in enumerate(fft_list(first)):
            to = slice(128 * b, 128 * b + 128)
            out[at, to] = amplitude[at, to] * (re + im) * (1.0 / IMG)
        return 0

    lax.fori_loop(0, 4, rows, 0)


def per_device(residual, position, owner, tile_local, xi, amplitude):
    n_base = lax.axis_size("base")
    n_slab = lax.axis_size("slab")
    devices = n_base * n_slab
    everywhere = ("base", "slab")
    t = {k: jnp.asarray(v) for k, v in tables(n_base, n_slab).items()}

    def exchange(a, axis):
        return lax.all_to_all(a, axis, split_axis=0, concat_axis=0, tiled=True)

    rows, width = xi.shape
    blocks = residual.shape[0]
    me = jnp.stack([lax.axis_index("base"), lax.axis_index("slab") & 1]).astype(jnp.int32)
    packed = call(
        first_kernel,
        (devices, 17, 1, 128),
        [SM, SM] + [VM] * 6,
        [SM((devices,), jnp.int32), VM((20, 32, 256), f32), VM((devices, 1, 128), f32)],
        2e9,
        [
            (0, SM((blocks,), jnp.int32)),
            (1, SM((blocks,), jnp.int32)),
            (2, VM(residual.shape, f32)),
            (3, VM(position.shape, f32)),
            (4, VM((rows, width), f32)),
            (5, VM((rows, width), f32)),
            (6, VM((2, 32, 128), f32)),
            (7, VM((256, 768), bf16)),
        ],
    )(owner[:, 0], tile_local, residual, position, xi, amplitude, t["tw_row"], t["w128"])
    data = exchange(packed, everywhere)
    mate = lax.ppermute(data, "slab", [(i, i ^ 1) for i in range(n_slab)])
    tags = tuple(a[:, 16, 0, 64:70].reshape(6 * devices).astype(jnp.int32) for a in (data, mate))
    spare = [VM((4, TILE, TILE), f32), SM((4 * devices + REST,), jnp.int32)]
    shape = (2, 8, 32, 128)
    grids = []
    for phase in range(2):
        parts = call(
            functools.partial(grid_parts_kernel, 8 * phase),
            [shape] * n_base,
            [SM, SM, SM, VM, VM],
            [*spare, VM((n_base, *shape), f32)],
            2e10,
        )(me, *tags, data, mate)
        if phase == 0:
            parts, tags = lax.optimization_barrier((parts, tags))
        else:
            parts, grids, field = lax.optimization_barrier((parts, grids, data))
        moved = {
            k: lax.ppermute(parts[k], "base", [(i, (i + k) % n_base) for i in range(n_base)]) for k in (2, 1, 3)
        }
        grids = [*grids, parts[0]] + [moved[k] for k in range(1, n_base)]
    sky = call(
        sky_kernel,
        (4, 256, 128),
        [VM] * 4,
        (),
        4e9,
        [(1, VM((256, 768), bf16)), (2, VM((2, 128, 128), f32)), (3, VM((768, 128), bf16))],
        True,
    )(field, t["w128"], t["tw_f"], t["r_f"])
    grids[0], sky = lax.optimization_barrier((grids[0], sky))
    cols = call(
        cols_kernel,
        (devices // 2, 2, 16, 128),
        [SM] + [VM] * 11,
        [VM((64, 32, 256), f32)],
        4e9,
        [
            (9, VM((n_base, 2, 64, 128), f32)),
            (10, VM((128, 1536), bf16)),
            (11, VM((128, 1536), bf16)),
        ],
    )(me, *grids, t["tw_cols"], t["w_cols"], t["w_back"])
    cols = exchange(cols.reshape(devices, 16, 128), everywhere)
    fold = call(
        image_kernel,
        (devices, 9, 1, 128),
        [VM] * 8,
        (),
        8e9,
        [
            (0, VM((4, 256, 128), f32)),
            (5, VM((512, 768), bf16)),
            (7, VM((1536, 128), bf16)),
        ],
    )(sky, cols, t["w128"], t["tw_f"], t["r_y"], t["w_b"], t["tw_b"], t["r_b"])
    fold = exchange(fold, everywhere)
    return call(last_kernel, (32, IMG), [VM] * 4, [VM((32, 32, 256), f32)], 3e9)(
        fold, amplitude, t["tw_row"], t["w128t"]
    )


def solution(mesh):
    placed = (
        P(("base", "slab"), None, None),
        P(("base", "slab"), None, None),
        P(("base", "slab"), None),
        P(("base", "slab")),
        P(("base", "slab"), None),
        P(("base", "slab"), None),
    )
    return jax.shard_map(
        per_device, mesh=mesh, in_specs=placed, out_specs=P(("base", "slab"), None), check_vma=False
    )
```
